128 devices in a mesh: loop: 8 (over x_lo, z), rep: 16 (over x_hi, y, core).
Axes of the slice: x: 4 (x_hi: 2, x_lo: 2; x = x_hi * 2 + x_lo), y: 4, z: 4, core: 2. Of those that a mesh axis runs over, the one named last changes fastest.
Arguments:
- features: bfloat16 [16, 4096, 2048], P('rep', 'loop'), may hold values from -8 to 8
- weight: bfloat16 [2048, 512], P(('loop', 'rep')), may hold values from -0.125 to 0.125
- pair_ids: int32 [16, 4096], P('rep', 'loop'), may hold values from 0 to 2047, as said below
- dup_ids: int32 [16, 4096], P('rep', 'loop'), may hold values from 0 to 682, as said below
Outputs:
- image_loss: float32 [16, 4096], P('rep', 'loop')
- feature_grad: bfloat16 [16, 4096, 2048], P('rep', 'loop')
- weight_grad: float32 [2048, 512], P(('loop', 'rep'))
The draws below stay inside these ranges and needn't reach their ends.
Inputs may be any that keep to these rules, and one draw needn't show every extreme that they name: `pair_ids`: within one replica every value is held by exactly two images. Images with equal pair_ids have equal dup_ids; within one replica a value is shared by at most three pairs.
All inputs are finite; a program needn't handle non-finite values.
Results may differ from the reference program's by a relative error of at most 0.013.
Values may be sent and summed in bfloat16 or wider, within the bound.
A program may use at most 64 MiB of HBM per device.

```python
import math
from functools import partial
import jax
import jax.numpy as jnp
from jax import lax

FEAT = 2048
EMB = 512
REPLICAS = 16
GROUP = 4096
TOTAL = 65536


def lookup_rows(lookup_table, positions):
    return lookup_table[positions]


def shuffled_ids(subkey, length):
    return jax.random.permutation(subkey, length).astype(jnp.int32)


def draw_labels(key):
    pair_keys = jax.random.split(jax.random.fold_in(key, 11), REPLICAS)
    dup_keys = jax.random.split(jax.random.fold_in(key, 12), REPLICAS)
    shuffled = jax.vmap(lambda subkey: shuffled_ids(subkey, GROUP))(pair_keys)
    pair_labels = shuffled // 2
    mixing = jax.vmap(lambda subkey: shuffled_ids(subkey, GROUP // 2))(dup_keys)
    dup_labels = jax.vmap(lookup_rows)(mixing, pair_labels) // 3
    return (pair_labels, dup_labels)


def draw_pair_ids(key, part):
    pair_labels, dup_labels = draw_labels(key)
    return pair_labels


def draw_dup_ids(key, part):
    pair_labels, dup_labels = draw_labels(key)
    return dup_labels


def draw_features(key, part):
    pair_labels, dup_labels = draw_labels(key)
    key = jax.random.fold_in(key, 3)
    base_key, dup_key, pair_key = jax.random.split(key, 3)
    dup_table = jax.random.normal(dup_key, (REPLICAS, GROUP // 6 + 1, FEAT), jnp.float32)
    pair_table = jax.random.normal(pair_key, (REPLICAS, GROUP // 2, FEAT), jnp.float32)
    shared = 0.9 * jax.vmap(lookup_rows)(dup_table, dup_labels) + 0.7 * jax.vmap(lookup_rows)(pair_table, pair_labels)
    base_noise = jax.random.normal(base_key, (REPLICAS, GROUP, FEAT), jnp.float32)
    return jnp.clip(base_noise + shared, -8.0, 8.0).astype(jnp.bfloat16)


def block_levels(key, extent, cuts, smallest, largest):
    level = 1.0
    for axis_at, parts in cuts:
        steps = jax.random.uniform(jax.random.fold_in(jax.random.fold_in(key, 6), axis_at), (parts,), jnp.float32, smallest / len(cuts), largest / len(cuts))
        level = level * jnp.repeat(jnp.exp(steps), extent[axis_at] // parts).reshape((-1,) + (1,) * (len(extent) - 1 - axis_at))
    return level


def centred(own_key, dims, deviation, bound, cuts=(), held_as=jnp.bfloat16):
    factor_of = block_levels(own_key, dims, cuts, -0.22, 0.18) if cuts else 1.0
    array = jax.random.normal(own_key, dims, jnp.float32) * deviation * factor_of
    return jnp.minimum(jnp.maximum(array, -bound), bound).astype(held_as)


def setup_inputs(seed: int = 0) -> dict:
    seeds = jax.random.split(jax.random.key(seed), 5)
    features = draw_features(jax.random.fold_in(seeds[4], 71), 0)
    weight = centred(seeds[1], (FEAT, EMB), FEAT ** -0.5, 0.125, ((0, 128),))
    pair_ids = draw_pair_ids(jax.random.fold_in(seeds[4], 71), 0)
    dup_ids = draw_dup_ids(jax.random.fold_in(seeds[4], 71), 0)
    return dict(features=features, weight=weight, pair_ids=pair_ids, dup_ids=dup_ids)


scale_logits = 20.0
norm_eps = 1e-06

def pair_masks(row_dups, row_pairs, row_first, col_dups, col_pairs, col_first):
    row_index = row_first + jnp.arange(row_dups.shape[0], dtype=jnp.int32)
    col_index = col_first + jnp.arange(col_dups.shape[0], dtype=jnp.int32)
    distinct = row_index[:, None] != col_index[None, :]
    partner = jnp.logical_and(row_pairs[:, None] == col_pairs[None, :], distinct)
    allowed = jnp.logical_and(distinct, jnp.logical_or(row_dups[:, None] != col_dups[None, :], partner))
    return (allowed.astype(jnp.float32), partner.astype(jnp.float32))

def pair_scores(left_embed, right_embed):
    return scale_logits * jnp.dot(left_embed, right_embed.T, preferred_element_type=jnp.float32)

def replica_terms(weight, packed):
    image_feats, pair_labels, dup_labels = packed
    projected = jnp.dot(image_feats, weight, preferred_element_type=jnp.float32)
    inverse_norm = lax.rsqrt(lax.optimization_barrier(jnp.sum(projected * projected, axis=1, keepdims=True)) + norm_eps)
    normed = projected * inverse_norm
    embedding = normed.astype(jnp.bfloat16)
    scores = pair_scores(embedding, embedding)
    allowed, partner = pair_masks(dup_labels, pair_labels, 0, dup_labels, pair_labels, 0)
    exp_total = lax.optimization_barrier(jnp.sum(allowed * jnp.exp(scores - scale_logits), axis=1))
    positive = lax.optimization_barrier(jnp.sum(partner * scores, axis=1))
    log_total = jnp.log(exp_total) + scale_logits
    image_loss = log_total - positive
    pair_weight = (allowed * jnp.exp(scores - log_total[:, None]) - partner).astype(jnp.bfloat16)
    grad_sum = jnp.dot(pair_weight, embedding, preferred_element_type=jnp.float32)
    grad_sum = grad_sum + jnp.dot(pair_weight.T, embedding, preferred_element_type=jnp.float32)
    grad_embed = scale_logits * grad_sum
    grad_pre = (inverse_norm * (grad_embed - normed * lax.optimization_barrier(jnp.sum(normed * grad_embed, axis=1, keepdims=True)))).astype(jnp.bfloat16)
    feature_grad = jnp.dot(grad_pre, weight.T, preferred_element_type=jnp.float32).astype(jnp.bfloat16)
    weight_term = lax.dot_general(image_feats, grad_pre, (((0,), (0,)), ((), ())), preferred_element_type=jnp.float32)
    return (image_loss, feature_grad, weight_term)

def reference(features, weight, pair_ids, dup_ids):
    image_loss, feature_grad, weight_terms = lax.map(partial(replica_terms, weight), (features, pair_ids, dup_ids))
    weight_grad = lax.optimization_barrier(jnp.sum(weight_terms, axis=0)) / math.sqrt(TOTAL)
    return (image_loss, feature_grad, weight_grad)
```

```python
import jax
import jax.numpy as jnp
from jax import lax
from jax.experimental import pallas as pl
from jax.experimental.pallas import tpu as pltpu
from jax.sharding import PartitionSpec as P

MESH = pl.DeviceIdType.MESH
scale_logits = 20.0
norm_eps = 1e-06
ROWS = 512
FEAT = 2048
EMB = 512
HALF = 256
BF16 = jnp.bfloat16
F32 = jnp.float32

ORDER = (
    (1, 0, 0),
    (1, 0, 1),
    (0, 3, 0),
    (0, 1, 1),
    (0, 3, 1),
    (0, 1, 0),
    (1, 3, 0),
    (1, 1, 1),
    (1, 3, 1),
    (1, 1, 0),
    (0, 2, 0),
    (0, 2, 1),
    (1, 2, 0),
    (1, 2, 1),
)


def device_at(x, y, z, core):
    return (lax.rem(x, 2) * 4 + z, lax.div(x, 2) * 8 + y * 2 + core)


def remote(src, dst, send_sem, recv_sem, device):
    return pltpu.make_async_remote_copy(
        src_ref=src,
        dst_ref=dst,
        send_sem=send_sem,
        recv_sem=recv_sem,
        device_id=device,
        device_id_type=MESH,
    )


def pick(step, column):
    value = jnp.int32(0)
    for index, entry in enumerate(ORDER):
        if entry[column]:
            value = jnp.where(step == index, entry[column], value)
    return value


def to_row(column):
    return jnp.broadcast_to(column, (ROWS, 128)).T[0:8, :]


def to_column(rows):
    return rows.T


def kernel(
    feat_hbm,
    weight_ref,
    pair_ref,
    dup_ref,
    loss_ref,
    fgrad_hbm,
    wgrad_ref,
    feat,
    featp,
    wpart,
    wfull,
    normed,
    inverse,
    home_emb,
    emb,
    labels,
    label_home,
    row_labels,
    dots,
    quot,
    acc,
    pos,
    norms,
    grad,
    grad_out,
    grad_in,
    aux_out,
    aux_in,
    pre,
    fgrad,
    sib_out,
    sib_in,
    first_out,
    first_in,
    first_sum,
    second_out,
    second_in,
    third_out,
    third_in,
    feat_sem,
    fgrad_sem,
    wx_send,
    wx_recv,
    ws_send,
    ws_recv,
    wf_send,
    wf_recv,
    wc_send,
    wc_recv,
    lab_send,
    lab_recv,
    labx_send,
    labx_recv,
    swap_send,
    swap_recv,
    ring_send,
    sib_send,
    emb_recv,
    norm_send,
    norm_recv,
    back_send,
    back_recv,
    rc_send,
    rc_recv,
    rf_send,
    rf_recv,
    rs_send,
    rs_recv,
    rx_send,
    rx_recv,
):
    loop, rep = lax.axis_index("loop"), lax.axis_index("rep")
    x_lo, z = lax.div(loop, 4), lax.rem(loop, 4)
    x_hi, y, core = lax.div(rep, 8), lax.rem(lax.div(rep, 2), 4), lax.rem(rep, 2)
    x = x_hi * 2 + x_lo
    other = 1 - core
    first = z * other + y * core
    second = y * other + z * core
    stays = core == x_lo
    slot = core * 4 + z

    def around(value, step):
        return lax.rem(value + step, 4)

    def x_peer(step):
        return device_at(around(x, step), y, z, core)

    def first_peer(step):
        return device_at(
            x, around(y, step * core), around(z, step * other), core
        )

    def second_peer(step):
        return device_at(
            x, around(y, step * other), around(z, step * core), core
        )

    def z_peer(step, which):
        return device_at(x, y, around(z, step), which)

    sibling = device_at(x, y, z, other)
    partner = device_at(x_hi * 2 + 1 - x_lo, y, z, other)

    load = pltpu.make_async_copy(feat_hbm, feat, feat_sem)
    load.start()

    barrier = pltpu.get_barrier_semaphore()
    everyone = [sibling, partner]
    for step in (1, 2, 3):
        everyone += [x_peer(step), first_peer(step), second_peer(step), z_peer(step, other)]
    for device in everyone:
        pl.semaphore_signal(barrier, inc=1, device_id=device, device_id_type=MESH)

    wpart[core, first, second, x] = weight_ref[...]
    label_home[...] = jnp.zeros((8, ROWS), jnp.int32)
    label_home[0:1, :] = pair_ref[...]
    label_home[1:2, :] = dup_ref[...]
    pl.semaphore_wait(barrier, len(everyone))

    wx = [
        remote(
            wpart.at[core, first, second, x],
            wpart.at[core, first, second, x],
            wx_send.at[step - 1],
            wx_recv.at[step - 1],
            x_peer(step),
        )
        for step in (1, 2, 3)
    ]
    for copy in wx:
        copy.start()

    lab_swap = remote(label_home, labels.at[other * 4 + z], labx_send.at[0], labx_recv.at[0], partner)
    lab_swap_in = remote(label_home, labels.at[slot], labx_send.at[0], labx_recv.at[0], partner)

    @pl.when(jnp.logical_not(stays))
    def _():
        lab_swap.start()

    @pl.when(stays)
    def _():
        labels[slot] = label_home[...]

    load.wait()

    def transpose_slab(slab, carry):
        slab_xlo, slab_z, slab_xhi = lax.div(slab, 8), lax.rem(lax.div(slab, 2), 4), lax.rem(slab, 2)
        slab_x = slab_xhi * 2 + slab_xlo
        turned = feat[:, pl.ds(pl.multiple_of(slab * 128, 128), 128)].T
        for at_y in range(4):
            zero = pl.multiple_of((at_y * 4 + slab_x) * 16, 16)
            featp[0, slab_z, pl.ds(zero, 16), :] = turned[at_y * 32 : at_y * 32 + 16]
            one = pl.multiple_of((slab_z * 4 + slab_x) * 16, 16)
            featp[1, at_y, pl.ds(one, 16), :] = turned[at_y * 32 + 16 : at_y * 32 + 32]
        return carry

    for step in (1, 2, 3):
        source = around(x, 4 - step)
        remote(
            wpart.at[core, first, second, source],
            wpart.at[core, first, second, source],
            wx_send.at[step - 1],
            wx_recv.at[step - 1],
            x_peer(step),
        ).wait_recv()
    started = list(wx)
    for step in (1, 2, 3):
        copy = remote(
            wpart.at[core, first, second],
            wpart.at[core, first, second],
            ws_send.at[step - 1],
            ws_recv.at[step - 1],
            second_peer(step),
        )
        copy.start()
        started.append(copy)
    for piece in range(4):
        source = around(second, 4 - piece)
        if piece:
            remote(
                wpart.at[core, first, source],
                wpart.at[core, first, source],
                ws_send.at[piece - 1],
                ws_recv.at[piece - 1],
                second_peer(piece),
            ).wait_recv()
        for step in (1, 2, 3):
            copy = remote(
                wpart.at[core, first, source],
                wpart.at[core, first, source],
                wf_send.at[step - 1, piece],
                wf_recv.at[step - 1, piece],
                first_peer(step),
            )
            copy.start()
            started.append(copy)
    to_sibling = remote(
        wpart.at[core, first], wpart.at[core, first], wc_send.at[0], wc_recv.at[0], sibling
    )
    to_sibling.start()
    started.append(to_sibling)

    lax.fori_loop(0, 16, transpose_slab, 0)

    @pl.when(jnp.logical_not(stays))
    def _():
        lab_swap_in.wait_recv()

    lab_copies = []
    for index, (step, which) in enumerate(
        [(0, other)] + [(step, which) for step in (1, 2, 3) for which in (core, other)]
    ):
        copy = remote(
            labels.at[slot],
            labels.at[slot],
            lab_send.at[index],
            lab_recv.at[slot],
            z_peer(step, which),
        )
        copy.start()
        lab_copies.append(copy)
    row_labels[...] = to_column(labels[slot])

    for step in (1, 2, 3):
        source = around(first, 4 - step)
        for piece in range(4):
            at = around(second, 4 - piece)
            remote(
                wpart.at[core, source, at],
                wpart.at[core, source, at],
                wf_send.at[step - 1, piece],
                wf_recv.at[step - 1, piece],
                first_peer(step),
            ).wait_recv()
        copy = remote(
            wpart.at[core, source],
            wpart.at[core, source],
            wc_send.at[step],
            wc_recv.at[step],
            sibling,
        )
        copy.start()
        started.append(copy)
    sibling_first = second
    for step in range(4):
        source = around(sibling_first, 4 - step)
        remote(
            wpart.at[other, source],
            wpart.at[other, source],
            wc_send.at[step],
            wc_recv.at[step],
            sibling,
        ).wait_recv()

    def place_block(index, carry):
        at_first, at_second, at_x = lax.div(index, 16), lax.rem(lax.div(index, 4), 4), lax.rem(index, 4)
        base = lax.rem(at_x, 2) * 64 + lax.div(at_x, 2) * 8
        zero = (base + at_first * 16 + at_second * 2) * 16
        one = (base + at_second * 16 + at_first * 2 + 1) * 16
        wfull[pl.ds(pl.multiple_of(zero, 16), 16), :] = wpart[0, at_first, at_second, at_x]
        wfull[pl.ds(pl.multiple_of(one, 16), 16), :] = wpart[1, at_first, at_second, at_x]
        return carry

    lax.fori_loop(0, 64, place_block, 0)

    def project(index, carry):
        columns = pl.ds(pl.multiple_of(index * HALF, HALF), HALF)
        normed[:, columns] = jnp.dot(feat[...], wfull[:, columns], preferred_element_type=F32)
        return carry

    lax.fori_loop(0, 2, project, 0)

    def normalise(index, carry):
        rows = pl.ds(pl.multiple_of(index * 64, 64), 64)
        projected = normed[rows, :]
        scale = lax.rsqrt(jnp.sum(projected * projected, axis=1, keepdims=True) + norm_eps)
        unit = projected * scale
        normed[rows, :] = unit
        inverse[rows, :] = jnp.broadcast_to(scale, (64, 128))
        home_emb[rows, :] = unit.astype(BF16)
        return carry

    lax.fori_loop(0, 8, normalise, 0)

    def half(ref, at, which):
        return ref.at[at, pl.ds(pl.multiple_of(which * HALF, HALF), HALF)]

    swaps = [
        remote(
            home_emb.at[pl.ds(part * HALF, HALF)],
            emb.at[other * 4 + z, pl.ds(part * HALF, HALF)],
            swap_send.at[part],
            swap_recv.at[part],
            partner,
        )
        for part in range(2)
    ]

    @pl.when(jnp.logical_not(stays))
    def _():
        for copy in swaps:
            copy.start()

    @pl.when(stays)
    def _():
        emb[slot] = home_emb[...]

    acc[...] = jnp.zeros((ROWS, 128), F32)
    pos[...] = jnp.zeros((ROWS, 128), F32)

    def ring(at, which, step, sem):
        return remote(
            half(emb, at, which), half(emb, at, which), ring_send.at[sem], emb_recv.at[at, which], z_peer(step, core)
        )

    def beside(at, which, sem):
        return remote(
            half(emb, at, which), half(emb, at, which), sib_send.at[sem], emb_recv.at[at, which], sibling
        )

    for part in range(2):

        @pl.when(jnp.logical_not(stays))
        def _():
            remote(
                home_emb.at[pl.ds(part * HALF, HALF)],
                emb.at[slot, pl.ds(part * HALF, HALF)],
                swap_send.at[part],
                swap_recv.at[part],
                partner,
            ).wait_recv()

        ring(slot, part, 1, part).start()
        ring(slot, part, 3, 2 + part).start()
        beside(slot, part, part).start()

    for index in range(7):
        other_slot = lax.rem(slot + 1 + index, 8)
        remote(
            labels.at[other_slot],
            labels.at[other_slot],
            lab_send.at[index],
            lab_recv.at[other_slot],
            sibling,
        ).wait_recv()

    def take(at, which, own):
        piece = at * 2 + which
        dots[...] = lax.dot_general(
            emb[slot],
            emb[at, pl.ds(pl.multiple_of(which * HALF, HALF), HALF), :],
            (((1,), (1,)), ((), ())),
            preferred_element_type=F32,
        )
        columns = pl.ds(pl.multiple_of(which * HALF, HALF), HALF)
        col_pair = labels[at, 0:1, columns]
        col_dup = labels[at, 1:2, columns]

        def rows_of(index, carry):
            start = pl.multiple_of(index * 64, 64)
            rows = pl.ds(start, 64)
            row_pair = row_labels[rows, 0:1]
            row_dup = row_labels[rows, 1:2]
            scores = scale_logits * dots[rows, :]
            mate = row_pair == col_pair
            allowed = jnp.logical_or(row_dup != col_dup, mate)
            if own:
                row_index = start + lax.broadcasted_iota(jnp.int32, (64, HALF), 0)
                col_index = which * HALF + lax.broadcasted_iota(jnp.int32, (64, HALF), 1)
                distinct = row_index != col_index
                mate = jnp.logical_and(mate, distinct)
                allowed = jnp.logical_and(allowed, distinct)
            weight = jnp.where(allowed, jnp.exp(scores - scale_logits), 0.0)
            quot[piece, rows, :] = weight
            acc[rows, :] += weight[:, :128] + weight[:, 128:]
            matched = jnp.where(mate, scores, 0.0)
            pos[rows, :] += matched[:, :128] + matched[:, 128:]
            return carry

        lax.fori_loop(0, 8, rows_of, 0)

    def own_piece(part, carry):
        take(slot, part, True)
        return carry

    lax.fori_loop(0, 2, own_piece, 0)

    def next_piece(step, carry):
        which_ring = jnp.where(pick(step, 0) == 0, core, other)
        at = which_ring * 4 + around(z, pick(step, 1))
        which = pick(step, 2)
        ring(at, which, 1, 0).wait_recv()

        @pl.when(step == 2)
        def _():
            ring(at, which, 1, 4).start()
            beside(at, which, 2).start()

        @pl.when(step == 3)
        def _():
            ring(at, which, 3, 5).start()
            beside(at, which, 3).start()

        for index, count in ((4, 4), (5, 5), (10, 6), (11, 7)):

            @pl.when(step == index)
            def _():
                beside(at, which, count).start()

        take(at, which, False)
        return carry

    lax.fori_loop(0, len(ORDER), next_piece, 0)

    total = jnp.sum(acc[...], axis=1, keepdims=True)
    loss = jnp.log(total) + scale_logits - jnp.sum(pos[...], axis=1, keepdims=True)
    own_norm = 1.0 / total
    norms[slot] = to_row(own_norm)
    norm_copies = []
    for index, (step, which) in enumerate(
        [(0, other)] + [(step, which) for step in (1, 2, 3) for which in (core, other)]
    ):
        copy = remote(
            norms.at[slot], norms.at[slot], norm_send.at[index], norm_recv.at[slot], z_peer(step, which)
        )
        copy.start()
        norm_copies.append(copy)
    acc[...] = jnp.broadcast_to(own_norm, (ROWS, 128))
    pos[...] = jnp.broadcast_to(loss, (ROWS, 128))
    aux_out[...] = to_row(loss)
    for index in range(7):
        other_slot = lax.rem(slot + 1 + index, 8)
        remote(
            norms.at[other_slot],
            norms.at[other_slot],
            norm_send.at[index],
            norm_recv.at[other_slot],
            sibling,
        ).wait_recv()

    for part in range(2):
        rows = pl.ds(part * HALF, HALF)
        row_pair = row_labels[rows, 0:1]
        row_norm = acc[rows, 0:1]

        def add_slot(at, carry):
            for which in range(2):
                columns = pl.ds(which * HALF, HALF)
                mate = row_pair == labels[at, 0:1, columns]
                own = jnp.logical_and(
                    at == slot,
                    part * HALF + lax.broadcasted_iota(jnp.int32, (HALF, HALF), 0)
                    == which * HALF + lax.broadcasted_iota(jnp.int32, (HALF, HALF), 1),
                )
                mate = jnp.logical_and(mate, jnp.logical_not(own))
                weight = quot[at * 2 + which, rows, :] * (row_norm + norms[at, 0:1, columns])
                weight = weight - jnp.where(mate, 2.0, 0.0)
                term = jnp.dot(weight.astype(BF16), emb[at, columns, :], preferred_element_type=F32)
                grad[rows, :] += term
            return carry

        grad[rows, :] = jnp.zeros((HALF, EMB), F32)
        lax.fori_loop(0, 8, add_slot, 0)

        @pl.when(jnp.logical_not(stays))
        def _():
            unit = emb[slot, rows, :].astype(F32)
            whole = grad[rows, :]
            along = jnp.sum(unit * whole, axis=1, keepdims=True)
            grad_out[rows, :] = (whole - along * unit).astype(BF16)
            inner = jnp.broadcast_to(along, (HALF, 128)).T[0:1, :]
            aux_out[1:2, part * HALF : (part + 1) * HALF] = inner
            remote(
                grad_out.at[rows], grad_in.at[rows], back_send.at[part], back_recv.at[part], partner
            ).start()

    @pl.when(jnp.logical_not(stays))
    def _():
        remote(aux_out, aux_in, back_send.at[2], back_recv.at[2], partner).start()
        remote(aux_out, aux_in, back_send.at[2], back_recv.at[2], partner).wait_recv()
        columns_of = to_column(aux_in[...])
        loss_ref[...] = aux_in[0:1, :]
        for part in range(2):
            rows = pl.ds(part * HALF, HALF)
            remote(
                grad_out.at[rows], grad_in.at[rows], back_send.at[part], back_recv.at[part], partner
            ).wait_recv()
            along = columns_of[part * HALF : (part + 1) * HALF, 1:2]
            grad[rows, :] = grad_in[rows, :].astype(F32) + along * home_emb[rows, :].astype(F32)

    @pl.when(stays)
    def _():
        loss_ref[...] = aux_out[0:1, :]

    def finish(index, carry):
        rows = pl.ds(pl.multiple_of(index * 64, 64), 64)
        unit = normed[rows, :]
        whole = scale_logits * grad[rows, :]
        along = jnp.sum(unit * whole, axis=1, keepdims=True)
        pre[rows, :] = (inverse[rows, 0:1] * (whole - unit * along)).astype(BF16)
        return carry

    lax.fori_loop(0, 8, finish, 0)

    def term_of(which, at):
        return jnp.dot(featp[which, at], pre[...], preferred_element_type=F32)

    reduce_copies = []
    for step in range(4):
        at = around(sibling_first, step + 1 if step < 3 else 0)
        sib_out[step] = term_of(other, at).astype(BF16)
        copy = remote(sib_out.at[step], sib_in.at[step], rc_send.at[step], rc_recv.at[step], sibling)
        copy.start()
        reduce_copies.append(copy)
    for step in range(4):
        at = around(first, step + 1 if step < 3 else 0)
        own = term_of(core, at)
        remote(sib_out.at[step], sib_in.at[step], rc_send.at[step], rc_recv.at[step], sibling).wait_recv()
        own = own + sib_in[step].astype(F32)
        if step < 3:
            first_out[step] = own.astype(BF16)
            copy = remote(
                first_out.at[step], first_in.at[step], rf_send.at[step], rf_recv.at[step], first_peer(step + 1)
            )
            copy.start()
            reduce_copies.append(copy)
        else:
            first_sum[...] = own

    def feature_part(index, carry):
        columns = pl.ds(pl.multiple_of(index * 512, 512), 512)
        fgrad[:, columns] = lax.dot_general(
            pre[...], wfull[columns, :], (((1,), (1,)), ((), ())), preferred_element_type=F32
        ).astype(BF16)
        return carry

    lax.fori_loop(0, 4, feature_part, 0)
    store = pltpu.make_async_copy(fgrad, fgrad_hbm, fgrad_sem)
    store.start()

    for step in range(3):
        remote(
            first_out.at[step], first_in.at[step], rf_send.at[step], rf_recv.at[step], first_peer(step + 1)
        ).wait_recv()

    def first_rows(at):
        rows = pl.ds(pl.multiple_of(at * 64, 64), 64)
        value = first_sum[rows, :]
        for step in range(3):
            value = value + first_in[step, rows, :].astype(F32)
        return value

    for step in range(3):
        second_out[step] = first_rows(around(second, step + 1)).astype(BF16)
        copy = remote(
            second_out.at[step], second_in.at[step], rs_send.at[step], rs_recv.at[step], second_peer(step + 1)
        )
        copy.start()
        reduce_copies.append(copy)
    second_sum = first_rows(second)
    for step in range(3):
        remote(
            second_out.at[step], second_in.at[step], rs_send.at[step], rs_recv.at[step], second_peer(step + 1)
        ).wait_recv()
        second_sum = second_sum + second_in[step].astype(F32)
    first_sum[0:64, :] = second_sum
    for step in range(3):
        rows = pl.ds(pl.multiple_of(around(x, step + 1) * 16, 16), 16)
        third_out[step] = first_sum[rows, :].astype(BF16)
        copy = remote(
            third_out.at[step], third_in.at[step], rx_send.at[step], rx_recv.at[step], x_peer(step + 1)
        )
        copy.start()
        reduce_copies.append(copy)
    value = first_sum[pl.ds(pl.multiple_of(x * 16, 16), 16), :]
    for step in range(3):
        remote(
            third_out.at[step], third_in.at[step], rx_send.at[step], rx_recv.at[step], x_peer(step + 1)
        ).wait_recv()
        value = value + third_in[step].astype(F32)
    wgrad_ref[...] = value * (1.0 / 256.0)

    for copy in started + lab_copies + norm_copies + reduce_copies:
        copy.wait_send()
    for index in range(6):
        ring(slot, 0, 1, index).wait_send()
    for index in range(8):
        beside(slot, 0, index).wait_send()

    @pl.when(jnp.logical_not(stays))
    def _():
        lab_swap.wait_send()
        for copy in swaps:
            copy.wait_send()
        for part in range(2):
            rows = pl.ds(part * HALF, HALF)
            remote(
                grad_out.at[rows], grad_in.at[rows], back_send.at[part], back_recv.at[part], partner
            ).wait_send()
        remote(aux_out, aux_in, back_send.at[2], back_recv.at[2], partner).wait_send()

    store.wait()


def body(features, weight, pair_ids, dup_ids):
    dma = pltpu.SemaphoreType.DMA
    vmem = pltpu.VMEM
    loss, feature_grad, weight_grad = pl.pallas_call(
        kernel,
        out_shape=(
            jax.ShapeDtypeStruct((1, ROWS), F32),
            jax.ShapeDtypeStruct((ROWS, FEAT), BF16),
            jax.ShapeDtypeStruct((16, EMB), F32),
        ),
        in_specs=[
            pl.BlockSpec(memory_space=pl.ANY),
            pl.BlockSpec(memory_space=vmem),
            pl.BlockSpec(memory_space=vmem),
            pl.BlockSpec(memory_space=vmem),
        ],
        out_specs=(
            pl.BlockSpec(memory_space=vmem),
            pl.BlockSpec(memory_space=pl.ANY),
            pl.BlockSpec(memory_space=vmem),
        ),
        scratch_shapes=[
            vmem((ROWS, FEAT), BF16),
            vmem((2, 4, 256, EMB), BF16),
            vmem((2, 4, 4, 4, 16, EMB), BF16),
            vmem((FEAT, EMB), BF16),
            vmem((ROWS, EMB), F32),
            vmem((ROWS, 128), F32),
            vmem((ROWS, EMB), BF16),
            vmem((8, ROWS, EMB), BF16),
            vmem((8, 8, ROWS), jnp.int32),
            vmem((8, ROWS), jnp.int32),
            vmem((ROWS, 8), jnp.int32),
            vmem((ROWS, HALF), F32),
            vmem((16, ROWS, HALF), F32),
            vmem((ROWS, 128), F32),
            vmem((ROWS, 128), F32),
            vmem((8, 8, ROWS), F32),
            vmem((ROWS, EMB), F32),
            vmem((ROWS, EMB), BF16),
            vmem((ROWS, EMB), BF16),
            vmem((8, ROWS), F32),
            vmem((8, ROWS), F32),
            vmem((ROWS, EMB), BF16),
            vmem((ROWS, FEAT), BF16),
            vmem((4, 256, EMB), BF16),
            vmem((4, 256, EMB), BF16),
            vmem((3, 256, EMB), BF16),
            vmem((3, 256, EMB), BF16),
            vmem((256, EMB), F32),
            vmem((3, 64, EMB), BF16),
            vmem((3, 64, EMB), BF16),
            vmem((3, 16, EMB), BF16),
            vmem((3, 16, EMB), BF16),
            dma,
            dma,
            dma((3,)),
            dma((3,)),
            dma((3,)),
            dma((3,)),
            dma((3, 4)),
            dma((3, 4)),
            dma((4,)),
            dma((4,)),
            dma((7,)),
            dma((8,)),
            dma((1,)),
            dma((1,)),
            dma((2,)),
            dma((2,)),
            dma((6,)),
            dma((8,)),
            dma((8, 2)),
            dma((7,)),
            dma((8,)),
            dma((3,)),
            dma((3,)),
            dma((4,)),
            dma((4,)),
            dma((3,)),
            dma((3,)),
            dma((3,)),
            dma((3,)),
            dma((3,)),
            dma((3,)),
        ],
        compiler_params=pltpu.CompilerParams(
            collective_id=0, has_side_effects=True, vmem_limit_bytes=56 << 20
        ),
        cost_estimate=pl.CostEstimate(
            flops=7_500_000_000, bytes_accessed=8 << 20, transcendentals=2 << 20
        ),
        name="infonce",
    )(features[0], weight, pair_ids, dup_ids)
    return loss, feature_grad[None], weight_grad


def solution(mesh):
    return jax.shard_map(
        body,
        mesh=mesh,
        in_specs=(
            P("rep", "loop", None),
            P(("loop", "rep"), None),
            P("rep", "loop"),
            P("rep", "loop"),
        ),
        out_specs=(P("rep", "loop"), P("rep", "loop", None), P(("loop", "rep"), None)),
        check_vma=False,
    )
```

```python
import jax
import jax.numpy as jnp
from jax import lax
from jax.experimental import pallas as pl
from jax.experimental.pallas import tpu as pltpu
from jax.sharding import PartitionSpec as P

MESH = pl.DeviceIdType.MESH
scale_logits = 20.0
norm_eps = 1e-06
ROWS = 512
FEAT = 2048
EMB = 512
HALF = 256
SLOPE = 28.853900817779268
BF16 = jnp.bfloat16
F32 = jnp.float32

ORDER = (
    (0, 3, 0),
    (0, 1, 0),
    (1, 0, 0),
    (0, 1, 1),
    (0, 3, 1),
    (1, 0, 1),
    (1, 3, 0),
    (1, 1, 0),
    (1, 1, 1),
    (1, 3, 1),
    (0, 2, 0),
    (0, 2, 1),
    (1, 2, 0),
    (1, 2, 1),
)
STEPS = (0, 1, 3, 2)
FAR_FIRST = (2, 1, 3, 0)
PLANE = (10, 6, 14, 9, 11, 2, 8, 5, 7, 13, 15, 1, 3, 4, 12)


def device_at(x, y, z, core):
    return (lax.rem(x, 2) * 4 + z, lax.div(x, 2) * 8 + y * 2 + core)


def remote(src, dst, send_sem, recv_sem, device):
    return pltpu.make_async_remote_copy(
        src_ref=src,
        dst_ref=dst,
        send_sem=send_sem,
        recv_sem=recv_sem,
        device_id=device,
        device_id_type=MESH,
    )


def pick(step, column):
    value = jnp.int32(0)
    for index, entry in enumerate(ORDER):
        if entry[column]:
            value = jnp.where(step == index, entry[column], value)
    return value


def to_column(rows):
    return rows.T


def kernel(
    feat_hbm,
    weight_ref,
    pair_ref,
    dup_ref,
    loss_ref,
    fgrad_hbm,
    wgrad_ref,
    feat,
    featp,
    wpart,
    wfull,
    normed,
    inverse,
    home_emb,
    emb,
    labels,
    label_home,
    row_pairs,
    row_dups,
    weights,
    dots,
    quot,
    acc,
    pos,
    norms,
    grad,
    grad_out,
    grad_in,
    aux_out,
    aux_in,
    pre,
    fgrad,
    sib_out,
    sib_in,
    own_term,
    first_out,
    first_in,
    first_sum,
    plane_out,
    plane_in,
    feat_sem,
    fgrad_sem,
    wp_send,
    wp_recv,
    wf_send,
    wf_recv,
    wc_send,
    wc_recv,
    lab_send,
    lab_recv,
    labx_send,
    labx_recv,
    swap_send,
    swap_recv,
    ring_send,
    sib_send,
    emb_recv,
    norm_send,
    norm_recv,
    back_send,
    back_recv,
    rc_send,
    rc_recv,
    rf_send,
    rf_recv,
    rp_send,
    rp_recv,
):
    loop, rep = lax.axis_index("loop"), lax.axis_index("rep")
    x_lo, z = lax.div(loop, 4), lax.rem(loop, 4)
    x_hi, y, core = lax.div(rep, 8), lax.rem(lax.div(rep, 2), 4), lax.rem(rep, 2)
    x = x_hi * 2 + x_lo
    other = 1 - core
    first = z * other + y * core
    second = y * other + z * core
    stays = core == x_lo
    slot = core * 4 + z

    def around(value, step):
        return lax.rem(value + step, 4)

    def plane_peer(index):
        step = index // 4
        return device_at(
            around(x, index % 4), around(y, step * other), around(z, step * core), core
        )

    def first_peer(step):
        return device_at(
            x, around(y, step * core), around(z, step * other), core
        )

    def z_peer(step, which):
        return device_at(x, y, around(z, step), which)

    sibling = device_at(x, y, z, other)
    partner = device_at(x_hi * 2 + 1 - x_lo, y, z, other)

    load = pltpu.make_async_copy(feat_hbm, feat, feat_sem)
    load.start()

    barrier = pltpu.get_barrier_semaphore()
    everyone = [sibling, partner] + [plane_peer(index) for index in range(1, 16)]
    for step in (1, 2, 3):
        everyone += [first_peer(step), z_peer(step, other)]
    for device in everyone:
        pl.semaphore_signal(barrier, inc=1, device_id=device, device_id_type=MESH)

    wpart[core, first, second, x] = weight_ref[...]
    label_home[...] = jnp.zeros((8, ROWS), jnp.int32)
    label_home[0:1, :] = pair_ref[...]
    label_home[1:2, :] = dup_ref[...]
    pl.semaphore_wait(barrier, len(everyone))

    started = []
    for index in PLANE:
        copy = remote(
            wpart.at[core, first, second, x],
            wpart.at[core, first, second, x],
            wp_send.at[index - 1],
            wp_recv.at[index - 1],
            plane_peer(index),
        )
        copy.start()
        started.append(copy)

    lab_swap = remote(label_home, labels.at[other * 4 + z], labx_send.at[0], labx_recv.at[0], partner)
    lab_swap_in = remote(label_home, labels.at[slot], labx_send.at[0], labx_recv.at[0], partner)

    @pl.when(jnp.logical_not(stays))
    def _():
        lab_swap.start()

    @pl.when(stays)
    def _():
        labels[slot] = label_home[...]

    load.wait()

    def transpose_slab(slab, carry):
        slab_xlo, slab_z, slab_xhi = lax.div(slab, 8), lax.rem(lax.div(slab, 2), 4), lax.rem(slab, 2)
        slab_x = slab_xhi * 2 + slab_xlo
        turned = feat[:, pl.ds(pl.multiple_of(slab * 128, 128), 128)].T
        for at_y in range(4):
            zero = pl.multiple_of((at_y * 4 + slab_x) * 16, 16)
            featp[0, slab_z, pl.ds(zero, 16), :] = turned[at_y * 32 : at_y * 32 + 16]
            one = pl.multiple_of((slab_z * 4 + slab_x) * 16, 16)
            featp[1, at_y, pl.ds(one, 16), :] = turned[at_y * 32 + 16 : at_y * 32 + 32]
        return carry

    def give(source_first, source_second, at):
        copy = remote(
            wpart.at[core, source_first, source_second],
            wpart.at[core, source_first, source_second],
            wc_send.at[at],
            wc_recv.at[at],
            sibling,
        )
        copy.start()
        started.append(copy)

    for piece in STEPS:
        source = around(second, 4 - piece)
        for index in range(piece * 4, piece * 4 + 4):
            if index:
                block = wpart.at[core, first, source, around(x, 4 - index % 4)]
                remote(
                    block, block, wp_send.at[index - 1], wp_recv.at[index - 1], plane_peer(index)
                ).wait_recv()
        for step in (2, 1, 3):
            copy = remote(
                wpart.at[core, first, source],
                wpart.at[core, first, source],
                wf_send.at[step - 1, piece],
                wf_recv.at[step - 1, piece],
                first_peer(step),
            )
            copy.start()
            started.append(copy)
        give(first, source, piece)

    lax.fori_loop(0, 16, transpose_slab, 0)

    @pl.when(jnp.logical_not(stays))
    def _():
        lab_swap_in.wait_recv()

    lab_copies = []
    for index, (step, which) in enumerate(
        [(0, other)] + [(step, which) for step in (1, 2, 3) for which in (core, other)]
    ):
        copy = remote(
            labels.at[slot],
            labels.at[slot],
            lab_send.at[index],
            lab_recv.at[slot],
            z_peer(step, which),
        )
        copy.start()
        lab_copies.append(copy)
    turned_labels = to_column(labels[slot])
    row_pairs[...] = jnp.broadcast_to(turned_labels[:, 0:1], (ROWS, 128))
    row_dups[...] = jnp.broadcast_to(turned_labels[:, 1:2], (ROWS, 128))

    for piece in STEPS:
        at = around(second, 4 - piece)
        for step in (1, 3, 2):
            source = around(first, 4 - step)
            remote(
                wpart.at[core, source, at],
                wpart.at[core, source, at],
                wf_send.at[step - 1, piece],
                wf_recv.at[step - 1, piece],
                first_peer(step),
            ).wait_recv()
            give(source, at, step * 4 + piece)
    for piece in STEPS:
        for step in range(4):
            block = wpart.at[other, around(second, 4 - step), around(first, 4 - piece)]
            at = step * 4 + piece
            remote(block, block, wc_send.at[at], wc_recv.at[at], sibling).wait_recv()

    def place_block(index, carry):
        at_first, at_second, at_x = lax.div(index, 16), lax.rem(lax.div(index, 4), 4), lax.rem(index, 4)
        base = lax.rem(at_x, 2) * 64 + lax.div(at_x, 2) * 8
        zero = (base + at_first * 16 + at_second * 2) * 16
        one = (base + at_second * 16 + at_first * 2 + 1) * 16
        wfull[pl.ds(pl.multiple_of(zero, 16), 16), :] = wpart[0, at_first, at_second, at_x]
        wfull[pl.ds(pl.multiple_of(one, 16), 16), :] = wpart[1, at_first, at_second, at_x]
        return carry

    lax.fori_loop(0, 64, place_block, 0, unroll=8)

    def half(ref, at, which):
        return ref.at[at, pl.ds(pl.multiple_of(which * HALF, HALF), HALF)]

    def ring(at, which, step, sem):
        return remote(
            half(emb, at, which), half(emb, at, which), ring_send.at[sem], emb_recv.at[at, which], z_peer(step, core)
        )

    def beside(at, which, sem):
        return remote(
            half(emb, at, which), half(emb, at, which), sib_send.at[sem], emb_recv.at[at, which], sibling
        )

    def send_own(part):
        ring(slot, part, 1, part).start()
        ring(slot, part, 3, 2 + part).start()
        beside(slot, part, part).start()

    swaps = [
        remote(
            home_emb.at[pl.ds(part * HALF, HALF)],
            emb.at[other * 4 + z, pl.ds(part * HALF, HALF)],
            swap_send.at[part],
            swap_recv.at[part],
            partner,
        )
        for part in range(2)
    ]
    for part in range(2):
        half_rows = pl.ds(part * HALF, HALF)
        normed[half_rows, :] = jnp.dot(feat[half_rows, :], wfull[...], preferred_element_type=F32)
        for start in range(part * HALF, part * HALF + HALF, 64):
            rows = pl.ds(start, 64)
            projected = normed[rows, :]
            scale = lax.rsqrt(jnp.sum(projected * projected, axis=1, keepdims=True) + norm_eps)
            unit = projected * scale
            normed[rows, :] = unit
            inverse[rows, :] = jnp.broadcast_to(scale, (64, 128))
            home_emb[rows, :] = unit.astype(BF16)

        @pl.when(jnp.logical_not(stays))
        def _():
            swaps[part].start()

        @pl.when(stays)
        def _():
            emb[slot, half_rows, :] = home_emb[half_rows, :]
            send_own(part)

    acc[...] = jnp.zeros((ROWS, 128), F32)
    pos[...] = jnp.zeros((ROWS, 128), F32)

    @pl.when(jnp.logical_not(stays))
    def _():
        for part in range(2):
            remote(
                home_emb.at[pl.ds(part * HALF, HALF)],
                emb.at[slot, pl.ds(part * HALF, HALF)],
                swap_send.at[part],
                swap_recv.at[part],
                partner,
            ).wait_recv()
            send_own(part)

    for index in range(7):
        other_slot = lax.rem(slot + 1 + index, 8)
        remote(
            labels.at[other_slot],
            labels.at[other_slot],
            lab_send.at[index],
            lab_recv.at[other_slot],
            sibling,
        ).wait_recv()

    def take(at, which, own):
        piece = at * 2 + which
        columns = pl.ds(pl.multiple_of(which * HALF, HALF), HALF)
        dots[...] = lax.dot_general(
            emb[slot], emb[at, columns, :], (((1,), (1,)), ((), ())), preferred_element_type=F32
        )
        for part in range(2):
            lanes = pl.ds(pl.multiple_of(which * HALF + part * 128, 128), 128)
            col_pair = labels[at, 0:1, lanes]
            col_dup = labels[at, 1:2, lanes]
            for start in range(0, ROWS, 64):
                rows = pl.ds(start, 64)
                power = dots[rows, part * 128 : (part + 1) * 128] * SLOPE - SLOPE
                value = jnp.exp2(power)
                mate = row_pairs[rows, :] == col_pair
                if own:
                    row_index = start + lax.broadcasted_iota(jnp.int32, (64, 128), 0)
                    col_index = which * HALF + part * 128 + lax.broadcasted_iota(jnp.int32, (64, 128), 1)
                    mate = jnp.logical_and(mate, row_index != col_index)
                apart = jnp.where(row_dups[rows, :] != col_dup, value, 0.0)
                paired = jnp.where(mate, value, 0.0)
                quot[piece, rows, part * 128 : (part + 1) * 128] = apart - paired
                acc[rows, :] += apart
                pos[rows, :] += paired

    def own_piece(part, carry):
        take(slot, part, True)
        return carry

    lax.fori_loop(0, 2, own_piece, 0)

    def next_piece(step, carry):
        which_ring = jnp.where(pick(step, 0) == 0, core, other)
        at = which_ring * 4 + around(z, pick(step, 1))
        which = pick(step, 2)
        ring(at, which, 1, 0).wait_recv()

        @pl.when(step == 0)
        def _():
            ring(at, which, 1, 4).start()
            beside(at, which, 2).start()

        @pl.when(step == 3)
        def _():
            ring(at, which, 3, 5).start()
            beside(at, which, 3).start()

        for index, count in ((1, 4), (4, 5), (10, 6), (11, 7)):

            @pl.when(step == index)
            def _():
                beside(at, which, count).start()

        take(at, which, False)
        return carry

    lax.fori_loop(0, len(ORDER), next_piece, 0)

    paired_row = jnp.sum(pos[...].T, axis=0, keepdims=True)
    total_row = jnp.sum(acc[...].T, axis=0, keepdims=True) + paired_row
    norms[slot] = jnp.broadcast_to(1.0 / total_row, (8, ROWS))
    norm_copies = []
    for index, (step, which) in enumerate(
        [(0, other)] + [(step, which) for step in (1, 2, 3) for which in (core, other)]
    ):
        copy = remote(
            norms.at[slot], norms.at[slot], norm_send.at[index], norm_recv.at[slot], z_peer(step, which)
        )
        copy.start()
        norm_copies.append(copy)
    aux_out[...] = jnp.broadcast_to(jnp.log(total_row) - jnp.log(paired_row), (8, ROWS))
    total = jnp.sum(acc[...] + pos[...], axis=1, keepdims=True)
    acc[...] = jnp.broadcast_to(1.0 / total, (ROWS, 128))

    def wait_norm(at):
        remote(norms.at[at], norms.at[at], norm_send.at[0], norm_recv.at[at], sibling).wait_recv()

    for part in range(2):
        rows = pl.ds(part * HALF, HALF)

        def add_slots(step, carry):
            at_z = around(z, jnp.where(step < 2, step, 5 - step))
            pair = (core * 4 + at_z, other * 4 + at_z)
            if part == 0:

                @pl.when(step > 0)
                def _():
                    wait_norm(pair[0])

                wait_norm(pair[1])
            for index, at in enumerate(pair):
                for lane in range(0, ROWS, 128):
                    norm = norms[at, 0:1, lane : lane + 128]
                    for start in range(0, HALF, 64):
                        take_rows = pl.ds(part * HALF + start, 64)
                        value = quot[at * 2 + lane // HALF, take_rows, lane % HALF : lane % HALF + 128]
                        weight = jnp.abs(value) * (acc[take_rows, :] + norm) - jnp.where(value < 0.0, 2.0, 0.0)
                        weights[start : start + 64, index * ROWS + lane : index * ROWS + lane + 128] = weight.astype(BF16)
            grad[rows, :] += jnp.dot(
                weights[:, :ROWS], emb[pair[0]], preferred_element_type=F32
            ) + jnp.dot(weights[:, ROWS:], emb[pair[1]], preferred_element_type=F32)
            return carry

        grad[rows, :] = jnp.zeros((HALF, EMB), F32)
        lax.fori_loop(0, 4, add_slots, 0)

        @pl.when(jnp.logical_not(stays))
        def _():
            unit = emb[slot, rows, :].astype(F32)
            whole = grad[rows, :]
            along = jnp.sum(unit * whole, axis=1, keepdims=True)
            grad_out[rows, :] = (whole - along * unit).astype(BF16)
            inner = jnp.broadcast_to(along, (HALF, 128)).T[0:1, :]
            aux_out[1:2, part * HALF : (part + 1) * HALF] = inner
            remote(
                grad_out.at[rows], grad_in.at[rows], back_send.at[part], back_recv.at[part], partner
            ).start()

    @pl.when(jnp.logical_not(stays))
    def _():
        remote(aux_out, aux_in, back_send.at[2], back_recv.at[2], partner).start()
        remote(aux_out, aux_in, back_send.at[2], back_recv.at[2], partner).wait_recv()
        columns_of = to_column(aux_in[...])
        loss_ref[...] = aux_in[0:1, :]
        for part in range(2):
            rows = pl.ds(part * HALF, HALF)
            remote(
                grad_out.at[rows], grad_in.at[rows], back_send.at[part], back_recv.at[part], partner
            ).wait_recv()
            along = columns_of[part * HALF : (part + 1) * HALF, 1:2]
            grad[rows, :] = grad_in[rows, :].astype(F32) + along * home_emb[rows, :].astype(F32)

    @pl.when(stays)
    def _():
        loss_ref[...] = aux_out[0:1, :]

    def finish(index, carry):
        rows = pl.ds(pl.multiple_of(index * 64, 64), 64)
        unit = normed[rows, :]
        whole = scale_logits * grad[rows, :]
        along = jnp.sum(unit * whole, axis=1, keepdims=True)
        pre[rows, :] = (inverse[rows, 0:1] * (whole - unit * along)).astype(BF16)
        return carry

    lax.fori_loop(0, 8, finish, 0, unroll=True)

    def term_of(which, at):
        return jnp.dot(featp[which, at], pre[...], preferred_element_type=F32)

    reduce_copies = []
    for at in range(4):
        term = term_of(other, at).astype(BF16)
        for group in range(4):
            sib_out[group, at] = term[group * 64 : group * 64 + 64]
    for index, offset in enumerate(FAR_FIRST):
        group = around(first, offset)
        copy = remote(sib_out.at[group], sib_in.at[group], rc_send.at[index], rc_recv.at[index], sibling)
        copy.start()
        reduce_copies.append(copy)
    for at in range(4):
        own_term[at] = term_of(core, at)
    for index, offset in enumerate(FAR_FIRST):
        group = around(second, offset)
        remote(
            sib_out.at[group], sib_in.at[group], rc_send.at[index], rc_recv.at[index], sibling
        ).wait_recv()
        rows = pl.ds(pl.multiple_of(group * 64, 64), 64)
        for count, step in enumerate(FAR_FIRST):
            at = around(first, step)
            value = own_term[at, rows, :] + sib_in[group, at].astype(F32)
            if step:
                first_out[index, count] = value.astype(BF16)
                copy = remote(
                    first_out.at[index, count],
                    first_in.at[index, count],
                    rf_send.at[index * 3 + count],
                    rf_recv.at[index * 3 + count],
                    first_peer(step),
                )
                copy.start()
                reduce_copies.append(copy)
            else:
                first_sum[index] = value

    def feature_part(index, carry):
        columns = pl.ds(pl.multiple_of(index * 512, 512), 512)
        fgrad[:, columns] = lax.dot_general(
            pre[...], wfull[columns, :], (((1,), (1,)), ((), ())), preferred_element_type=F32
        ).astype(BF16)
        return carry

    lax.fori_loop(0, 4, feature_part, 0)
    store = pltpu.make_async_copy(fgrad, fgrad_hbm, fgrad_sem)
    store.start()

    for index, offset in enumerate(FAR_FIRST):
        whole = first_sum[index]
        for count in (1, 2, 0):
            remote(
                first_out.at[index, count],
                first_in.at[index, count],
                rf_send.at[index * 3 + count],
                rf_recv.at[index * 3 + count],
                first_peer(1),
            ).wait_recv()
            whole = whole + first_in[index, count].astype(F32)
        plane_out[index] = whole.astype(BF16)
        for step in FAR_FIRST:
            target = offset * 4 + step
            if target:
                copy = remote(
                    plane_out.at[index, pl.ds(pl.multiple_of(around(x, step) * 16, 16), 16)],
                    plane_in.at[target - 1],
                    rp_send.at[target - 1],
                    rp_recv.at[target - 1],
                    plane_peer(target),
                )
                copy.start()
                reduce_copies.append(copy)
        if offset == 0:
            first_sum[index] = whole
    value = first_sum[3, pl.ds(pl.multiple_of(x * 16, 16), 16), :]
    for offset in FAR_FIRST:
        for step in (1, 3, 2, 0):
            target = offset * 4 + step
            if target:
                remote(
                    plane_out.at[0, pl.ds(0, 16)],
                    plane_in.at[target - 1],
                    rp_send.at[target - 1],
                    rp_recv.at[target - 1],
                    plane_peer(target),
                ).wait_recv()
                value = value + plane_in[target - 1].astype(F32)
    wgrad_ref[...] = value * (1.0 / 256.0)

    for copy in started + lab_copies + norm_copies + reduce_copies:
        copy.wait_send()
    for index in range(6):
        ring(slot, 0, 1, index).wait_send()
    for index in range(8):
        beside(slot, 0, index).wait_send()

    @pl.when(jnp.logical_not(stays))
    def _():
        lab_swap.wait_send()
        for copy in swaps:
            copy.wait_send()
        for part in range(2):
            rows = pl.ds(part * HALF, HALF)
            remote(
                grad_out.at[rows], grad_in.at[rows], back_send.at[part], back_recv.at[part], partner
            ).wait_send()
        remote(aux_out, aux_in, back_send.at[2], back_recv.at[2], partner).wait_send()

    store.wait()


def deliver(loss_in, fgrad_in, wgrad_in, loss_out, fgrad_out, wgrad_out, loss, fgrad, wgrad, load_sem, store_sem):
    parts = [
        (fgrad_in.at[pl.ds(at, 128)], fgrad.at[pl.ds(at, 128)], fgrad_out.at[pl.ds(at, 128)])
        for at in range(0, ROWS, 128)
    ]
    parts += [(loss_in, loss, loss_out), (wgrad_in, wgrad, wgrad_out)]
    loads = [
        pltpu.make_async_copy(source, held, load_sem.at[index]) for index, (source, held, _) in enumerate(parts)
    ]
    stores = [
        pltpu.make_async_copy(held, target, store_sem.at[index]) for index, (_, held, target) in enumerate(parts)
    ]
    for copy in loads:
        copy.start()
    for load, store in zip(loads, stores):
        load.wait()
        store.start()
    for store in stores:
        store.wait()


def body(features, weight, pair_ids, dup_ids):
    dma = pltpu.SemaphoreType.DMA
    vmem = pltpu.VMEM
    loss, feature_grad, weight_grad = pl.pallas_call(
        kernel,
        out_shape=(
            jax.ShapeDtypeStruct((1, ROWS), F32),
            jax.ShapeDtypeStruct((ROWS, FEAT), BF16),
            jax.ShapeDtypeStruct((16, EMB), F32),
        ),
        in_specs=[
            pl.BlockSpec(memory_space=pl.ANY),
            pl.BlockSpec(memory_space=vmem),
            pl.BlockSpec(memory_space=vmem),
            pl.BlockSpec(memory_space=vmem),
        ],
        out_specs=(
            pl.BlockSpec(memory_space=vmem),
            pl.BlockSpec(memory_space=pl.ANY),
            pl.BlockSpec(memory_space=vmem),
        ),
        scratch_shapes=[
            vmem((ROWS, FEAT), BF16),
            vmem((2, 4, 256, EMB), BF16),
            vmem((2, 4, 4, 4, 16, EMB), BF16),
            vmem((FEAT, EMB), BF16),
            vmem((ROWS, EMB), F32),
            vmem((ROWS, 128), F32),
            vmem((ROWS, EMB), BF16),
            vmem((8, ROWS, EMB), BF16),
            vmem((8, 8, ROWS), jnp.int32),
            vmem((8, ROWS), jnp.int32),
            vmem((ROWS, 128), jnp.int32),
            vmem((ROWS, 128), jnp.int32),
            vmem((HALF, 2 * ROWS), BF16),
            vmem((ROWS, HALF), F32),
            vmem((16, ROWS, HALF), F32),
            vmem((ROWS, 128), F32),
            vmem((ROWS, 128), F32),
            vmem((8, 8, ROWS), F32),
            vmem((ROWS, EMB), F32),
            vmem((ROWS, EMB), BF16),
            vmem((ROWS, EMB), BF16),
            vmem((8, ROWS), F32),
            vmem((8, ROWS), F32),
            vmem((ROWS, EMB), BF16),
            vmem((ROWS, FEAT), BF16),
            vmem((4, 4, 64, EMB), BF16),
            vmem((4, 4, 64, EMB), BF16),
            vmem((4, 256, EMB), F32),
            vmem((4, 3, 64, EMB), BF16),
            vmem((4, 3, 64, EMB), BF16),
            vmem((4, 64, EMB), F32),
            vmem((4, 64, EMB), BF16),
            vmem((15, 16, EMB), BF16),
            dma,
            dma,
            dma((15,)),
            dma((15,)),
            dma((3, 4)),
            dma((3, 4)),
            dma((16,)),
            dma((16,)),
            dma((7,)),
            dma((8,)),
            dma((1,)),
            dma((1,)),
            dma((2,)),
            dma((2,)),
            dma((6,)),
            dma((8,)),
            dma((8, 2)),
            dma((7,)),
            dma((8,)),
            dma((3,)),
            dma((3,)),
            dma((4,)),
            dma((4,)),
            dma((12,)),
            dma((12,)),
            dma((15,)),
            dma((15,)),
        ],
        compiler_params=pltpu.CompilerParams(
            collective_id=0, has_side_effects=True, vmem_limit_bytes=56 << 20
        ),
        cost_estimate=pl.CostEstimate(
            flops=7_500_000_000, bytes_accessed=8 << 20, transcendentals=2 << 20
        ),
        name="infonce",
    )(features[0], weight, pair_ids, dup_ids)
    anywhere = pl.BlockSpec(memory_space=pl.ANY)
    loss, feature_grad, weight_grad = pl.pallas_call(
        deliver,
        out_shape=(
            jax.ShapeDtypeStruct((1, ROWS), F32),
            jax.ShapeDtypeStruct((ROWS, FEAT), BF16),
            jax.ShapeDtypeStruct((16, EMB), F32),
        ),
        in_specs=[anywhere] * 3,
        out_specs=(anywhere,) * 3,
        scratch_shapes=[
            vmem((1, ROWS), F32),
            vmem((ROWS, FEAT), BF16),
            vmem((16, EMB), F32),
            dma((6,)),
            dma((6,)),
        ],
        name="deliver",
    )(loss, feature_grad, weight_grad)
    return loss, feature_grad[None], weight_grad


def solution(mesh):
    return jax.shard_map(
        body,
        mesh=mesh,
        in_specs=(
            P("rep", "loop", None),
            P(("loop", "rep"), None),
            P("rep", "loop"),
            P("rep", "loop"),
        ),
        out_specs=(P("rep", "loop"), P("rep", "loop", None), P(("loop", "rep"), None)),
        check_vma=False,
    )
```

```python
import jax
import jax.numpy as jnp
from jax import lax
from jax.experimental import pallas as pl
from jax.experimental.pallas import tpu as pltpu
from jax.sharding import PartitionSpec as P

MESH = pl.DeviceIdType.MESH
scale_logits = 20.0
norm_eps = 1e-06
ROWS = 512
FEAT = 2048
EMB = 512
HALF = 256
SLOPE = 28.853900817779268
BF16 = jnp.bfloat16
F32 = jnp.float32

ORDER = (
    (0, 3, 0),
    (0, 1, 0),
    (1, 0, 0),
    (0, 1, 1),
    (0, 3, 1),
    (1, 0, 1),
    (1, 3, 0),
    (1, 1, 0),
    (1, 1, 1),
    (1, 3, 1),
    (0, 2, 0),
    (0, 2, 1),
    (1, 2, 0),
    (1, 2, 1),
)
STEPS = (0, 1, 3, 2)
FAR_FIRST = (2, 1, 3, 0)
PLANE = (10, 6, 14, 9, 11, 2, 8, 5, 7, 13, 15, 1, 3, 4, 12)


def device_at(x, y, z, core):
    return (lax.rem(x, 2) * 4 + z, lax.div(x, 2) * 8 + y * 2 + core)


def remote(src, dst, send_sem, recv_sem, device):
    return pltpu.make_async_remote_copy(
        src_ref=src,
        dst_ref=dst,
        send_sem=send_sem,
        recv_sem=recv_sem,
        device_id=device,
        device_id_type=MESH,
    )


def pick(step, column):
    value = jnp.int32(0)
    for index, entry in enumerate(ORDER):
        if entry[column]:
            value = jnp.where(step == index, entry[column], value)
    return value


def to_column(rows):
    return rows.T


def kernel(
    feat_hbm,
    weight_ref,
    pair_ref,
    dup_ref,
    loss_ref,
    fgrad_hbm,
    wgrad_ref,
    feat,
    work,
    featp,
    wpart,
    wfull,
    normed,
    inverse,
    home_emb,
    emb,
    labels,
    label_home,
    row_pairs,
    row_dups,
    weights,
    dots,
    quot,
    acc,
    pos,
    norms,
    grad,
    loss_out,
    loss_in,
    pre,
    home_pre,
    fgrad,
    sib_out,
    sib_in,
    own_term,
    first_out,
    first_in,
    first_sum,
    plane_out,
    plane_in,
    feat_sem,
    fgrad_sem,
    wp_send,
    wp_recv,
    wf_send,
    wf_recv,
    wc_send,
    wc_recv,
    lab_send,
    lab_recv,
    labx_send,
    labx_recv,
    swap_send,
    swap_recv,
    ring_send,
    sib_send,
    emb_recv,
    norm_send,
    norm_recv,
    back_send,
    back_recv,
    loss_send,
    loss_recv,
    feat_send,
    feat_recv,
    rc_send,
    rc_recv,
    rf_send,
    rf_recv,
    rp_send,
    rp_recv,
):
    loop, rep = lax.axis_index("loop"), lax.axis_index("rep")
    x_lo, z = lax.div(loop, 4), lax.rem(loop, 4)
    x_hi, y, core = lax.div(rep, 8), lax.rem(lax.div(rep, 2), 4), lax.rem(rep, 2)
    x = x_hi * 2 + x_lo
    other = 1 - core
    first = z * other + y * core
    second = y * other + z * core
    stays = core == x_lo
    slot = z * 2 + core

    def around(value, step):
        return lax.rem(value + step, 4)

    def plane_peer(index):
        step = index // 4
        return device_at(
            around(x, index % 4), around(y, step * other), around(z, step * core), core
        )

    def first_peer(step):
        return device_at(
            x, around(y, step * core), around(z, step * other), core
        )

    def z_peer(step, which):
        return device_at(x, y, around(z, step), which)

    sibling = device_at(x, y, z, other)
    partner = device_at(x_hi * 2 + 1 - x_lo, y, z, other)

    load = pltpu.make_async_copy(feat_hbm, feat, feat_sem)
    load.start()

    barrier = pltpu.get_barrier_semaphore()
    everyone = [sibling, partner] + [plane_peer(index) for index in range(1, 16)]
    for step in (1, 2, 3):
        everyone += [first_peer(step), z_peer(step, other)]
    for device in everyone:
        pl.semaphore_signal(barrier, inc=1, device_id=device, device_id_type=MESH)

    wpart[core, first, second, x] = weight_ref[...]
    label_home[...] = jnp.zeros((8, ROWS), jnp.int32)
    label_home[0:1, :] = pair_ref[...]
    label_home[1:2, :] = dup_ref[...]
    pl.semaphore_wait(barrier, len(everyone))

    started = []
    for index in PLANE:
        copy = remote(
            wpart.at[core, first, second, x],
            wpart.at[core, first, second, x],
            wp_send.at[index - 1],
            wp_recv.at[index - 1],
            plane_peer(index),
        )
        copy.start()
        started.append(copy)

    lab_swap = remote(label_home, labels.at[z * 2 + other], labx_send.at[0], labx_recv.at[0], partner)
    lab_swap_in = remote(label_home, labels.at[slot], labx_send.at[0], labx_recv.at[0], partner)

    @pl.when(jnp.logical_not(stays))
    def _():
        lab_swap.start()

    @pl.when(stays)
    def _():
        labels[slot] = label_home[...]

    load.wait()

    def transpose_half(source, part):
        rows = pl.ds(part * HALF, HALF)

        def transpose_slab(slab, carry):
            slab_xlo, slab_z, slab_xhi = lax.div(slab, 8), lax.rem(lax.div(slab, 2), 4), lax.rem(slab, 2)
            slab_x = slab_xhi * 2 + slab_xlo
            turned = source[rows, pl.ds(pl.multiple_of(slab * 128, 128), 128)].T
            for at_y in range(4):
                zero = pl.multiple_of((slab_z * 4 + slab_x) * 16, 16)
                featp[0, at_y, pl.ds(zero, 16), rows] = turned[at_y * 32 : at_y * 32 + 16]
                one = pl.multiple_of((at_y * 4 + slab_x) * 16, 16)
                featp[1, slab_z, pl.ds(one, 16), rows] = turned[at_y * 32 + 16 : at_y * 32 + 32]
            return carry

        lax.fori_loop(0, 16, transpose_slab, 0)

    def give(source_first, source_second, at):
        copy = remote(
            wpart.at[core, source_first, source_second],
            wpart.at[core, source_first, source_second],
            wc_send.at[at],
            wc_recv.at[at],
            sibling,
        )
        copy.start()
        started.append(copy)

    for piece in STEPS:
        source = around(second, 4 - piece)
        for index in range(piece * 4, piece * 4 + 4):
            if index:
                block = wpart.at[core, first, source, around(x, 4 - index % 4)]
                remote(
                    block, block, wp_send.at[index - 1], wp_recv.at[index - 1], plane_peer(index)
                ).wait_recv()
        for step in (2, 1, 3):
            copy = remote(
                wpart.at[core, first, source],
                wpart.at[core, first, source],
                wf_send.at[step - 1, piece],
                wf_recv.at[step - 1, piece],
                first_peer(step),
            )
            copy.start()
            started.append(copy)
        give(first, source, piece)

    def follow(chunk):
        rows = pl.ds(chunk * 128, 128)
        return remote(feat.at[rows], work.at[rows], feat_send.at[chunk], feat_recv.at[chunk], partner)

    @pl.when(jnp.logical_not(stays))
    def _():
        follow(0).start()
        follow(1).start()

    @pl.when(stays)
    def _():
        for part in range(2):
            transpose_half(feat, part)

    @pl.when(jnp.logical_not(stays))
    def _():
        lab_swap_in.wait_recv()

    lab_copies = []
    for index, (step, which) in enumerate(
        [(0, other)] + [(step, which) for step in (1, 2, 3) for which in (core, other)]
    ):
        copy = remote(
            labels.at[slot],
            labels.at[slot],
            lab_send.at[index],
            lab_recv.at[slot],
            z_peer(step, which),
        )
        copy.start()
        lab_copies.append(copy)
    turned_labels = to_column(labels[slot])
    row_pairs[...] = jnp.broadcast_to(turned_labels[:, 0:1], (ROWS, 128))
    row_dups[...] = jnp.broadcast_to(turned_labels[:, 1:2], (ROWS, 128))

    for piece in STEPS:
        at = around(second, 4 - piece)
        for step in (1, 3, 2):
            source = around(first, 4 - step)
            remote(
                wpart.at[core, source, at],
                wpart.at[core, source, at],
                wf_send.at[step - 1, piece],
                wf_recv.at[step - 1, piece],
                first_peer(step),
            ).wait_recv()
            give(source, at, step * 4 + piece)
    for piece in STEPS:
        for step in range(4):
            block = wpart.at[other, around(second, 4 - step), around(first, 4 - piece)]
            at = step * 4 + piece
            remote(block, block, wc_send.at[at], wc_recv.at[at], sibling).wait_recv()

    def place_block(index, carry):
        at_first, at_second, at_x = lax.div(index, 16), lax.rem(lax.div(index, 4), 4), lax.rem(index, 4)
        base = lax.rem(at_x, 2) * 64 + lax.div(at_x, 2) * 8
        zero = (base + at_first * 16 + at_second * 2) * 16
        one = (base + at_second * 16 + at_first * 2 + 1) * 16
        wfull[pl.ds(pl.multiple_of(zero, 16), 16), :] = wpart[0, at_first, at_second, at_x]
        wfull[pl.ds(pl.multiple_of(one, 16), 16), :] = wpart[1, at_first, at_second, at_x]
        return carry

    lax.fori_loop(0, 64, place_block, 0, unroll=8)

    def half(ref, at, which):
        return ref.at[at, pl.ds(pl.multiple_of(which * HALF, HALF), HALF)]

    def ring(at, which, step, sem):
        return remote(
            half(emb, at, which), half(emb, at, which), ring_send.at[sem], emb_recv.at[at, which], z_peer(step, core)
        )

    def beside(at, which, sem):
        return remote(
            half(emb, at, which), half(emb, at, which), sib_send.at[sem], emb_recv.at[at, which], sibling
        )

    def send_own(part):
        ring(slot, part, 1, part).start()
        ring(slot, part, 3, 2 + part).start()
        beside(slot, part, part).start()

    swaps = [
        remote(
            home_emb.at[pl.ds(part * HALF, HALF)],
            emb.at[z * 2 + other, pl.ds(part * HALF, HALF)],
            swap_send.at[part],
            swap_recv.at[part],
            partner,
        )
        for part in range(2)
    ]
    def project(source, part):
        half_rows = pl.ds(part * HALF, HALF)
        normed[half_rows, :] = jnp.dot(source[half_rows, :], wfull[...], preferred_element_type=F32)
        for start in range(part * HALF, part * HALF + HALF, 64):
            rows = pl.ds(start, 64)
            projected = normed[rows, :]
            scale = lax.rsqrt(jnp.sum(projected * projected, axis=1, keepdims=True) + norm_eps)
            normed[rows, :] = projected * scale
            inverse[rows, :] = jnp.broadcast_to(scale, (64, 128))

    for part in range(2):
        half_rows = pl.ds(part * HALF, HALF)
        project(feat, part)
        home_emb[half_rows, :] = normed[half_rows, :].astype(BF16)

        @pl.when(jnp.logical_not(stays))
        def _():
            swaps[part].start()

        @pl.when(stays)
        def _():
            emb[slot, half_rows, :] = home_emb[half_rows, :]
            send_own(part)

    acc[...] = jnp.zeros((ROWS, 128), F32)
    pos[...] = jnp.zeros((ROWS, 128), F32)

    @pl.when(jnp.logical_not(stays))
    def _():
        for part in range(2):
            remote(
                home_emb.at[pl.ds(part * HALF, HALF)],
                emb.at[slot, pl.ds(part * HALF, HALF)],
                swap_send.at[part],
                swap_recv.at[part],
                partner,
            ).wait_recv()
            send_own(part)
        follow(2).start()
        follow(3).start()

    for index in range(7):
        other_slot = lax.rem(slot + 1 + index, 8)
        remote(
            labels.at[other_slot],
            labels.at[other_slot],
            lab_send.at[index],
            lab_recv.at[other_slot],
            sibling,
        ).wait_recv()

    def take(at, which, own):
        piece = at * 2 + which
        columns = pl.ds(pl.multiple_of(which * HALF, HALF), HALF)
        dots[...] = lax.dot_general(
            emb[slot], emb[at, columns, :], (((1,), (1,)), ((), ())), preferred_element_type=F32
        )
        for part in range(2):
            lanes = pl.ds(pl.multiple_of(which * HALF + part * 128, 128), 128)
            col_pair = labels[at, 0:1, lanes]
            col_dup = labels[at, 1:2, lanes]
            for start in range(0, ROWS, 64):
                rows = pl.ds(start, 64)
                power = dots[rows, part * 128 : (part + 1) * 128] * SLOPE - SLOPE
                value = jnp.exp2(power)
                mate = row_pairs[rows, :] == col_pair
                if own:
                    row_index = start + lax.broadcasted_iota(jnp.int32, (64, 128), 0)
                    col_index = which * HALF + part * 128 + lax.broadcasted_iota(jnp.int32, (64, 128), 1)
                    mate = jnp.logical_and(mate, row_index != col_index)
                apart = jnp.where(row_dups[rows, :] != col_dup, value, 0.0)
                paired = jnp.where(mate, value, 0.0)
                quot[piece, rows, part * 128 : (part + 1) * 128] = apart - paired
                acc[rows, :] += apart
                pos[rows, :] += paired

    def own_piece(part, carry):
        take(slot, part, True)
        return carry

    lax.fori_loop(0, 2, own_piece, 0)

    def next_piece(step, carry):
        which_ring = jnp.where(pick(step, 0) == 0, core, other)
        at = around(z, pick(step, 1)) * 2 + which_ring
        which = pick(step, 2)
        ring(at, which, 1, 0).wait_recv()

        @pl.when(step == 0)
        def _():
            ring(at, which, 1, 4).start()
            beside(at, which, 2).start()

        @pl.when(step == 3)
        def _():
            ring(at, which, 3, 5).start()
            beside(at, which, 3).start()

        for index, count in ((1, 4), (4, 5), (10, 6), (11, 7)):

            @pl.when(step == index)
            def _():
                beside(at, which, count).start()

        take(at, which, False)
        for part in range(2):

            @pl.when(jnp.logical_and(step == (5, 11)[part], jnp.logical_not(stays)))
            def _():
                follow(2 * part).wait_recv()
                follow(2 * part + 1).wait_recv()
                project(work, part)
                transpose_half(work, part)

        return carry

    lax.fori_loop(0, len(ORDER), next_piece, 0)

    paired_row = jnp.sum(pos[...].T, axis=0, keepdims=True)
    total_row = jnp.sum(acc[...].T, axis=0, keepdims=True) + paired_row
    norms[slot] = jnp.broadcast_to(1.0 / total_row, (8, ROWS))
    norm_copies = []
    for index, (step, which) in enumerate(
        [(0, other)] + [(step, which) for step in (1, 2, 3) for which in (core, other)]
    ):
        copy = remote(
            norms.at[slot], norms.at[slot], norm_send.at[index], norm_recv.at[slot], z_peer(step, which)
        )
        copy.start()
        norm_copies.append(copy)
    loss_out[...] = jnp.broadcast_to(jnp.log(total_row) - jnp.log(paired_row), (8, ROWS))
    total = jnp.sum(acc[...] + pos[...], axis=1, keepdims=True)
    acc[...] = jnp.broadcast_to(1.0 / total, (ROWS, 128))

    def wait_norm(at):
        remote(norms.at[at], norms.at[at], norm_send.at[0], norm_recv.at[at], sibling).wait_recv()

    loss_back = remote(loss_out, loss_in, loss_send, loss_recv, partner)

    @pl.when(jnp.logical_not(stays))
    def _():
        loss_back.start()

    def back(part):
        rows = pl.ds(part * HALF, HALF)
        return remote(pre.at[rows], home_pre.at[rows], back_send.at[part], back_recv.at[part], partner)

    for part in range(2):
        rows = pl.ds(part * HALF, HALF)
        for step in STEPS:
            pair = around(z, step)
            if part == 0:
                if step:
                    wait_norm(pair * 2 + core)
                wait_norm(pair * 2 + other)
            buffer = step % 2
            for index in range(4):
                for lane in range(0, HALF, 128):
                    column = (index % 2) * HALF + lane
                    norm = norms[pair * 2 + index // 2, 0:1, column : column + 128]
                    for start in range(0, HALF, 64):
                        take_rows = pl.ds(part * HALF + start, 64)
                        value = quot[pair * 4 + index, take_rows, lane : lane + 128]
                        weight = jnp.abs(value) * (acc[take_rows, :] + norm) - jnp.where(value < 0.0, 2.0, 0.0)
                        weights[buffer, start : start + 64, index * HALF + lane : index * HALF + lane + 128] = (
                            weight.astype(BF16)
                        )
            term = jnp.dot(
                weights[buffer],
                emb[pl.ds(pair * 2, 2)].reshape(2 * ROWS, EMB),
                preferred_element_type=F32,
            )
            if step:
                grad[rows, :] += term
            else:
                grad[rows, :] = term

        for start in range(part * HALF, part * HALF + HALF, 64):
            tile = pl.ds(start, 64)
            unit = normed[tile, :]
            whole = scale_logits * grad[tile, :]
            along = jnp.sum(unit * whole, axis=1, keepdims=True)
            pre[tile, :] = (inverse[tile, 0:1] * (whole - unit * along)).astype(BF16)

        @pl.when(jnp.logical_not(stays))
        def _():
            back(part).start()

        @pl.when(stays)
        def _():
            home_pre[rows, :] = pre[rows, :]

    reduce_copies = []
    for index, offset in enumerate(FAR_FIRST):
        group = around(first, offset)
        sib_out[group] = jnp.dot(featp[other, group], pre[...], preferred_element_type=F32).astype(BF16)
        copy = remote(sib_out.at[group], sib_in.at[group], rc_send.at[index], rc_recv.at[index], sibling)
        copy.start()
        reduce_copies.append(copy)
    for at in range(4):
        own_term[at] = jnp.dot(featp[core, at], pre[...], preferred_element_type=F32)
    for index, offset in enumerate(FAR_FIRST):
        group = around(second, offset)
        remote(
            sib_out.at[group], sib_in.at[group], rc_send.at[index], rc_recv.at[index], sibling
        ).wait_recv()
        for count, step in enumerate(FAR_FIRST):
            rows = pl.ds(pl.multiple_of(around(first, step) * 64, 64), 64)
            value = own_term[group, rows, :] + sib_in[group, rows, :].astype(F32)
            if step:
                first_out[index, count] = value.astype(BF16)
                copy = remote(
                    first_out.at[index, count],
                    first_in.at[index, count],
                    rf_send.at[index * 3 + count],
                    rf_recv.at[index * 3 + count],
                    first_peer(step),
                )
                copy.start()
                reduce_copies.append(copy)
            else:
                first_sum[index] = value

    for index, offset in enumerate(FAR_FIRST):
        whole = first_sum[index]
        for count in (1, 2, 0):
            remote(
                first_out.at[index, count],
                first_in.at[index, count],
                rf_send.at[index * 3 + count],
                rf_recv.at[index * 3 + count],
                first_peer(1),
            ).wait_recv()
            whole = whole + first_in[index, count].astype(F32)
        plane_out[index] = whole.astype(BF16)
        for step in FAR_FIRST:
            target = offset * 4 + step
            if target:
                copy = remote(
                    plane_out.at[index, pl.ds(pl.multiple_of(around(x, step) * 16, 16), 16)],
                    plane_in.at[target - 1],
                    rp_send.at[target - 1],
                    rp_recv.at[target - 1],
                    plane_peer(target),
                )
                copy.start()
                reduce_copies.append(copy)
        if offset == 0:
            first_sum[index] = whole
    @pl.when(jnp.logical_not(stays))
    def _():
        loss_back.wait_recv()
        for part in range(2):
            back(part).wait_recv()
        loss_ref[...] = loss_in[0:1, :]

    @pl.when(stays)
    def _():
        loss_ref[...] = loss_out[0:1, :]

    def feature_part(index, carry):
        columns = pl.ds(pl.multiple_of(index * 512, 512), 512)
        fgrad[:, columns] = lax.dot_general(
            home_pre[...], wfull[columns, :], (((1,), (1,)), ((), ())), preferred_element_type=F32
        ).astype(BF16)
        return carry

    lax.fori_loop(0, 4, feature_part, 0)
    store = pltpu.make_async_copy(fgrad, fgrad_hbm, fgrad_sem)
    store.start()

    value = first_sum[3, pl.ds(pl.multiple_of(x * 16, 16), 16), :]
    for offset in FAR_FIRST:
        for step in (1, 3, 2, 0):
            target = offset * 4 + step
            if target:
                remote(
                    plane_out.at[0, pl.ds(0, 16)],
                    plane_in.at[target - 1],
                    rp_send.at[target - 1],
                    rp_recv.at[target - 1],
                    plane_peer(target),
                ).wait_recv()
                value = value + plane_in[target - 1].astype(F32)
    wgrad_ref[...] = value * (1.0 / 256.0)

    for copy in started + lab_copies + norm_copies + reduce_copies:
        copy.wait_send()
    for index in range(6):
        ring(slot, 0, 1, index).wait_send()
    for index in range(8):
        beside(slot, 0, index).wait_send()

    @pl.when(jnp.logical_not(stays))
    def _():
        lab_swap.wait_send()
        for copy in swaps:
            copy.wait_send()
        loss_back.wait_send()
        for part in range(2):
            back(part).wait_send()
        for chunk in range(4):
            follow(chunk).wait_send()

    store.wait()


def deliver(loss_in, fgrad_in, wgrad_in, loss_out, fgrad_out, wgrad_out, loss, fgrad, wgrad, load_sem, store_sem):
    parts = [
        (fgrad_in.at[pl.ds(at, 128)], fgrad.at[pl.ds(at, 128)], fgrad_out.at[pl.ds(at, 128)])
        for at in range(0, ROWS, 128)
    ]
    parts += [(loss_in, loss, loss_out), (wgrad_in, wgrad, wgrad_out)]
    loads = [
        pltpu.make_async_copy(source, held, load_sem.at[index]) for index, (source, held, _) in enumerate(parts)
    ]
    stores = [
        pltpu.make_async_copy(held, target, store_sem.at[index]) for index, (_, held, target) in enumerate(parts)
    ]
    for copy in loads:
        copy.start()
    for load, store in zip(loads, stores):
        load.wait()
        store.start()
    for store in stores:
        store.wait()


def body(features, weight, pair_ids, dup_ids):
    dma = pltpu.SemaphoreType.DMA
    vmem = pltpu.VMEM
    loss, feature_grad, weight_grad = pl.pallas_call(
        kernel,
        out_shape=(
            jax.ShapeDtypeStruct((1, ROWS), F32),
            jax.ShapeDtypeStruct((ROWS, FEAT), BF16),
            jax.ShapeDtypeStruct((16, EMB), F32),
        ),
        in_specs=[
            pl.BlockSpec(memory_space=pl.ANY),
            pl.BlockSpec(memory_space=vmem),
            pl.BlockSpec(memory_space=vmem),
            pl.BlockSpec(memory_space=vmem),
        ],
        out_specs=(
            pl.BlockSpec(memory_space=vmem),
            pl.BlockSpec(memory_space=pl.ANY),
            pl.BlockSpec(memory_space=vmem),
        ),
        scratch_shapes=[
            vmem((ROWS, FEAT), BF16),
            vmem((ROWS, FEAT), BF16),
            vmem((2, 4, 256, EMB), BF16),
            vmem((2, 4, 4, 4, 16, EMB), BF16),
            vmem((FEAT, EMB), BF16),
            vmem((ROWS, EMB), F32),
            vmem((ROWS, 128), F32),
            vmem((ROWS, EMB), BF16),
            vmem((8, ROWS, EMB), BF16),
            vmem((8, 8, ROWS), jnp.int32),
            vmem((8, ROWS), jnp.int32),
            vmem((ROWS, 128), jnp.int32),
            vmem((ROWS, 128), jnp.int32),
            vmem((2, HALF, 2 * ROWS), BF16),
            vmem((ROWS, HALF), F32),
            vmem((16, ROWS, HALF), F32),
            vmem((ROWS, 128), F32),
            vmem((ROWS, 128), F32),
            vmem((8, 8, ROWS), F32),
            vmem((ROWS, EMB), F32),
            vmem((8, ROWS), F32),
            vmem((8, ROWS), F32),
            vmem((ROWS, EMB), BF16),
            vmem((ROWS, EMB), BF16),
            vmem((ROWS, FEAT), BF16),
            vmem((4, 256, EMB), BF16),
            vmem((4, 256, EMB), BF16),
            vmem((4, 256, EMB), F32),
            vmem((4, 3, 64, EMB), BF16),
            vmem((4, 3, 64, EMB), BF16),
            vmem((4, 64, EMB), F32),
            vmem((4, 64, EMB), BF16),
            vmem((15, 16, EMB), BF16),
            dma,
            dma,
            dma((15,)),
            dma((15,)),
            dma((3, 4)),
            dma((3, 4)),
            dma((16,)),
            dma((16,)),
            dma((7,)),
            dma((8,)),
            dma((1,)),
            dma((1,)),
            dma((2,)),
            dma((2,)),
            dma((6,)),
            dma((8,)),
            dma((8, 2)),
            dma((7,)),
            dma((8,)),
            dma((2,)),
            dma((2,)),
            dma,
            dma,
            dma((4,)),
            dma((4,)),
            dma((4,)),
            dma((4,)),
            dma((12,)),
            dma((12,)),
            dma((15,)),
            dma((15,)),
        ],
        compiler_params=pltpu.CompilerParams(
            collective_id=0, has_side_effects=True, vmem_limit_bytes=56 << 20
        ),
        cost_estimate=pl.CostEstimate(
            flops=7_500_000_000, bytes_accessed=8 << 20, transcendentals=2 << 20
        ),
        name="infonce",
    )(features[0], weight, pair_ids, dup_ids)
    anywhere = pl.BlockSpec(memory_space=pl.ANY)
    loss, feature_grad, weight_grad = pl.pallas_call(
        deliver,
        out_shape=(
            jax.ShapeDtypeStruct((1, ROWS), F32),
            jax.ShapeDtypeStruct((ROWS, FEAT), BF16),
            jax.ShapeDtypeStruct((16, EMB), F32),
        ),
        in_specs=[anywhere] * 3,
        out_specs=(anywhere,) * 3,
        scratch_shapes=[
            vmem((1, ROWS), F32),
            vmem((ROWS, FEAT), BF16),
            vmem((16, EMB), F32),
            dma((6,)),
            dma((6,)),
        ],
        name="deliver",
    )(loss, feature_grad, weight_grad)
    return loss, feature_grad[None], weight_grad


def solution(mesh):
    return jax.shard_map(
        body,
        mesh=mesh,
        in_specs=(
            P("rep", "loop", None),
            P(("loop", "rep"), None),
            P("rep", "loop"),
            P("rep", "loop"),
        ),
        out_specs=(P("rep", "loop"), P("rep", "loop", None), P(("loop", "rep"), None)),
        check_vma=False,
    )
```

```python
import jax
import jax.numpy as jnp
from jax import lax
from jax.experimental import pallas as pl
from jax.experimental.pallas import tpu as pltpu
from jax.sharding import PartitionSpec as P

MESH = pl.DeviceIdType.MESH
scale_logits = 20.0
norm_eps = 1e-06
ROWS = 512
FEAT = 2048
EMB = 512
HALF = 256
SLOPE = 28.853900817779268
BF16 = jnp.bfloat16
F32 = jnp.float32

ORDER = (
    (0, 3, 0),
    (0, 1, 0),
    (1, 0, 0),
    (0, 1, 1),
    (0, 3, 1),
    (1, 0, 1),
    (1, 3, 0),
    (1, 1, 0),
    (1, 1, 1),
    (1, 3, 1),
    (0, 2, 0),
    (0, 2, 1),
    (1, 2, 0),
    (1, 2, 1),
)
STEPS = (0, 1, 3, 2)
FAR_FIRST = (2, 1, 3, 0)
PLANE = (10, 6, 14, 9, 11, 2, 8, 5, 7, 13, 15, 1, 3, 4, 12)


def device_at(x, y, z, core):
    return (lax.rem(x, 2) * 4 + z, lax.div(x, 2) * 8 + y * 2 + core)


def remote(src, dst, send_sem, recv_sem, device):
    return pltpu.make_async_remote_copy(
        src_ref=src,
        dst_ref=dst,
        send_sem=send_sem,
        recv_sem=recv_sem,
        device_id=device,
        device_id_type=MESH,
    )


def pick(step, column):
    value = jnp.int32(0)
    for index, entry in enumerate(ORDER):
        if entry[column]:
            value = jnp.where(step == index, entry[column], value)
    return value


def to_column(rows):
    return rows.T


def kernel(
    feat_hbm,
    weight_ref,
    pair_ref,
    dup_ref,
    loss_ref,
    fgrad_hbm,
    wgrad_ref,
    feat,
    work,
    featp,
    wpart,
    wfull,
    normed,
    inverse,
    home_emb,
    emb,
    labels,
    label_home,
    row_pairs,
    row_dups,
    weights,
    dots,
    quot,
    acc,
    pos,
    norms,
    grad,
    loss_out,
    loss_in,
    pre,
    home_pre,
    fgrad,
    sib_out,
    sib_in,
    own_term,
    first_out,
    first_in,
    first_sum,
    plane_out,
    plane_in,
    feat_sem,
    fgrad_sem,
    wp_send,
    wp_recv,
    wf_send,
    wf_recv,
    wc_send,
    wc_recv,
    lab_send,
    lab_recv,
    labx_send,
    labx_recv,
    swap_send,
    swap_recv,
    ring_send,
    sib_send,
    emb_recv,
    norm_send,
    norm_recv,
    back_send,
    back_recv,
    loss_send,
    loss_recv,
    feat_send,
    feat_recv,
    rc_send,
    rc_recv,
    rf_send,
    rf_recv,
    rp_send,
    rp_recv,
):
    loop, rep = lax.axis_index("loop"), lax.axis_index("rep")
    x_lo, z = lax.div(loop, 4), lax.rem(loop, 4)
    x_hi, y, core = lax.div(rep, 8), lax.rem(lax.div(rep, 2), 4), lax.rem(rep, 2)
    x = x_hi * 2 + x_lo
    other = 1 - core
    first = z * other + y * core
    second = y * other + z * core
    stays = core == x_lo
    slot = z * 2 + core

    def around(value, step):
        return lax.rem(value + step, 4)

    def plane_peer(index):
        step = index // 4
        return device_at(
            around(x, index % 4), around(y, step * other), around(z, step * core), core
        )

    def first_peer(step):
        return device_at(
            x, around(y, step * core), around(z, step * other), core
        )

    def z_peer(step, which):
        return device_at(x, y, around(z, step), which)

    sibling = device_at(x, y, z, other)
    partner = device_at(x_hi * 2 + 1 - x_lo, y, z, other)

    load = pltpu.make_async_copy(feat_hbm, feat, feat_sem)
    load.start()

    barrier = pltpu.get_barrier_semaphore()
    everyone = [plane_peer(index) for index in PLANE]
    for step in (2, 1, 3):
        everyone += [z_peer(step, other), first_peer(step)]
    everyone += [partner, sibling]
    for device in everyone:
        pl.semaphore_signal(barrier, inc=1, device_id=device, device_id_type=MESH)

    wpart[core, first, second, x] = weight_ref[...]
    label_home[...] = jnp.zeros((8, ROWS), jnp.int32)
    label_home[0:1, :] = pair_ref[...]
    label_home[1:2, :] = dup_ref[...]
    pl.semaphore_wait(barrier, len(everyone))

    started = []
    for index in PLANE:
        copy = remote(
            wpart.at[core, first, second, x],
            wpart.at[core, first, second, x],
            wp_send.at[index - 1],
            wp_recv.at[index - 1],
            plane_peer(index),
        )
        copy.start()
        started.append(copy)

    lab_swap = remote(label_home, labels.at[z * 2 + other], labx_send.at[0], labx_recv.at[0], partner)
    lab_swap_in = remote(label_home, labels.at[slot], labx_send.at[0], labx_recv.at[0], partner)

    @pl.when(jnp.logical_not(stays))
    def _():
        lab_swap.start()

    @pl.when(stays)
    def _():
        labels[slot] = label_home[...]

    load.wait()

    def transpose_half(source, part):
        rows = pl.ds(part * HALF, HALF)

        def transpose_slab(slab, carry):
            slab_xlo, slab_z, slab_xhi = lax.div(slab, 8), lax.rem(lax.div(slab, 2), 4), lax.rem(slab, 2)
            slab_x = slab_xhi * 2 + slab_xlo
            turned = source[rows, pl.ds(pl.multiple_of(slab * 128, 128), 128)].T
            for at_y in range(4):
                zero = pl.multiple_of((slab_z * 4 + slab_x) * 16, 16)
                featp[0, at_y, pl.ds(zero, 16), rows] = turned[at_y * 32 : at_y * 32 + 16]
                one = pl.multiple_of((at_y * 4 + slab_x) * 16, 16)
                featp[1, slab_z, pl.ds(one, 16), rows] = turned[at_y * 32 + 16 : at_y * 32 + 32]
            return carry

        lax.fori_loop(0, 16, transpose_slab, 0)

    def give(source_first, source_second, at):
        copy = remote(
            wpart.at[core, source_first, source_second],
            wpart.at[core, source_first, source_second],
            wc_send.at[at],
            wc_recv.at[at],
            sibling,
        )
        copy.start()
        started.append(copy)

    for piece in STEPS:
        source = around(second, 4 - piece)
        for index in range(piece * 4, piece * 4 + 4):
            if index:
                block = wpart.at[core, first, source, around(x, 4 - index % 4)]
                remote(
                    block, block, wp_send.at[index - 1], wp_recv.at[index - 1], plane_peer(index)
                ).wait_recv()
        for step in (2, 1, 3):
            copy = remote(
                wpart.at[core, first, source],
                wpart.at[core, first, source],
                wf_send.at[step - 1, piece],
                wf_recv.at[step - 1, piece],
                first_peer(step),
            )
            copy.start()
            started.append(copy)
        give(first, source, piece)

    def follow(chunk):
        rows = pl.ds(chunk * 128, 128)
        return remote(feat.at[rows], work.at[rows], feat_send.at[chunk], feat_recv.at[chunk], partner)

    @pl.when(jnp.logical_not(stays))
    def _():
        follow(0).start()
        follow(1).start()

    @pl.when(stays)
    def _():
        for part in range(2):
            transpose_half(feat, part)

    @pl.when(jnp.logical_not(stays))
    def _():
        lab_swap_in.wait_recv()

    lab_copies = []
    for index, (step, which) in enumerate(
        [(0, other)] + [(step, which) for step in (1, 2, 3) for which in (core, other)]
    ):
        copy = remote(
            labels.at[slot],
            labels.at[slot],
            lab_send.at[index],
            lab_recv.at[slot],
            z_peer(step, which),
        )
        copy.start()
        lab_copies.append(copy)
    turned_labels = to_column(labels[slot])
    row_pairs[...] = jnp.broadcast_to(turned_labels[:, 0:1], (ROWS, 128))
    row_dups[...] = jnp.broadcast_to(turned_labels[:, 1:2], (ROWS, 128))

    def place(which, at_first, at_second):
        at_z = at_first * (1 - which) + at_second * which
        at_y = at_second * (1 - which) + at_first * which
        for at_x in range(4):
            block = (at_x % 2) * 64 + at_z * 16 + (at_x // 2) * 8 + at_y * 2 + which
            wfull[pl.ds(pl.multiple_of(block * 16, 16), 16), :] = wpart[which, at_first, at_second, at_x]

    for steps in ((1, 3), (2,)):
        for piece in STEPS:
            at = around(second, 4 - piece)
            for step in steps:
                source = around(first, 4 - step)
                remote(
                    wpart.at[core, source, at],
                    wpart.at[core, source, at],
                    wf_send.at[step - 1, piece],
                    wf_recv.at[step - 1, piece],
                    first_peer(step),
                ).wait_recv()
                give(source, at, step * 4 + piece)
    for at_first in range(4):
        for at_second in range(4):
            place(core, at_first, at_second)
    for step in (0, 1, 3, 2):
        for piece in STEPS:
            source = (around(second, 4 - step), around(first, 4 - piece))
            block = wpart.at[other, source[0], source[1]]
            at = step * 4 + piece
            remote(block, block, wc_send.at[at], wc_recv.at[at], sibling).wait_recv()
            place(other, source[0], source[1])

    def chunk_of(at, chunk):
        return emb.at[at, pl.ds(pl.multiple_of(chunk * 128, 128), 128)]

    def ring(at, chunk, step, sem):
        block = chunk_of(at, chunk)
        return remote(block, block, ring_send.at[sem], emb_recv.at[at, chunk], z_peer(step, core))

    def beside(at, chunk, sem):
        block = chunk_of(at, chunk)
        return remote(block, block, sib_send.at[sem], emb_recv.at[at, chunk], sibling)

    def send_own(chunk):
        ring(slot, chunk, 1, chunk).start()
        ring(slot, chunk, 3, 4 + chunk).start()
        beside(slot, chunk, chunk).start()

    def swap(chunk, at):
        return remote(
            home_emb.at[pl.ds(chunk * 128, 128)],
            emb.at[at, pl.ds(chunk * 128, 128)],
            swap_send.at[chunk],
            swap_recv.at[chunk],
            partner,
        )

    def project(source, part):
        half_rows = pl.ds(part * HALF, HALF)
        normed[half_rows, :] = jnp.dot(source[half_rows, :], wfull[...], preferred_element_type=F32)
        for start in range(part * HALF, part * HALF + HALF, 64):
            rows = pl.ds(start, 64)
            projected = normed[rows, :]
            scale = lax.rsqrt(jnp.sum(projected * projected, axis=1, keepdims=True) + norm_eps)
            normed[rows, :] = projected * scale
            inverse[rows, :] = jnp.broadcast_to(scale, (64, 128))

    for part in range(2):
        half_rows = pl.ds(part * HALF, HALF)
        project(feat, part)
        home_emb[half_rows, :] = normed[half_rows, :].astype(BF16)

        @pl.when(jnp.logical_not(stays))
        def _():
            for chunk in (2 * part, 2 * part + 1):
                swap(chunk, z * 2 + other).start()

        @pl.when(stays)
        def _():
            emb[slot, half_rows, :] = home_emb[half_rows, :]
            for chunk in (2 * part, 2 * part + 1):
                send_own(chunk)

    def catch_up(part):
        follow(2 * part).wait_recv()
        follow(2 * part + 1).wait_recv()
        project(work, part)
        transpose_half(work, part)

    acc[...] = jnp.zeros((ROWS, 128), F32)
    pos[...] = jnp.zeros((ROWS, 128), F32)

    @pl.when(jnp.logical_not(stays))
    def _():
        for chunk in range(4):
            swap(chunk, slot).wait_recv()
            send_own(chunk)
        follow(2).start()
        follow(3).start()
        catch_up(0)

    for index in range(7):
        other_slot = lax.rem(slot + 1 + index, 8)
        remote(
            labels.at[other_slot],
            labels.at[other_slot],
            lab_send.at[index],
            lab_recv.at[other_slot],
            sibling,
        ).wait_recv()

    def take(at, which, own):
        piece = at * 2 + which
        columns = pl.ds(pl.multiple_of(which * HALF, HALF), HALF)
        dots[...] = lax.dot_general(
            emb[slot], emb[at, columns, :], (((1,), (1,)), ((), ())), preferred_element_type=F32
        )
        for part in range(2):
            lanes = pl.ds(pl.multiple_of(which * HALF + part * 128, 128), 128)
            col_pair = labels[at, 0:1, lanes]
            col_dup = labels[at, 1:2, lanes]
            for start in range(0, ROWS, 64):
                rows = pl.ds(start, 64)
                power = dots[rows, part * 128 : (part + 1) * 128] * SLOPE - SLOPE
                value = jnp.exp2(power)
                mate = row_pairs[rows, :] == col_pair
                if own:
                    row_index = start + lax.broadcasted_iota(jnp.int32, (64, 128), 0)
                    col_index = which * HALF + part * 128 + lax.broadcasted_iota(jnp.int32, (64, 128), 1)
                    mate = jnp.logical_and(mate, row_index != col_index)
                apart = jnp.where(row_dups[rows, :] != col_dup, value, 0.0)
                paired = jnp.where(mate, value, 0.0)
                quot[piece, rows, part * 128 : (part + 1) * 128] = apart - paired
                acc[rows, :] += apart
                pos[rows, :] += paired

    def own_piece(part, carry):
        take(slot, part, True)
        return carry

    lax.fori_loop(0, 2, own_piece, 0)

    def next_piece(step, carry):
        which_ring = jnp.where(pick(step, 0) == 0, core, other)
        at = around(z, pick(step, 1)) * 2 + which_ring
        which = pick(step, 2)
        for sub in range(2):
            chunk = which * 2 + sub
            ring(at, chunk, 1, 0).wait_recv()

            @pl.when(step == 0)
            def _():
                ring(at, chunk, 1, 8 + sub).start()
                beside(at, chunk, 4 + sub).start()

            @pl.when(step == 3)
            def _():
                ring(at, chunk, 3, 10 + sub).start()
                beside(at, chunk, 6 + sub).start()

            for index, count in ((1, 8), (4, 10), (10, 12), (11, 14)):

                @pl.when(step == index)
                def _():
                    beside(at, chunk, count + sub).start()

        take(at, which, False)
        return carry

    lax.fori_loop(0, len(ORDER), next_piece, 0)

    paired_row = jnp.sum(pos[...].T, axis=0, keepdims=True)
    total_row = jnp.sum(acc[...].T, axis=0, keepdims=True) + paired_row
    norms[slot] = jnp.broadcast_to(1.0 / total_row, (8, ROWS))
    norm_copies = []
    for index, (step, which) in enumerate(
        [(0, other)] + [(step, which) for step in (1, 2, 3) for which in (core, other)]
    ):
        copy = remote(
            norms.at[slot], norms.at[slot], norm_send.at[index], norm_recv.at[slot], z_peer(step, which)
        )
        copy.start()
        norm_copies.append(copy)
    loss_out[...] = jnp.broadcast_to(jnp.log(total_row) - jnp.log(paired_row), (8, ROWS))
    total = jnp.sum(acc[...] + pos[...], axis=1, keepdims=True)
    acc[...] = jnp.broadcast_to(1.0 / total, (ROWS, 128))

    def wait_norm(at):
        remote(norms.at[at], norms.at[at], norm_send.at[0], norm_recv.at[at], sibling).wait_recv()

    loss_back = remote(loss_out, loss_in, loss_send, loss_recv, partner)

    @pl.when(jnp.logical_not(stays))
    def _():
        loss_back.start()
        catch_up(1)

    def back(part):
        rows = pl.ds(part * HALF, HALF)
        return remote(pre.at[rows], home_pre.at[rows], back_send.at[part], back_recv.at[part], partner)

    for step in STEPS:
        pair = around(z, step)
        if step:
            wait_norm(pair * 2 + core)
        wait_norm(pair * 2 + other)
        buffer = step % 2
        for index in range(4):
            for lane in range(0, HALF, 128):
                column = (index % 2) * HALF + lane
                norm = norms[pair * 2 + index // 2, 0:1, column : column + 128]
                for start in range(0, ROWS, 64):
                    rows = pl.ds(start, 64)
                    value = quot[pair * 4 + index, rows, lane : lane + 128]
                    weight = jnp.abs(value) * (acc[rows, :] + norm) - jnp.where(value < 0.0, 2.0, 0.0)
                    weights[buffer, start : start + 64, index * HALF + lane : index * HALF + lane + 128] = (
                        weight.astype(BF16)
                    )
        term = jnp.dot(
            weights[buffer], emb[pl.ds(pair * 2, 2)].reshape(2 * ROWS, EMB), preferred_element_type=F32
        )
        if step:
            grad[...] += term
        else:
            grad[...] = term

    for start in range(0, ROWS, 64):
        rows = pl.ds(start, 64)
        unit = normed[rows, :]
        whole = scale_logits * grad[rows, :]
        along = jnp.sum(unit * whole, axis=1, keepdims=True)
        pre[rows, :] = (inverse[rows, 0:1] * (whole - unit * along)).astype(BF16)

    @pl.when(jnp.logical_not(stays))
    def _():
        for part in range(2):
            back(part).start()

    @pl.when(stays)
    def _():
        home_pre[...] = pre[...]

    reduce_copies = []
    for index, offset in enumerate(FAR_FIRST):
        group = around(first, offset)
        sib_out[group] = jnp.dot(featp[other, group], pre[...], preferred_element_type=F32).astype(BF16)
        copy = remote(sib_out.at[group], sib_in.at[group], rc_send.at[index], rc_recv.at[index], sibling)
        copy.start()
        reduce_copies.append(copy)
    for at in range(4):
        own_term[at] = jnp.dot(featp[core, at], pre[...], preferred_element_type=F32)
    def first_copy(index, count):
        return remote(
            first_out.at[index, count],
            first_in.at[index, count],
            rf_send.at[index * 3 + count],
            rf_recv.at[index * 3 + count],
            first_peer(FAR_FIRST[count]),
        )

    def send_group(index):
        group = around(second, FAR_FIRST[index])
        remote(
            sib_out.at[group], sib_in.at[group], rc_send.at[index], rc_recv.at[index], sibling
        ).wait_recv()
        for count, step in enumerate(FAR_FIRST):
            rows = pl.ds(pl.multiple_of(around(first, step) * 64, 64), 64)
            value = own_term[group, rows, :] + sib_in[group, rows, :].astype(F32)
            if step:
                first_out[index, count] = value.astype(BF16)
                first_copy(index, count).start()
            else:
                first_sum[index] = value

    send_group(0)
    send_group(1)
    for index, offset in enumerate(FAR_FIRST):
        for count in range(3):
            first_copy(index, count).wait_send()
        if index < 2:
            send_group(index + 2)
        whole = first_sum[index]
        for count in (1, 2, 0):
            first_copy(index, count).wait_recv()
            whole = whole + first_in[index, count].astype(F32)
        plane_out[index] = whole.astype(BF16)
        for step in FAR_FIRST:
            target = offset * 4 + step
            if target:
                copy = remote(
                    plane_out.at[index, pl.ds(pl.multiple_of(around(x, step) * 16, 16), 16)],
                    plane_in.at[target - 1],
                    rp_send.at[target - 1],
                    rp_recv.at[target - 1],
                    plane_peer(target),
                )
                copy.start()
                reduce_copies.append(copy)
        if offset == 0:
            first_sum[index] = whole
    @pl.when(jnp.logical_not(stays))
    def _():
        loss_back.wait_recv()
        for part in range(2):
            back(part).wait_recv()
        loss_ref[...] = loss_in[0:1, :]

    @pl.when(stays)
    def _():
        loss_ref[...] = loss_out[0:1, :]

    def feature_part(index, carry):
        columns = pl.ds(pl.multiple_of(index * 512, 512), 512)
        fgrad[:, columns] = lax.dot_general(
            home_pre[...], wfull[columns, :], (((1,), (1,)), ((), ())), preferred_element_type=F32
        ).astype(BF16)
        return carry

    lax.fori_loop(0, 4, feature_part, 0)
    store = pltpu.make_async_copy(fgrad, fgrad_hbm, fgrad_sem)
    store.start()

    value = first_sum[3, pl.ds(pl.multiple_of(x * 16, 16), 16), :]
    for offset in FAR_FIRST:
        for step in (1, 3, 2, 0):
            target = offset * 4 + step
            if target:
                remote(
                    plane_out.at[0, pl.ds(0, 16)],
                    plane_in.at[target - 1],
                    rp_send.at[target - 1],
                    rp_recv.at[target - 1],
                    plane_peer(target),
                ).wait_recv()
                value = value + plane_in[target - 1].astype(F32)
    wgrad_ref[...] = value * (1.0 / 256.0)

    for copy in started + lab_copies + norm_copies + reduce_copies:
        copy.wait_send()
    for index in range(12):
        ring(slot, 0, 1, index).wait_send()
    for index in range(16):
        beside(slot, 0, index).wait_send()

    @pl.when(jnp.logical_not(stays))
    def _():
        lab_swap.wait_send()
        for chunk in range(4):
            swap(chunk, z * 2 + other).wait_send()
        loss_back.wait_send()
        for part in range(2):
            back(part).wait_send()
        for chunk in range(4):
            follow(chunk).wait_send()

    store.wait()


def deliver(loss_in, fgrad_in, wgrad_in, loss_out, fgrad_out, wgrad_out, loss, fgrad, wgrad, load_sem, store_sem):
    parts = [
        (fgrad_in.at[pl.ds(at, 128)], fgrad.at[pl.ds(at, 128)], fgrad_out.at[pl.ds(at, 128)])
        for at in range(0, ROWS, 128)
    ]
    parts += [(loss_in, loss, loss_out), (wgrad_in, wgrad, wgrad_out)]
    loads = [
        pltpu.make_async_copy(source, held, load_sem.at[index]) for index, (source, held, _) in enumerate(parts)
    ]
    stores = [
        pltpu.make_async_copy(held, target, store_sem.at[index]) for index, (_, held, target) in enumerate(parts)
    ]
    for copy in loads:
        copy.start()
    for load, store in zip(loads, stores):
        load.wait()
        store.start()
    for store in stores:
        store.wait()


def body(features, weight, pair_ids, dup_ids):
    dma = pltpu.SemaphoreType.DMA
    vmem = pltpu.VMEM
    loss, feature_grad, weight_grad = pl.pallas_call(
        kernel,
        out_shape=(
            jax.ShapeDtypeStruct((1, ROWS), F32),
            jax.ShapeDtypeStruct((ROWS, FEAT), BF16),
            jax.ShapeDtypeStruct((16, EMB), F32),
        ),
        in_specs=[
            pl.BlockSpec(memory_space=pl.ANY),
            pl.BlockSpec(memory_space=vmem),
            pl.BlockSpec(memory_space=vmem),
            pl.BlockSpec(memory_space=vmem),
        ],
        out_specs=(
            pl.BlockSpec(memory_space=vmem),
            pl.BlockSpec(memory_space=pl.ANY),
            pl.BlockSpec(memory_space=vmem),
        ),
        scratch_shapes=[
            vmem((ROWS, FEAT), BF16),
            vmem((ROWS, FEAT), BF16),
            vmem((2, 4, 256, EMB), BF16),
            vmem((2, 4, 4, 4, 16, EMB), BF16),
            vmem((FEAT, EMB), BF16),
            vmem((ROWS, EMB), F32),
            vmem((ROWS, 128), F32),
            vmem((ROWS, EMB), BF16),
            vmem((8, ROWS, EMB), BF16),
            vmem((8, 8, ROWS), jnp.int32),
            vmem((8, ROWS), jnp.int32),
            vmem((ROWS, 128), jnp.int32),
            vmem((ROWS, 128), jnp.int32),
            vmem((2, ROWS, 2 * ROWS), BF16),
            vmem((ROWS, HALF), F32),
            vmem((16, ROWS, HALF), F32),
            vmem((ROWS, 128), F32),
            vmem((ROWS, 128), F32),
            vmem((8, 8, ROWS), F32),
            vmem((ROWS, EMB), F32),
            vmem((8, ROWS), F32),
            vmem((8, ROWS), F32),
            vmem((ROWS, EMB), BF16),
            vmem((ROWS, EMB), BF16),
            vmem((ROWS, FEAT), BF16),
            vmem((4, 256, EMB), BF16),
            vmem((4, 256, EMB), BF16),
            vmem((4, 256, EMB), F32),
            vmem((4, 3, 64, EMB), BF16),
            vmem((4, 3, 64, EMB), BF16),
            vmem((4, 64, EMB), F32),
            vmem((4, 64, EMB), BF16),
            vmem((15, 16, EMB), BF16),
            dma,
            dma,
            dma((15,)),
            dma((15,)),
            dma((3, 4)),
            dma((3, 4)),
            dma((16,)),
            dma((16,)),
            dma((7,)),
            dma((8,)),
            dma((1,)),
            dma((1,)),
            dma((4,)),
            dma((4,)),
            dma((12,)),
            dma((16,)),
            dma((8, 4)),
            dma((7,)),
            dma((8,)),
            dma((2,)),
            dma((2,)),
            dma,
            dma,
            dma((4,)),
            dma((4,)),
            dma((4,)),
            dma((4,)),
            dma((12,)),
            dma((12,)),
            dma((15,)),
            dma((15,)),
        ],
        compiler_params=pltpu.CompilerParams(
            collective_id=0, has_side_effects=True, vmem_limit_bytes=56 << 20
        ),
        cost_estimate=pl.CostEstimate(
            flops=7_500_000_000, bytes_accessed=8 << 20, transcendentals=2 << 20
        ),
        name="infonce",
    )(features[0], weight, pair_ids, dup_ids)
    anywhere = pl.BlockSpec(memory_space=pl.ANY)
    loss, feature_grad, weight_grad = pl.pallas_call(
        deliver,
        out_shape=(
            jax.ShapeDtypeStruct((1, ROWS), F32),
            jax.ShapeDtypeStruct((ROWS, FEAT), BF16),
            jax.ShapeDtypeStruct((16, EMB), F32),
        ),
        in_specs=[anywhere] * 3,
        out_specs=(anywhere,) * 3,
        scratch_shapes=[
            vmem((1, ROWS), F32),
            vmem((ROWS, FEAT), BF16),
            vmem((16, EMB), F32),
            dma((6,)),
            dma((6,)),
        ],
        name="deliver",
    )(loss, feature_grad, weight_grad)
    return loss, feature_grad[None], weight_grad


def solution(mesh):
    return jax.shard_map(
        body,
        mesh=mesh,
        in_specs=(
            P("rep", "loop", None),
            P(("loop", "rep"), None),
            P("rep", "loop"),
            P("rep", "loop"),
        ),
        out_specs=(P("rep", "loop"), P("rep", "loop", None), P(("loop", "rep"), None)),
        check_vma=False,
    )
```

```python
import jax
import jax.numpy as jnp
from jax import lax
from jax.experimental import pallas as pl
from jax.experimental.pallas import tpu as pltpu
from jax.sharding import PartitionSpec as P

MESH = pl.DeviceIdType.MESH
scale_logits = 20.0
norm_eps = 1e-06
ROWS = 512
FEAT = 2048
EMB = 512
HALF = 256
SLOPE = 28.853900817779268
BF16 = jnp.bfloat16
F32 = jnp.float32

ORDER = (
    (0, 3, 0),
    (0, 1, 0),
    (1, 0, 0),
    (0, 1, 1),
    (0, 3, 1),
    (1, 0, 1),
    (1, 3, 0),
    (1, 1, 0),
    (1, 1, 1),
    (1, 3, 1),
    (0, 2, 0),
    (0, 2, 1),
    (1, 2, 0),
    (1, 2, 1),
)
STEPS = (0, 1, 3, 2)
FAR_FIRST = (2, 1, 3, 0)
PLANE = (2, 1, 3, 10, 6, 14, 9, 11, 8, 5, 7, 13, 15, 4, 12)


def device_at(x, y, z, core):
    return (lax.rem(x, 2) * 4 + z, lax.div(x, 2) * 8 + y * 2 + core)


def remote(src, dst, send_sem, recv_sem, device):
    return pltpu.make_async_remote_copy(
        src_ref=src,
        dst_ref=dst,
        send_sem=send_sem,
        recv_sem=recv_sem,
        device_id=device,
        device_id_type=MESH,
    )


def pick(step, column):
    value = jnp.int32(0)
    for index, entry in enumerate(ORDER):
        if entry[column]:
            value = jnp.where(step == index, entry[column], value)
    return value


def to_column(rows):
    return rows.T


def kernel(
    feat_hbm,
    weight_hbm,
    pair_hbm,
    dup_hbm,
    loss_ref,
    fgrad_hbm,
    wgrad_ref,
    feat,
    work,
    featp,
    wpart,
    wfull,
    normed,
    inverse,
    home_emb,
    emb,
    labels,
    label_home,
    row_pairs,
    row_dups,
    weights,
    dots,
    quot,
    acc,
    pos,
    norms,
    grad,
    loss_out,
    loss_in,
    pre,
    home_pre,
    fgrad,
    sib_out,
    sib_in,
    own_term,
    first_out,
    first_in,
    first_sum,
    plane_out,
    plane_in,
    pair_row,
    dup_row,
    small_sem,
    feat_sem,
    fgrad_sem,
    wp_send,
    wp_recv,
    wf_send,
    wf_recv,
    wc_send,
    wc_recv,
    lab_send,
    lab_recv,
    labx_send,
    labx_recv,
    swap_send,
    swap_recv,
    ring_send,
    sib_send,
    emb_recv,
    norm_send,
    norm_recv,
    back_send,
    back_recv,
    loss_send,
    loss_recv,
    feat_send,
    feat_recv,
    rc_send,
    rc_recv,
    rf_send,
    rf_recv,
    rp_send,
    rp_recv,
):
    loop, rep = lax.axis_index("loop"), lax.axis_index("rep")
    x_lo, z = lax.div(loop, 4), lax.rem(loop, 4)
    x_hi, y, core = lax.div(rep, 8), lax.rem(lax.div(rep, 2), 4), lax.rem(rep, 2)
    x = x_hi * 2 + x_lo
    other = 1 - core
    first = z * other + y * core
    second = y * other + z * core
    stays = core == x_lo
    slot = z * 2 + core

    def around(value, step):
        return lax.rem(value + step, 4)

    def plane_peer(index):
        step = index // 4
        return device_at(
            around(x, index % 4), around(y, step * other), around(z, step * core), core
        )

    def first_peer(step):
        return device_at(
            x, around(y, step * core), around(z, step * other), core
        )

    def z_peer(step, which):
        return device_at(x, y, around(z, step), which)

    sibling = device_at(x, y, z, other)
    partner = device_at(x_hi * 2 + 1 - x_lo, y, z, other)

    load = pltpu.make_async_copy(feat_hbm, feat, feat_sem)
    small_loads = [
        pltpu.make_async_copy(weight_hbm, wpart.at[core, first, second, x], small_sem.at[0]),
        pltpu.make_async_copy(pair_hbm, pair_row, small_sem.at[1]),
        pltpu.make_async_copy(dup_hbm, dup_row, small_sem.at[2]),
    ]
    for copy in small_loads:
        copy.start()
    load.start()

    barrier = pltpu.get_barrier_semaphore()
    everyone = [plane_peer(index) for index in PLANE]
    for step in (2, 1, 3):
        everyone += [z_peer(step, other), first_peer(step)]
    everyone += [partner, sibling]
    for device in everyone:
        pl.semaphore_signal(barrier, inc=1, device_id=device, device_id_type=MESH)

    label_home[...] = jnp.zeros((8, ROWS), jnp.int32)
    for copy in small_loads:
        copy.wait()
    label_home[0:1, :] = pair_row[...]
    label_home[1:2, :] = dup_row[...]
    pl.semaphore_wait(barrier, len(everyone))

    started = []
    for index in PLANE:
        copy = remote(
            wpart.at[core, first, second, x],
            wpart.at[core, first, second, x],
            wp_send.at[index - 1],
            wp_recv.at[index - 1],
            plane_peer(index),
        )
        copy.start()
        started.append(copy)

    lab_swap = remote(label_home, labels.at[z * 2 + other], labx_send.at[0], labx_recv.at[0], partner)
    lab_swap_in = remote(label_home, labels.at[slot], labx_send.at[0], labx_recv.at[0], partner)

    @pl.when(jnp.logical_not(stays))
    def _():
        lab_swap.start()

    @pl.when(stays)
    def _():
        labels[slot] = label_home[...]

    load.wait()

    def transpose_half(source, part):
        rows = pl.ds(part * HALF, HALF)

        def transpose_slab(slab, carry):
            slab_xlo, slab_z, slab_xhi = lax.div(slab, 8), lax.rem(lax.div(slab, 2), 4), lax.rem(slab, 2)
            slab_x = slab_xhi * 2 + slab_xlo
            turned = source[rows, pl.ds(pl.multiple_of(slab * 128, 128), 128)].T
            for at_y in range(4):
                zero = pl.multiple_of((slab_z * 4 + slab_x) * 16, 16)
                featp[0, at_y, pl.ds(zero, 16), rows] = turned[at_y * 32 : at_y * 32 + 16]
                one = pl.multiple_of((at_y * 4 + slab_x) * 16, 16)
                featp[1, slab_z, pl.ds(one, 16), rows] = turned[at_y * 32 + 16 : at_y * 32 + 32]
            return carry

        lax.fori_loop(0, 16, transpose_slab, 0)

    def give(source_first, source_second, at):
        copy = remote(
            wpart.at[core, source_first, source_second],
            wpart.at[core, source_first, source_second],
            wc_send.at[at],
            wc_recv.at[at],
            sibling,
        )
        copy.start()
        started.append(copy)

    for piece in STEPS:
        source = around(second, 4 - piece)
        for index in range(piece * 4, piece * 4 + 4):
            if index:
                block = wpart.at[core, first, source, around(x, 4 - index % 4)]
                remote(
                    block, block, wp_send.at[index - 1], wp_recv.at[index - 1], plane_peer(index)
                ).wait_recv()
        for step in (1, 3, 2):
            copy = remote(
                wpart.at[core, first, source],
                wpart.at[core, first, source],
                wf_send.at[step - 1, piece],
                wf_recv.at[step - 1, piece],
                first_peer(step),
            )
            copy.start()
            started.append(copy)
        give(first, source, piece)

    def follow(chunk):
        rows = pl.ds(chunk * 128, 128)
        return remote(feat.at[rows], work.at[rows], feat_send.at[chunk], feat_recv.at[chunk], partner)

    @pl.when(jnp.logical_not(stays))
    def _():
        follow(0).start()
        follow(1).start()

    @pl.when(jnp.logical_not(stays))
    def _():
        lab_swap_in.wait_recv()

    lab_copies = []
    for index, (step, which) in enumerate(
        [(0, other)] + [(step, which) for step in (1, 2, 3) for which in (core, other)]
    ):
        copy = remote(
            labels.at[slot],
            labels.at[slot],
            lab_send.at[index],
            lab_recv.at[slot],
            z_peer(step, which),
        )
        copy.start()
        lab_copies.append(copy)
    turned_labels = to_column(labels[slot])
    row_pairs[...] = jnp.broadcast_to(turned_labels[:, 0:1], (ROWS, 128))
    row_dups[...] = jnp.broadcast_to(turned_labels[:, 1:2], (ROWS, 128))

    def place(which, at_first, at_second):
        at_z = at_first * (1 - which) + at_second * which
        at_y = at_second * (1 - which) + at_first * which
        for at_x in range(4):
            block = (at_x % 2) * 64 + at_z * 16 + (at_x // 2) * 8 + at_y * 2 + which
            wfull[pl.ds(pl.multiple_of(block * 16, 16), 16), :] = wpart[which, at_first, at_second, at_x]

    for steps in ((1, 3), (2,)):
        for piece in STEPS:
            at = around(second, 4 - piece)
            for step in steps:
                source = around(first, 4 - step)
                remote(
                    wpart.at[core, source, at],
                    wpart.at[core, source, at],
                    wf_send.at[step - 1, piece],
                    wf_recv.at[step - 1, piece],
                    first_peer(step),
                ).wait_recv()
                give(source, at, step * 4 + piece)
    for at_first in range(4):
        for at_second in range(4):
            place(core, at_first, at_second)
    for step in (0, 1, 3, 2):
        for piece in STEPS:
            source = (around(second, 4 - step), around(first, 4 - piece))
            block = wpart.at[other, source[0], source[1]]
            at = step * 4 + piece
            remote(block, block, wc_send.at[at], wc_recv.at[at], sibling).wait_recv()
            place(other, source[0], source[1])

    def chunk_of(at, chunk):
        return emb.at[at, pl.ds(pl.multiple_of(chunk * 128, 128), 128)]

    def ring(at, chunk, step, sem):
        block = chunk_of(at, chunk)
        return remote(block, block, ring_send.at[sem], emb_recv.at[at, chunk], z_peer(step, core))

    def beside(at, chunk, sem):
        block = chunk_of(at, chunk)
        return remote(block, block, sib_send.at[sem], emb_recv.at[at, chunk], sibling)

    def send_own(chunk):
        ring(slot, chunk, 1, chunk).start()
        ring(slot, chunk, 3, 4 + chunk).start()
        beside(slot, chunk, chunk).start()

    def swap(chunk, at):
        return remote(
            home_emb.at[pl.ds(chunk * 128, 128)],
            emb.at[at, pl.ds(chunk * 128, 128)],
            swap_send.at[chunk],
            swap_recv.at[chunk],
            partner,
        )

    def project(source, part):
        half_rows = pl.ds(part * HALF, HALF)
        normed[half_rows, :] = jnp.dot(source[half_rows, :], wfull[...], preferred_element_type=F32)
        for start in range(part * HALF, part * HALF + HALF, 64):
            rows = pl.ds(start, 64)
            projected = normed[rows, :]
            scale = lax.rsqrt(jnp.sum(projected * projected, axis=1, keepdims=True) + norm_eps)
            normed[rows, :] = projected * scale
            inverse[rows, :] = jnp.broadcast_to(scale, (64, 128))

    for part in range(2):
        half_rows = pl.ds(part * HALF, HALF)
        project(feat, part)
        home_emb[half_rows, :] = normed[half_rows, :].astype(BF16)

        @pl.when(jnp.logical_not(stays))
        def _():
            for chunk in (2 * part, 2 * part + 1):
                swap(chunk, z * 2 + other).start()

        @pl.when(stays)
        def _():
            emb[slot, half_rows, :] = home_emb[half_rows, :]
            for chunk in (2 * part, 2 * part + 1):
                send_own(chunk)

    def catch_up(part):
        follow(2 * part).wait_recv()
        follow(2 * part + 1).wait_recv()
        project(work, part)
        transpose_half(work, part)

    acc[...] = jnp.zeros((ROWS, 128), F32)
    pos[...] = jnp.zeros((ROWS, 128), F32)

    @pl.when(stays)
    def _():
        for part in range(2):
            transpose_half(feat, part)


    @pl.when(jnp.logical_not(stays))
    def _():
        for chunk in range(4):
            swap(chunk, slot).wait_recv()
            send_own(chunk)
        follow(2).start()
        follow(3).start()
        catch_up(0)

    for index in range(7):
        other_slot = lax.rem(slot + 1 + index, 8)
        remote(
            labels.at[other_slot],
            labels.at[other_slot],
            lab_send.at[index],
            lab_recv.at[other_slot],
            sibling,
        ).wait_recv()

    def take(at, which, own):
        piece = at * 2 + which
        columns = pl.ds(pl.multiple_of(which * HALF, HALF), HALF)
        dots[...] = lax.dot_general(
            emb[slot], emb[at, columns, :], (((1,), (1,)), ((), ())), preferred_element_type=F32
        )
        for part in range(2):
            lanes = pl.ds(pl.multiple_of(which * HALF + part * 128, 128), 128)
            col_pair = labels[at, 0:1, lanes]
            col_dup = labels[at, 1:2, lanes]
            for start in range(0, ROWS, 64):
                rows = pl.ds(start, 64)
                power = dots[rows, part * 128 : (part + 1) * 128] * SLOPE - SLOPE
                value = jnp.exp2(power)
                mate = row_pairs[rows, :] == col_pair
                if own:
                    row_index = start + lax.broadcasted_iota(jnp.int32, (64, 128), 0)
                    col_index = which * HALF + part * 128 + lax.broadcasted_iota(jnp.int32, (64, 128), 1)
                    mate = jnp.logical_and(mate, row_index != col_index)
                apart = jnp.where(row_dups[rows, :] != col_dup, value, 0.0)
                paired = jnp.where(mate, value, 0.0)
                quot[piece, rows, part * 128 : (part + 1) * 128] = apart - paired
                acc[rows, :] += apart
                pos[rows, :] += paired

    def own_piece(part, carry):
        take(slot, part, True)
        return carry

    lax.fori_loop(0, 2, own_piece, 0)

    def next_piece(step, carry):
        which_ring = jnp.where(pick(step, 0) == 0, core, other)
        at = around(z, pick(step, 1)) * 2 + which_ring
        which = pick(step, 2)
        for sub in range(2):
            chunk = which * 2 + sub
            ring(at, chunk, 1, 0).wait_recv()

            @pl.when(step == 0)
            def _():
                ring(at, chunk, 1, 8 + sub).start()
                beside(at, chunk, 4 + sub).start()

            @pl.when(step == 3)
            def _():
                ring(at, chunk, 3, 10 + sub).start()
                beside(at, chunk, 6 + sub).start()

            for index, count in ((1, 8), (4, 10), (10, 12), (11, 14)):

                @pl.when(step == index)
                def _():
                    beside(at, chunk, count + sub).start()

        take(at, which, False)
        return carry

    lax.fori_loop(0, len(ORDER), next_piece, 0)

    total_row = jnp.sum((acc[...] + pos[...]).T, axis=0, keepdims=True)
    norms[slot] = jnp.broadcast_to(1.0 / total_row, (8, ROWS))
    norm_copies = []
    for index, (step, which) in enumerate(
        [(0, other)] + [(step, which) for step in (1, 2, 3) for which in (core, other)]
    ):
        copy = remote(
            norms.at[slot], norms.at[slot], norm_send.at[index], norm_recv.at[slot], z_peer(step, which)
        )
        copy.start()
        norm_copies.append(copy)
    paired_row = jnp.sum(pos[...].T, axis=0, keepdims=True)
    loss_out[...] = jnp.broadcast_to(jnp.log(total_row) - jnp.log(paired_row), (8, ROWS))
    total = jnp.sum(acc[...] + pos[...], axis=1, keepdims=True)
    acc[...] = jnp.broadcast_to(1.0 / total, (ROWS, 128))

    def wait_norm(at):
        remote(norms.at[at], norms.at[at], norm_send.at[0], norm_recv.at[at], sibling).wait_recv()

    loss_back = remote(loss_out, loss_in, loss_send, loss_recv, partner)

    @pl.when(jnp.logical_not(stays))
    def _():
        loss_back.start()
        catch_up(1)

    def back(part):
        rows = pl.ds(part * HALF, HALF)
        return remote(pre.at[rows], home_pre.at[rows], back_send.at[part], back_recv.at[part], partner)

    for step in STEPS:
        pair = around(z, step)
        if step:
            wait_norm(pair * 2 + core)
        wait_norm(pair * 2 + other)
        buffer = step % 2
        for index in range(4):
            for lane in range(0, HALF, 128):
                column = (index % 2) * HALF + lane
                norm = norms[pair * 2 + index // 2, 0:1, column : column + 128]
                for start in range(0, ROWS, 64):
                    rows = pl.ds(start, 64)
                    value = quot[pair * 4 + index, rows, lane : lane + 128]
                    weight = jnp.abs(value) * (acc[rows, :] + norm) - jnp.where(value < 0.0, 2.0, 0.0)
                    weights[buffer, start : start + 64, index * HALF + lane : index * HALF + lane + 128] = (
                        weight.astype(BF16)
                    )
        term = jnp.dot(
            weights[buffer], emb[pl.ds(pair * 2, 2)].reshape(2 * ROWS, EMB), preferred_element_type=F32
        )
        if step:
            grad[...] += term
        else:
            grad[...] = term

    for start in range(0, ROWS, 64):
        rows = pl.ds(start, 64)
        unit = normed[rows, :]
        whole = scale_logits * grad[rows, :]
        along = jnp.sum(unit * whole, axis=1, keepdims=True)
        pre[rows, :] = (inverse[rows, 0:1] * (whole - unit * along)).astype(BF16)

    @pl.when(jnp.logical_not(stays))
    def _():
        for part in range(2):
            back(part).start()

    @pl.when(stays)
    def _():
        home_pre[...] = pre[...]

    reduce_copies = []
    for index, offset in enumerate(FAR_FIRST):
        group = around(first, offset)
        sib_out[group] = jnp.dot(featp[other, group], pre[...], preferred_element_type=F32).astype(BF16)
        copy = remote(sib_out.at[group], sib_in.at[group], rc_send.at[index], rc_recv.at[index], sibling)
        copy.start()
        reduce_copies.append(copy)
    for at in range(4):
        own_term[at] = jnp.dot(featp[core, at], pre[...], preferred_element_type=F32)
    def first_copy(index, count):
        return remote(
            first_out.at[index, count],
            first_in.at[index, count],
            rf_send.at[index * 3 + count],
            rf_recv.at[index * 3 + count],
            first_peer(FAR_FIRST[count]),
        )

    def send_group(index):
        group = around(second, FAR_FIRST[index])
        remote(
            sib_out.at[group], sib_in.at[group], rc_send.at[index], rc_recv.at[index], sibling
        ).wait_recv()
        for count, step in enumerate(FAR_FIRST):
            rows = pl.ds(pl.multiple_of(around(first, step) * 64, 64), 64)
            value = own_term[group, rows, :] + sib_in[group, rows, :].astype(F32)
            if step:
                first_out[index, count] = value.astype(BF16)
                first_copy(index, count).start()
            else:
                first_sum[index] = value

    send_group(0)
    send_group(1)
    for index, offset in enumerate(FAR_FIRST):
        for count in range(3):
            first_copy(index, count).wait_send()
        if index < 2:
            send_group(index + 2)
        whole = first_sum[index]
        for count in (1, 2, 0):
            first_copy(index, count).wait_recv()
            whole = whole + first_in[index, count].astype(F32)
        plane_out[index] = whole.astype(BF16)
        for step in FAR_FIRST:
            target = offset * 4 + step
            if target:
                copy = remote(
                    plane_out.at[index, pl.ds(pl.multiple_of(around(x, step) * 16, 16), 16)],
                    plane_in.at[target - 1],
                    rp_send.at[target - 1],
                    rp_recv.at[target - 1],
                    plane_peer(target),
                )
                copy.start()
                reduce_copies.append(copy)
        if offset == 0:
            first_sum[index] = whole
    @pl.when(jnp.logical_not(stays))
    def _():
        loss_back.wait_recv()
        for part in range(2):
            back(part).wait_recv()
        loss_ref[...] = loss_in[0:1, :]

    @pl.when(stays)
    def _():
        loss_ref[...] = loss_out[0:1, :]

    def feature_part(index, carry):
        columns = pl.ds(pl.multiple_of(index * 512, 512), 512)
        fgrad[:, columns] = lax.dot_general(
            home_pre[...], wfull[columns, :], (((1,), (1,)), ((), ())), preferred_element_type=F32
        ).astype(BF16)
        return carry

    lax.fori_loop(0, 4, feature_part, 0)
    store = pltpu.make_async_copy(fgrad, fgrad_hbm, fgrad_sem)
    store.start()

    value = first_sum[3, pl.ds(pl.multiple_of(x * 16, 16), 16), :]
    for offset in FAR_FIRST:
        for step in (1, 3, 2, 0):
            target = offset * 4 + step
            if target:
                remote(
                    plane_out.at[0, pl.ds(0, 16)],
                    plane_in.at[target - 1],
                    rp_send.at[target - 1],
                    rp_recv.at[target - 1],
                    plane_peer(target),
                ).wait_recv()
                value = value + plane_in[target - 1].astype(F32)
    wgrad_ref[...] = value * (1.0 / 256.0)

    for copy in started + lab_copies + norm_copies + reduce_copies:
        copy.wait_send()
    for index in range(12):
        ring(slot, 0, 1, index).wait_send()
    for index in range(16):
        beside(slot, 0, index).wait_send()

    @pl.when(jnp.logical_not(stays))
    def _():
        lab_swap.wait_send()
        for chunk in range(4):
            swap(chunk, z * 2 + other).wait_send()
        loss_back.wait_send()
        for part in range(2):
            back(part).wait_send()
        for chunk in range(4):
            follow(chunk).wait_send()

    store.wait()


def deliver(loss_in, fgrad_in, wgrad_in, loss_out, fgrad_out, wgrad_out, loss, fgrad, wgrad, load_sem, store_sem):
    parts = [
        (fgrad_in.at[pl.ds(at, 64)], fgrad.at[pl.ds(at, 64)], fgrad_out.at[pl.ds(at, 64)])
        for at in range(0, ROWS, 64)
    ]
    parts += [(loss_in, loss, loss_out), (wgrad_in, wgrad, wgrad_out)]
    loads = [
        pltpu.make_async_copy(source, held, load_sem.at[index]) for index, (source, held, _) in enumerate(parts)
    ]
    stores = [
        pltpu.make_async_copy(held, target, store_sem.at[index]) for index, (_, held, target) in enumerate(parts)
    ]
    for copy in loads:
        copy.start()
    for load, store in zip(loads, stores):
        load.wait()
        store.start()
    for store in stores:
        store.wait()


def body(features, weight, pair_ids, dup_ids):
    dma = pltpu.SemaphoreType.DMA
    vmem = pltpu.VMEM
    loss, feature_grad, weight_grad = pl.pallas_call(
        kernel,
        out_shape=(
            jax.ShapeDtypeStruct((1, ROWS), F32),
            jax.ShapeDtypeStruct((ROWS, FEAT), BF16),
            jax.ShapeDtypeStruct((16, EMB), F32),
        ),
        in_specs=[pl.BlockSpec(memory_space=pl.ANY)] * 4,
        out_specs=(
            pl.BlockSpec(memory_space=vmem),
            pl.BlockSpec(memory_space=pl.ANY),
            pl.BlockSpec(memory_space=vmem),
        ),
        scratch_shapes=[
            vmem((ROWS, FEAT), BF16),
            vmem((ROWS, FEAT), BF16),
            vmem((2, 4, 256, EMB), BF16),
            vmem((2, 4, 4, 4, 16, EMB), BF16),
            vmem((FEAT, EMB), BF16),
            vmem((ROWS, EMB), F32),
            vmem((ROWS, 128), F32),
            vmem((ROWS, EMB), BF16),
            vmem((8, ROWS, EMB), BF16),
            vmem((8, 8, ROWS), jnp.int32),
            vmem((8, ROWS), jnp.int32),
            vmem((ROWS, 128), jnp.int32),
            vmem((ROWS, 128), jnp.int32),
            vmem((2, ROWS, 2 * ROWS), BF16),
            vmem((ROWS, HALF), F32),
            vmem((16, ROWS, HALF), F32),
            vmem((ROWS, 128), F32),
            vmem((ROWS, 128), F32),
            vmem((8, 8, ROWS), F32),
            vmem((ROWS, EMB), F32),
            vmem((8, ROWS), F32),
            vmem((8, ROWS), F32),
            vmem((ROWS, EMB), BF16),
            vmem((ROWS, EMB), BF16),
            vmem((ROWS, FEAT), BF16),
            vmem((4, 256, EMB), BF16),
            vmem((4, 256, EMB), BF16),
            vmem((4, 256, EMB), F32),
            vmem((4, 3, 64, EMB), BF16),
            vmem((4, 3, 64, EMB), BF16),
            vmem((4, 64, EMB), F32),
            vmem((4, 64, EMB), BF16),
            vmem((15, 16, EMB), BF16),
            vmem((1, ROWS), jnp.int32),
            vmem((1, ROWS), jnp.int32),
            dma((3,)),
            dma,
            dma,
            dma((15,)),
            dma((15,)),
            dma((3, 4)),
            dma((3, 4)),
            dma((16,)),
            dma((16,)),
            dma((7,)),
            dma((8,)),
            dma((1,)),
            dma((1,)),
            dma((4,)),
            dma((4,)),
            dma((12,)),
            dma((16,)),
            dma((8, 4)),
            dma((7,)),
            dma((8,)),
            dma((2,)),
            dma((2,)),
            dma,
            dma,
            dma((4,)),
            dma((4,)),
            dma((4,)),
            dma((4,)),
            dma((12,)),
            dma((12,)),
            dma((15,)),
            dma((15,)),
        ],
        compiler_params=pltpu.CompilerParams(
            collective_id=0, has_side_effects=True, vmem_limit_bytes=56 << 20
        ),
        cost_estimate=pl.CostEstimate(
            flops=7_500_000_000, bytes_accessed=8 << 20, transcendentals=2 << 20
        ),
        name="infonce",
    )(features[0], weight, pair_ids, dup_ids)
    anywhere = pl.BlockSpec(memory_space=pl.ANY)
    loss, feature_grad, weight_grad = pl.pallas_call(
        deliver,
        out_shape=(
            jax.ShapeDtypeStruct((1, ROWS), F32),
            jax.ShapeDtypeStruct((ROWS, FEAT), BF16),
            jax.ShapeDtypeStruct((16, EMB), F32),
        ),
        in_specs=[anywhere] * 3,
        out_specs=(anywhere,) * 3,
        scratch_shapes=[
            vmem((1, ROWS), F32),
            vmem((ROWS, FEAT), BF16),
            vmem((16, EMB), F32),
            dma((10,)),
            dma((10,)),
        ],
        name="deliver",
    )(loss, feature_grad, weight_grad)
    return loss, feature_grad[None], weight_grad


def solution(mesh):
    return jax.shard_map(
        body,
        mesh=mesh,
        in_specs=(
            P("rep", "loop", None),
            P(("loop", "rep"), None),
            P("rep", "loop"),
            P("rep", "loop"),
        ),
        out_specs=(P("rep", "loop"), P("rep", "loop", None), P(("loop", "rep"), None)),
        check_vma=False,
    )
```

```python
import jax
import jax.numpy as jnp
from jax import lax
from jax.experimental import pallas as pl
from jax.experimental.pallas import tpu as pltpu
from jax.sharding import PartitionSpec as P

MESH = pl.DeviceIdType.MESH
scale_logits = 20.0
norm_eps = 1e-06
ROWS = 512
FEAT = 2048
EMB = 512
HALF = 256
SLOPE = 28.853900817779268
BF16 = jnp.bfloat16
F32 = jnp.float32

ORDER = (
    (0, 3, 0),
    (0, 1, 0),
    (1, 0, 0),
    (0, 1, 1),
    (0, 3, 1),
    (1, 0, 1),
    (1, 3, 0),
    (1, 1, 0),
    (1, 1, 1),
    (1, 3, 1),
    (0, 2, 0),
    (0, 2, 1),
    (1, 2, 0),
    (1, 2, 1),
)
STEPS = (0, 1, 3, 2)
FAR_FIRST = (2, 1, 3, 0)
PLANE = (2, 1, 3, 10, 6, 14, 9, 11, 8, 5, 7, 13, 15, 4, 12)


def device_at(x, y, z, core):
    return (lax.rem(x, 2) * 4 + z, lax.div(x, 2) * 8 + y * 2 + core)


def remote(src, dst, send_sem, recv_sem, device):
    return pltpu.make_async_remote_copy(
        src_ref=src,
        dst_ref=dst,
        send_sem=send_sem,
        recv_sem=recv_sem,
        device_id=device,
        device_id_type=MESH,
    )


def pick(step, column):
    value = jnp.int32(0)
    for index, entry in enumerate(ORDER):
        if entry[column]:
            value = jnp.where(step == index, entry[column], value)
    return value


def to_column(rows):
    return rows.T


def kernel(
    feat_hbm,
    weight_hbm,
    pair_hbm,
    dup_hbm,
    loss_ref,
    fgrad_hbm,
    wgrad_ref,
    feat,
    work,
    featp,
    wpart,
    wfull,
    normed,
    inverse,
    home_emb,
    emb,
    labels,
    label_home,
    row_pairs,
    row_dups,
    weights,
    dots,
    quot,
    acc,
    pos,
    norms,
    grad,
    loss_out,
    loss_in,
    pre,
    home_pre,
    fgrad,
    sib_out,
    sib_in,
    own_term,
    first_out,
    first_in,
    first_sum,
    plane_out,
    plane_in,
    pair_row,
    dup_row,
    small_sem,
    feat_sem,
    fgrad_sem,
    wp_send,
    wp_recv,
    wf_send,
    wf_recv,
    wc_send,
    wc_recv,
    lab_send,
    lab_recv,
    labx_send,
    labx_recv,
    swap_send,
    swap_recv,
    ring_send,
    sib_send,
    emb_recv,
    norm_send,
    norm_recv,
    back_send,
    back_recv,
    loss_send,
    loss_recv,
    feat_send,
    feat_recv,
    rc_send,
    rc_recv,
    rf_send,
    rf_recv,
    rp_send,
    rp_recv,
):
    loop, rep = lax.axis_index("loop"), lax.axis_index("rep")
    x_lo, z = lax.div(loop, 4), lax.rem(loop, 4)
    x_hi, y, core = lax.div(rep, 8), lax.rem(lax.div(rep, 2), 4), lax.rem(rep, 2)
    x = x_hi * 2 + x_lo
    other = 1 - core
    first = z * other + y * core
    second = y * other + z * core
    stays = core == x_lo
    slot = z * 2 + core

    def around(value, step):
        return lax.rem(value + step, 4)

    def plane_peer(index):
        step = index // 4
        return device_at(
            around(x, index % 4), around(y, step * other), around(z, step * core), core
        )

    def first_peer(step):
        return device_at(
            x, around(y, step * core), around(z, step * other), core
        )

    def z_peer(step, which):
        return device_at(x, y, around(z, step), which)

    sibling = device_at(x, y, z, other)
    partner = device_at(x_hi * 2 + 1 - x_lo, y, z, other)

    load = pltpu.make_async_copy(feat_hbm, feat, feat_sem)
    small_loads = [
        pltpu.make_async_copy(weight_hbm, wpart.at[core, first, second, x], small_sem.at[0]),
        pltpu.make_async_copy(pair_hbm, pair_row, small_sem.at[1]),
        pltpu.make_async_copy(dup_hbm, dup_row, small_sem.at[2]),
    ]
    for copy in small_loads:
        copy.start()
    load.start()

    barrier = pltpu.get_barrier_semaphore()
    everyone = [plane_peer(index) for index in PLANE]
    for step in (2, 1, 3):
        everyone += [z_peer(step, other), first_peer(step)]
    everyone += [partner, sibling]
    for device in everyone:
        pl.semaphore_signal(barrier, inc=1, device_id=device, device_id_type=MESH)

    label_home[...] = jnp.zeros((8, ROWS), jnp.int32)
    for copy in small_loads:
        copy.wait()
    label_home[0:1, :] = pair_row[...]
    label_home[1:2, :] = dup_row[...]
    pl.semaphore_wait(barrier, len(everyone))

    started = []
    for index in PLANE:
        copy = remote(
            wpart.at[core, first, second, x],
            wpart.at[core, first, second, x],
            wp_send.at[index - 1],
            wp_recv.at[index - 1],
            plane_peer(index),
        )
        copy.start()
        started.append(copy)

    lab_swap = remote(label_home, labels.at[z * 2 + other], labx_send.at[0], labx_recv.at[0], partner)
    lab_swap_in = remote(label_home, labels.at[slot], labx_send.at[0], labx_recv.at[0], partner)

    @pl.when(jnp.logical_not(stays))
    def _():
        lab_swap.start()

    @pl.when(stays)
    def _():
        labels[slot] = label_home[...]

    load.wait()

    def transpose_half(source, part):
        rows = pl.ds(part * HALF, HALF)

        def transpose_slab(slab, carry):
            slab_xlo, slab_z, slab_xhi = lax.div(slab, 8), lax.rem(lax.div(slab, 2), 4), lax.rem(slab, 2)
            slab_x = slab_xhi * 2 + slab_xlo
            turned = source[rows, pl.ds(pl.multiple_of(slab * 128, 128), 128)].T
            for at_y in range(4):
                zero = pl.multiple_of((slab_z * 4 + slab_x) * 16, 16)
                featp[0, at_y, pl.ds(zero, 16), rows] = turned[at_y * 32 : at_y * 32 + 16]
                one = pl.multiple_of((at_y * 4 + slab_x) * 16, 16)
                featp[1, slab_z, pl.ds(one, 16), rows] = turned[at_y * 32 + 16 : at_y * 32 + 32]
            return carry

        lax.fori_loop(0, 16, transpose_slab, 0)

    def give(source_first, source_second, at):
        copy = remote(
            wpart.at[core, source_first, source_second],
            wpart.at[core, source_first, source_second],
            wc_send.at[at],
            wc_recv.at[at],
            sibling,
        )
        copy.start()
        started.append(copy)

    for piece in STEPS:
        source = around(second, 4 - piece)
        for index in range(piece * 4, piece * 4 + 4):
            if index:
                block = wpart.at[core, first, source, around(x, 4 - index % 4)]
                remote(
                    block, block, wp_send.at[index - 1], wp_recv.at[index - 1], plane_peer(index)
                ).wait_recv()
        for step in (1, 3, 2):
            copy = remote(
                wpart.at[core, first, source],
                wpart.at[core, first, source],
                wf_send.at[step - 1, piece],
                wf_recv.at[step - 1, piece],
                first_peer(step),
            )
            copy.start()
            started.append(copy)
        give(first, source, piece)

    def follow(chunk):
        rows = pl.ds(chunk * 128, 128)
        return remote(feat.at[rows], work.at[rows], feat_send.at[chunk], feat_recv.at[chunk], partner)

    @pl.when(jnp.logical_not(stays))
    def _():
        follow(0).start()
        follow(1).start()

    @pl.when(jnp.logical_not(stays))
    def _():
        lab_swap_in.wait_recv()

    lab_copies = []
    for index, (step, which) in enumerate(
        [(0, other)] + [(step, which) for step in (1, 2, 3) for which in (core, other)]
    ):
        copy = remote(
            labels.at[slot],
            labels.at[slot],
            lab_send.at[index],
            lab_recv.at[slot],
            z_peer(step, which),
        )
        copy.start()
        lab_copies.append(copy)
    turned_labels = to_column(labels[slot])
    row_pairs[...] = jnp.broadcast_to(turned_labels[:, 0:1], (ROWS, 128))
    row_dups[...] = jnp.broadcast_to(turned_labels[:, 1:2], (ROWS, 128))

    def place(which, at_first, at_second):
        at_z = at_first * (1 - which) + at_second * which
        at_y = at_second * (1 - which) + at_first * which
        for at_x in range(4):
            block = (at_x % 2) * 64 + at_z * 16 + (at_x // 2) * 8 + at_y * 2 + which
            wfull[pl.ds(pl.multiple_of(block * 16, 16), 16), :] = wpart[which, at_first, at_second, at_x]

    for steps in ((1, 3), (2,)):
        for piece in STEPS:
            at = around(second, 4 - piece)
            for step in steps:
                source = around(first, 4 - step)
                remote(
                    wpart.at[core, source, at],
                    wpart.at[core, source, at],
                    wf_send.at[step - 1, piece],
                    wf_recv.at[step - 1, piece],
                    first_peer(step),
                ).wait_recv()
                give(source, at, step * 4 + piece)
    for at_first in range(4):
        for at_second in range(4):
            place(core, at_first, at_second)
    for step in (0, 1, 3, 2):
        for piece in STEPS:
            source = (around(second, 4 - step), around(first, 4 - piece))
            block = wpart.at[other, source[0], source[1]]
            at = step * 4 + piece
            remote(block, block, wc_send.at[at], wc_recv.at[at], sibling).wait_recv()
            place(other, source[0], source[1])

    def chunk_of(at, chunk):
        return emb.at[at, pl.ds(pl.multiple_of(chunk * 128, 128), 128)]

    def ring(at, chunk, step, sem):
        block = chunk_of(at, chunk)
        return remote(block, block, ring_send.at[sem], emb_recv.at[at, chunk], z_peer(step, core))

    def beside(at, chunk, sem):
        block = chunk_of(at, chunk)
        return remote(block, block, sib_send.at[sem], emb_recv.at[at, chunk], sibling)

    def send_own(chunk):
        ring(slot, chunk, 1, chunk).start()
        ring(slot, chunk, 3, 4 + chunk).start()
        beside(slot, chunk, chunk).start()

    def swap(chunk, at):
        return remote(
            home_emb.at[pl.ds(chunk * 128, 128)],
            emb.at[at, pl.ds(chunk * 128, 128)],
            swap_send.at[chunk],
            swap_recv.at[chunk],
            partner,
        )

    def project(source, start, count):
        span = pl.ds(start, count)
        normed[span, :] = jnp.dot(source[span, :], wfull[...], preferred_element_type=F32)
        for at in range(start, start + count, 64):
            rows = pl.ds(at, 64)
            projected = normed[rows, :]
            scale = lax.rsqrt(jnp.sum(projected * projected, axis=1, keepdims=True) + norm_eps)
            normed[rows, :] = projected * scale
            inverse[rows, :] = jnp.broadcast_to(scale, (64, 128))

    for start, count in ((0, 128), (128, 128), (256, 256)):
        span = pl.ds(start, count)
        chunks = range(start // 128, (start + count) // 128)
        project(feat, start, count)

        @pl.when(jnp.logical_not(stays))
        def _():
            home_emb[span, :] = normed[span, :].astype(BF16)
            for chunk in chunks:
                swap(chunk, z * 2 + other).start()

        @pl.when(stays)
        def _():
            emb[slot, span, :] = normed[span, :].astype(BF16)
            for chunk in chunks:
                send_own(chunk)

    def catch_up(part):
        follow(2 * part).wait_recv()
        follow(2 * part + 1).wait_recv()
        project(work, part * HALF, HALF)
        transpose_half(work, part)

    acc[...] = jnp.zeros((ROWS, 128), F32)
    pos[...] = jnp.zeros((ROWS, 128), F32)

    @pl.when(stays)
    def _():
        for part in range(2):
            transpose_half(feat, part)


    @pl.when(jnp.logical_not(stays))
    def _():
        for chunk in range(4):
            swap(chunk, slot).wait_recv()
            send_own(chunk)
        follow(2).start()
        follow(3).start()
        catch_up(0)

    for index in range(7):
        other_slot = lax.rem(slot + 1 + index, 8)
        remote(
            labels.at[other_slot],
            labels.at[other_slot],
            lab_send.at[index],
            lab_recv.at[other_slot],
            sibling,
        ).wait_recv()

    def take(at, which, own):
        piece = at * 2 + which
        columns = pl.ds(pl.multiple_of(which * HALF, HALF), HALF)
        dots[...] = lax.dot_general(
            emb[slot], emb[at, columns, :], (((1,), (1,)), ((), ())), preferred_element_type=F32
        )
        for part in range(2):
            lanes = pl.ds(pl.multiple_of(which * HALF + part * 128, 128), 128)
            col_pair = labels[at, 0:1, lanes]
            col_dup = labels[at, 1:2, lanes]
            for start in range(0, ROWS, 64):
                rows = pl.ds(start, 64)
                power = dots[rows, part * 128 : (part + 1) * 128] * SLOPE - SLOPE
                value = jnp.exp2(power)
                mate = row_pairs[rows, :] == col_pair
                if own:
                    row_index = start + lax.broadcasted_iota(jnp.int32, (64, 128), 0)
                    col_index = which * HALF + part * 128 + lax.broadcasted_iota(jnp.int32, (64, 128), 1)
                    mate = jnp.logical_and(mate, row_index != col_index)
                apart = jnp.where(row_dups[rows, :] != col_dup, value, 0.0)
                paired = jnp.where(mate, value, 0.0)
                quot[piece, rows, part * 128 : (part + 1) * 128] = apart - paired
                acc[rows, :] += apart
                pos[rows, :] += paired

    def own_piece(part, carry):
        take(slot, part, True)
        return carry

    lax.fori_loop(0, 2, own_piece, 0)

    def next_piece(step, carry):
        which_ring = jnp.where(pick(step, 0) == 0, core, other)
        at = around(z, pick(step, 1)) * 2 + which_ring
        which = pick(step, 2)
        for sub in range(2):
            chunk = which * 2 + sub
            ring(at, chunk, 1, 0).wait_recv()

            @pl.when(step == 0)
            def _():
                ring(at, chunk, 1, 8 + sub).start()
                beside(at, chunk, 4 + sub).start()

            @pl.when(step == 3)
            def _():
                ring(at, chunk, 3, 10 + sub).start()
                beside(at, chunk, 6 + sub).start()

            for index, count in ((1, 8), (4, 10), (10, 12), (11, 14)):

                @pl.when(step == index)
                def _():
                    beside(at, chunk, count + sub).start()

        take(at, which, False)
        return carry

    lax.fori_loop(0, len(ORDER), next_piece, 0)

    total_row = jnp.sum((acc[...] + pos[...]).T, axis=0, keepdims=True)
    norms[slot] = 1.0 / total_row
    norm_copies = []
    for index, (step, which) in enumerate(
        [(0, other)] + [(step, which) for step in (1, 2, 3) for which in (core, other)]
    ):
        copy = remote(
            norms.at[slot], norms.at[slot], norm_send.at[index], norm_recv.at[slot], z_peer(step, which)
        )
        copy.start()
        norm_copies.append(copy)
    paired_row = jnp.sum(pos[...].T, axis=0, keepdims=True)
    loss_out[...] = jnp.broadcast_to(jnp.log(total_row) - jnp.log(paired_row), (8, ROWS))
    total = jnp.sum(acc[...] + pos[...], axis=1, keepdims=True)
    acc[...] = jnp.broadcast_to(1.0 / total, (ROWS, 128))

    def wait_norm(at):
        remote(norms.at[at], norms.at[at], norm_send.at[0], norm_recv.at[at], sibling).wait_recv()

    loss_back = remote(loss_out, loss_in, loss_send, loss_recv, partner)

    @pl.when(jnp.logical_not(stays))
    def _():
        loss_back.start()
        catch_up(1)

    def back(part):
        rows = pl.ds(part * HALF, HALF)
        return remote(pre.at[rows], home_pre.at[rows], back_send.at[part], back_recv.at[part], partner)

    for step in STEPS:
        pair = around(z, step)
        if step:
            wait_norm(pair * 2 + core)
        wait_norm(pair * 2 + other)
        buffer = step % 2
        for index in range(4):
            for lane in range(0, HALF, 128):
                column = (index % 2) * HALF + lane
                norm = norms[pair * 2 + index // 2, 0:1, column : column + 128]
                for start in range(0, ROWS, 64):
                    rows = pl.ds(start, 64)
                    value = quot[pair * 4 + index, rows, lane : lane + 128]
                    weight = jnp.abs(value) * (acc[rows, :] + norm) - jnp.where(value < 0.0, 2.0, 0.0)
                    weights[buffer, start : start + 64, index * HALF + lane : index * HALF + lane + 128] = (
                        weight.astype(BF16)
                    )
        term = jnp.dot(
            weights[buffer], emb[pl.ds(pair * 2, 2)].reshape(2 * ROWS, EMB), preferred_element_type=F32
        )
        if step:
            grad[...] += term
        else:
            grad[...] = term

    for start in range(0, ROWS, 64):
        rows = pl.ds(start, 64)
        unit = normed[rows, :]
        whole = scale_logits * grad[rows, :]
        along = jnp.sum(unit * whole, axis=1, keepdims=True)
        pre[rows, :] = (inverse[rows, 0:1] * (whole - unit * along)).astype(BF16)

    @pl.when(jnp.logical_not(stays))
    def _():
        for part in range(2):
            back(part).start()

    @pl.when(stays)
    def _():
        home_pre[...] = pre[...]

    reduce_copies = []
    for index, offset in enumerate(FAR_FIRST):
        group = around(first, offset)
        sib_out[group] = jnp.dot(featp[other, group], pre[...], preferred_element_type=F32).astype(BF16)
        copy = remote(sib_out.at[group], sib_in.at[group], rc_send.at[index], rc_recv.at[index], sibling)
        copy.start()
        reduce_copies.append(copy)
    for at in range(4):
        own_term[at] = jnp.dot(featp[core, at], pre[...], preferred_element_type=F32)
    def first_copy(index, count):
        return remote(
            first_out.at[index, count],
            first_in.at[index, count],
            rf_send.at[index * 3 + count],
            rf_recv.at[index * 3 + count],
            first_peer(FAR_FIRST[count]),
        )

    def send_group(index):
        group = around(second, FAR_FIRST[index])
        remote(
            sib_out.at[group], sib_in.at[group], rc_send.at[index], rc_recv.at[index], sibling
        ).wait_recv()
        for count, step in enumerate(FAR_FIRST):
            rows = pl.ds(pl.multiple_of(around(first, step) * 64, 64), 64)
            value = own_term[group, rows, :] + sib_in[group, rows, :].astype(F32)
            if step:
                first_out[index, count] = value.astype(BF16)
                first_copy(index, count).start()
            else:
                first_sum[index] = value

    send_group(0)
    send_group(1)
    for index, offset in enumerate(FAR_FIRST):
        for count in range(3):
            first_copy(index, count).wait_send()
        if index < 2:
            send_group(index + 2)
        whole = first_sum[index]
        for count in (1, 2, 0):
            first_copy(index, count).wait_recv()
            whole = whole + first_in[index, count].astype(F32)
        plane_out[index] = whole.astype(BF16)
        for step in FAR_FIRST:
            target = offset * 4 + step
            if target:
                copy = remote(
                    plane_out.at[index, pl.ds(pl.multiple_of(around(x, step) * 16, 16), 16)],
                    plane_in.at[target - 1],
                    rp_send.at[target - 1],
                    rp_recv.at[target - 1],
                    plane_peer(target),
                )
                copy.start()
                reduce_copies.append(copy)
        if offset == 0:
            first_sum[index] = whole
    @pl.when(jnp.logical_not(stays))
    def _():
        loss_back.wait_recv()
        for part in range(2):
            back(part).wait_recv()
        loss_ref[...] = loss_in[0:1, :]

    @pl.when(stays)
    def _():
        loss_ref[...] = loss_out[0:1, :]

    def feature_part(index, carry):
        columns = pl.ds(pl.multiple_of(index * 512, 512), 512)
        fgrad[:, columns] = lax.dot_general(
            home_pre[...], wfull[columns, :], (((1,), (1,)), ((), ())), preferred_element_type=F32
        ).astype(BF16)
        return carry

    lax.fori_loop(0, 4, feature_part, 0)
    store = pltpu.make_async_copy(fgrad, fgrad_hbm, fgrad_sem)
    store.start()

    value = first_sum[3, pl.ds(pl.multiple_of(x * 16, 16), 16), :]
    for offset in FAR_FIRST:
        for step in (1, 3, 2, 0):
            target = offset * 4 + step
            if target:
                remote(
                    plane_out.at[0, pl.ds(0, 16)],
                    plane_in.at[target - 1],
                    rp_send.at[target - 1],
                    rp_recv.at[target - 1],
                    plane_peer(target),
                ).wait_recv()
                value = value + plane_in[target - 1].astype(F32)
    wgrad_ref[...] = value * (1.0 / 256.0)

    for copy in started + lab_copies + norm_copies + reduce_copies:
        copy.wait_send()
    for index in range(12):
        ring(slot, 0, 1, index).wait_send()
    for index in range(16):
        beside(slot, 0, index).wait_send()

    @pl.when(jnp.logical_not(stays))
    def _():
        lab_swap.wait_send()
        for chunk in range(4):
            swap(chunk, z * 2 + other).wait_send()
        loss_back.wait_send()
        for part in range(2):
            back(part).wait_send()
        for chunk in range(4):
            follow(chunk).wait_send()

    store.wait()


def deliver(loss_in, fgrad_in, wgrad_in, loss_out, fgrad_out, wgrad_out, loss, fgrad, wgrad, load_sem, store_sem):
    parts = [
        (fgrad_in.at[pl.ds(at, 64)], fgrad.at[pl.ds(at, 64)], fgrad_out.at[pl.ds(at, 64)])
        for at in range(0, ROWS, 64)
    ]
    parts += [(loss_in, loss, loss_out), (wgrad_in, wgrad, wgrad_out)]
    loads = [
        pltpu.make_async_copy(source, held, load_sem.at[index]) for index, (source, held, _) in enumerate(parts)
    ]
    stores = [
        pltpu.make_async_copy(held, target, store_sem.at[index]) for index, (_, held, target) in enumerate(parts)
    ]
    for copy in loads:
        copy.start()
    for load, store in zip(loads, stores):
        load.wait()
        store.start()
    for store in stores:
        store.wait()


def body(features, weight, pair_ids, dup_ids):
    dma = pltpu.SemaphoreType.DMA
    vmem = pltpu.VMEM
    loss, feature_grad, weight_grad = pl.pallas_call(
        kernel,
        out_shape=(
            jax.ShapeDtypeStruct((1, ROWS), F32),
            jax.ShapeDtypeStruct((ROWS, FEAT), BF16),
            jax.ShapeDtypeStruct((16, EMB), F32),
        ),
        in_specs=[pl.BlockSpec(memory_space=pl.ANY)] * 4,
        out_specs=(
            pl.BlockSpec(memory_space=vmem),
            pl.BlockSpec(memory_space=pl.ANY),
            pl.BlockSpec(memory_space=vmem),
        ),
        scratch_shapes=[
            vmem((ROWS, FEAT), BF16),
            vmem((ROWS, FEAT), BF16),
            vmem((2, 4, 256, EMB), BF16),
            vmem((2, 4, 4, 4, 16, EMB), BF16),
            vmem((FEAT, EMB), BF16),
            vmem((ROWS, EMB), F32),
            vmem((ROWS, 128), F32),
            vmem((ROWS, EMB), BF16),
            vmem((8, ROWS, EMB), BF16),
            vmem((8, 8, ROWS), jnp.int32),
            vmem((8, ROWS), jnp.int32),
            vmem((ROWS, 128), jnp.int32),
            vmem((ROWS, 128), jnp.int32),
            vmem((2, ROWS, 2 * ROWS), BF16),
            vmem((ROWS, HALF), F32),
            vmem((16, ROWS, HALF), F32),
            vmem((ROWS, 128), F32),
            vmem((ROWS, 128), F32),
            vmem((8, 1, ROWS), F32),
            vmem((ROWS, EMB), F32),
            vmem((8, ROWS), F32),
            vmem((8, ROWS), F32),
            vmem((ROWS, EMB), BF16),
            vmem((ROWS, EMB), BF16),
            vmem((ROWS, FEAT), BF16),
            vmem((4, 256, EMB), BF16),
            vmem((4, 256, EMB), BF16),
            vmem((4, 256, EMB), F32),
            vmem((4, 3, 64, EMB), BF16),
            vmem((4, 3, 64, EMB), BF16),
            vmem((4, 64, EMB), F32),
            vmem((4, 64, EMB), BF16),
            vmem((15, 16, EMB), BF16),
            vmem((1, ROWS), jnp.int32),
            vmem((1, ROWS), jnp.int32),
            dma((3,)),
            dma,
            dma,
            dma((15,)),
            dma((15,)),
            dma((3, 4)),
            dma((3, 4)),
            dma((16,)),
            dma((16,)),
            dma((7,)),
            dma((8,)),
            dma((1,)),
            dma((1,)),
            dma((4,)),
            dma((4,)),
            dma((12,)),
            dma((16,)),
            dma((8, 4)),
            dma((7,)),
            dma((8,)),
            dma((2,)),
            dma((2,)),
            dma,
            dma,
            dma((4,)),
            dma((4,)),
            dma((4,)),
            dma((4,)),
            dma((12,)),
            dma((12,)),
            dma((15,)),
            dma((15,)),
        ],
        compiler_params=pltpu.CompilerParams(
            collective_id=0, has_side_effects=True, vmem_limit_bytes=56 << 20
        ),
        cost_estimate=pl.CostEstimate(
            flops=7_500_000_000, bytes_accessed=8 << 20, transcendentals=2 << 20
        ),
        name="infonce",
    )(features[0], weight, pair_ids, dup_ids)
    anywhere = pl.BlockSpec(memory_space=pl.ANY)
    loss, feature_grad, weight_grad = pl.pallas_call(
        deliver,
        out_shape=(
            jax.ShapeDtypeStruct((1, ROWS), F32),
            jax.ShapeDtypeStruct((ROWS, FEAT), BF16),
            jax.ShapeDtypeStruct((16, EMB), F32),
        ),
        in_specs=[anywhere] * 3,
        out_specs=(anywhere,) * 3,
        scratch_shapes=[
            vmem((1, ROWS), F32),
            vmem((ROWS, FEAT), BF16),
            vmem((16, EMB), F32),
            dma((10,)),
            dma((10,)),
        ],
        name="deliver",
    )(loss, feature_grad, weight_grad)
    return loss, feature_grad[None], weight_grad


def solution(mesh):
    return jax.shard_map(
        body,
        mesh=mesh,
        in_specs=(
            P("rep", "loop", None),
            P(("loop", "rep"), None),
            P("rep", "loop"),
            P("rep", "loop"),
        ),
        out_specs=(P("rep", "loop"), P("rep", "loop", None), P(("loop", "rep"), None)),
        check_vma=False,
    )
```

```python
import jax
import jax.numpy as jnp
from jax import lax
from jax.experimental import pallas as pl
from jax.experimental.pallas import tpu as pltpu
from jax.sharding import PartitionSpec as P

MESH = pl.DeviceIdType.MESH
scale_logits = 20.0
norm_eps = 1e-06
ROWS = 512
FEAT = 2048
EMB = 512
HALF = 256
SLOPE = 28.853900817779268
BF16 = jnp.bfloat16
F32 = jnp.float32

ORDER = (
    (0, 3, 0),
    (0, 1, 0),
    (1, 0, 0),
    (0, 1, 1),
    (0, 3, 1),
    (1, 0, 1),
    (1, 3, 0),
    (1, 1, 0),
    (1, 1, 1),
    (1, 3, 1),
    (0, 2, 0),
    (0, 2, 1),
    (1, 2, 0),
    (1, 2, 1),
)
STEPS = (0, 1, 3, 2)
FAR_FIRST = (2, 1, 3, 0)
PLANE = (2, 1, 3, 10, 6, 14, 9, 11, 8, 5, 7, 13, 15, 4, 12)


def device_at(x, y, z, core):
    return (lax.rem(x, 2) * 4 + z, lax.div(x, 2) * 8 + y * 2 + core)


def remote(src, dst, send_sem, recv_sem, device):
    return pltpu.make_async_remote_copy(
        src_ref=src,
        dst_ref=dst,
        send_sem=send_sem,
        recv_sem=recv_sem,
        device_id=device,
        device_id_type=MESH,
    )


def pick(step, column):
    value = jnp.int32(0)
    for index, entry in enumerate(ORDER):
        if entry[column]:
            value = jnp.where(step == index, entry[column], value)
    return value


def to_column(rows):
    return rows.T


def kernel(
    feat_hbm,
    weight_hbm,
    pair_hbm,
    dup_hbm,
    loss_ref,
    fgrad_hbm,
    wgrad_ref,
    feat,
    work,
    featp,
    wpart,
    wfull,
    normed,
    inverse,
    home_emb,
    emb,
    labels,
    label_home,
    row_pairs,
    row_dups,
    weights,
    dots,
    quot,
    acc,
    pos,
    norms,
    grad,
    loss_out,
    loss_in,
    pre,
    home_pre,
    fgrad,
    sib_out,
    sib_in,
    own_term,
    first_out,
    first_in,
    first_sum,
    plane_out,
    plane_in,
    pair_row,
    dup_row,
    small_sem,
    feat_sem,
    fgrad_sem,
    wp_send,
    wp_recv,
    wf_send,
    wf_recv,
    wc_send,
    wc_recv,
    lab_send,
    lab_recv,
    labx_send,
    labx_recv,
    swap_send,
    swap_recv,
    ring_send,
    sib_send,
    emb_recv,
    norm_send,
    norm_recv,
    back_send,
    back_recv,
    loss_send,
    loss_recv,
    feat_send,
    feat_recv,
    rc_send,
    rc_recv,
    rf_send,
    rf_recv,
    rp_send,
    rp_recv,
):
    loop, rep = lax.axis_index("loop"), lax.axis_index("rep")
    x_lo, z = lax.div(loop, 4), lax.rem(loop, 4)
    x_hi, y, core = lax.div(rep, 8), lax.rem(lax.div(rep, 2), 4), lax.rem(rep, 2)
    x = x_hi * 2 + x_lo
    other = 1 - core
    first = z * other + y * core
    second = y * other + z * core
    stays = core == x_lo
    slot = z * 2 + core

    def around(value, step):
        return lax.rem(value + step, 4)

    def plane_peer(index):
        step = index // 4
        return device_at(
            around(x, index % 4), around(y, step * other), around(z, step * core), core
        )

    def first_peer(step):
        return device_at(
            x, around(y, step * core), around(z, step * other), core
        )

    def z_peer(step, which):
        return device_at(x, y, around(z, step), which)

    sibling = device_at(x, y, z, other)
    partner = device_at(x_hi * 2 + 1 - x_lo, y, z, other)

    load = pltpu.make_async_copy(feat_hbm, feat, feat_sem)
    small_loads = [
        pltpu.make_async_copy(weight_hbm, wpart.at[core, first, second, x], small_sem.at[0]),
        pltpu.make_async_copy(pair_hbm, pair_row, small_sem.at[1]),
        pltpu.make_async_copy(dup_hbm, dup_row, small_sem.at[2]),
    ]
    for copy in small_loads:
        copy.start()
    load.start()

    barrier = pltpu.get_barrier_semaphore()
    everyone = [plane_peer(index) for index in PLANE]
    for step in (2, 1, 3):
        everyone += [z_peer(step, other), first_peer(step)]
    everyone += [partner, sibling]
    for device in everyone:
        pl.semaphore_signal(barrier, inc=1, device_id=device, device_id_type=MESH)

    label_home[...] = jnp.zeros((8, ROWS), jnp.int32)
    for copy in small_loads:
        copy.wait()
    label_home[0:1, :] = pair_row[...]
    label_home[1:2, :] = dup_row[...]
    pl.semaphore_wait(barrier, len(everyone))

    started = []
    for index in PLANE:
        copy = remote(
            wpart.at[core, first, second, x],
            wpart.at[core, first, second, x],
            wp_send.at[index - 1],
            wp_recv.at[index - 1],
            plane_peer(index),
        )
        copy.start()
        started.append(copy)

    lab_swap = remote(label_home, labels.at[z * 2 + other], labx_send.at[0], labx_recv.at[0], partner)
    lab_swap_in = remote(label_home, labels.at[slot], labx_send.at[0], labx_recv.at[0], partner)

    @pl.when(jnp.logical_not(stays))
    def _():
        lab_swap.start()

    @pl.when(stays)
    def _():
        labels[slot] = label_home[...]

    load.wait()

    def follow(chunk):
        rows = pl.ds(chunk * 128, 128)
        return remote(feat.at[rows], work.at[rows], feat_send.at[chunk], feat_recv.at[chunk], partner)

    @pl.when(jnp.logical_not(stays))
    def _():
        follow(0).start()

    def transpose_half(source, part):
        rows = pl.ds(part * HALF, HALF)

        def transpose_slab(slab, carry):
            slab_xlo, slab_z, slab_xhi = lax.div(slab, 8), lax.rem(lax.div(slab, 2), 4), lax.rem(slab, 2)
            slab_x = slab_xhi * 2 + slab_xlo
            turned = source[rows, pl.ds(pl.multiple_of(slab * 128, 128), 128)].T
            for at_y in range(4):
                zero = pl.multiple_of((slab_z * 4 + slab_x) * 16, 16)
                featp[0, at_y, pl.ds(zero, 16), rows] = turned[at_y * 32 : at_y * 32 + 16]
                one = pl.multiple_of((at_y * 4 + slab_x) * 16, 16)
                featp[1, slab_z, pl.ds(one, 16), rows] = turned[at_y * 32 + 16 : at_y * 32 + 32]
            return carry

        lax.fori_loop(0, 16, transpose_slab, 0)

    def give(source_first, source_second, at):
        copy = remote(
            wpart.at[core, source_first, source_second],
            wpart.at[core, source_first, source_second],
            wc_send.at[at],
            wc_recv.at[at],
            sibling,
        )
        copy.start()
        started.append(copy)

    for piece in STEPS:
        source = around(second, 4 - piece)
        for index in range(piece * 4, piece * 4 + 4):
            if index:
                block = wpart.at[core, first, source, around(x, 4 - index % 4)]
                remote(
                    block, block, wp_send.at[index - 1], wp_recv.at[index - 1], plane_peer(index)
                ).wait_recv()
        for step in (1, 3, 2):
            copy = remote(
                wpart.at[core, first, source],
                wpart.at[core, first, source],
                wf_send.at[step - 1, piece],
                wf_recv.at[step - 1, piece],
                first_peer(step),
            )
            copy.start()
            started.append(copy)
        give(first, source, piece)

    @pl.when(jnp.logical_not(stays))
    def _():
        follow(1).start()

    @pl.when(jnp.logical_not(stays))
    def _():
        lab_swap_in.wait_recv()

    lab_copies = []
    for index, (step, which) in enumerate(
        [(0, other)] + [(step, which) for step in (1, 2, 3) for which in (core, other)]
    ):
        copy = remote(
            labels.at[slot],
            labels.at[slot],
            lab_send.at[index],
            lab_recv.at[slot],
            z_peer(step, which),
        )
        copy.start()
        lab_copies.append(copy)
    turned_labels = to_column(labels[slot])
    row_pairs[...] = jnp.broadcast_to(turned_labels[:, 0:1], (ROWS, 128))
    row_dups[...] = jnp.broadcast_to(turned_labels[:, 1:2], (ROWS, 128))

    def place(which, at_first, at_second):
        at_z = at_first * (1 - which) + at_second * which
        at_y = at_second * (1 - which) + at_first * which
        for at_x in range(4):
            block = (at_x % 2) * 64 + at_z * 16 + (at_x // 2) * 8 + at_y * 2 + which
            wfull[pl.ds(pl.multiple_of(block * 16, 16), 16), :] = wpart[which, at_first, at_second, at_x]

    for steps in ((1, 3), (2,)):
        for piece in STEPS:
            at = around(second, 4 - piece)
            for step in steps:
                source = around(first, 4 - step)
                remote(
                    wpart.at[core, source, at],
                    wpart.at[core, source, at],
                    wf_send.at[step - 1, piece],
                    wf_recv.at[step - 1, piece],
                    first_peer(step),
                ).wait_recv()
                give(source, at, step * 4 + piece)
    for at_first in range(4):
        for at_second in range(4):
            place(core, at_first, at_second)
    for step in (0, 1, 3, 2):
        for piece in STEPS:
            source = (around(second, 4 - step), around(first, 4 - piece))
            block = wpart.at[other, source[0], source[1]]
            at = step * 4 + piece
            remote(block, block, wc_send.at[at], wc_recv.at[at], sibling).wait_recv()
            place(other, source[0], source[1])

    def chunk_of(at, chunk):
        return emb.at[at, pl.ds(pl.multiple_of(chunk * 128, 128), 128)]

    def ring(at, chunk, step, sem):
        block = chunk_of(at, chunk)
        return remote(block, block, ring_send.at[sem], emb_recv.at[at, chunk], z_peer(step, core))

    def beside(at, chunk, sem):
        block = chunk_of(at, chunk)
        return remote(block, block, sib_send.at[sem], emb_recv.at[at, chunk], sibling)

    def send_own(chunk):
        ring(slot, chunk, 1, chunk).start()
        ring(slot, chunk, 3, 4 + chunk).start()
        beside(slot, chunk, chunk).start()

    def swap(chunk, at):
        return remote(
            home_emb.at[pl.ds(chunk * 128, 128)],
            emb.at[at, pl.ds(chunk * 128, 128)],
            swap_send.at[chunk],
            swap_recv.at[chunk],
            partner,
        )

    def project(source, start, count):
        span = pl.ds(start, count)
        normed[span, :] = jnp.dot(source[span, :], wfull[...], preferred_element_type=F32)
        for at in range(start, start + count, 64):
            rows = pl.ds(at, 64)
            projected = normed[rows, :]
            scale = lax.rsqrt(jnp.sum(projected * projected, axis=1, keepdims=True) + norm_eps)
            normed[rows, :] = projected * scale
            inverse[rows, :] = jnp.broadcast_to(scale, (64, 128))

    for start, count in ((0, 128), (128, 128), (256, 256)):
        span = pl.ds(start, count)
        chunks = range(start // 128, (start + count) // 128)
        project(feat, start, count)

        @pl.when(jnp.logical_not(stays))
        def _():
            home_emb[span, :] = normed[span, :].astype(BF16)
            for chunk in chunks:
                swap(chunk, z * 2 + other).start()

        @pl.when(stays)
        def _():
            emb[slot, span, :] = normed[span, :].astype(BF16)
            for chunk in chunks:
                send_own(chunk)

    def catch_up(part):
        follow(2 * part).wait_recv()
        follow(2 * part + 1).wait_recv()
        project(work, part * HALF, HALF)
        transpose_half(work, part)

    acc[...] = jnp.zeros((ROWS, 128), F32)
    pos[...] = jnp.zeros((ROWS, 128), F32)

    @pl.when(stays)
    def _():
        for part in range(2):
            transpose_half(feat, part)


    @pl.when(jnp.logical_not(stays))
    def _():
        for chunk in range(4):
            swap(chunk, slot).wait_recv()
            send_own(chunk)
        follow(2).start()
        follow(3).start()
        catch_up(0)

    for index in range(7):
        other_slot = lax.rem(slot + 1 + index, 8)
        remote(
            labels.at[other_slot],
            labels.at[other_slot],
            lab_send.at[index],
            lab_recv.at[other_slot],
            sibling,
        ).wait_recv()

    def take(at, which, own):
        piece = at * 2 + which
        columns = pl.ds(pl.multiple_of(which * HALF, HALF), HALF)
        dots[...] = lax.dot_general(
            emb[slot], emb[at, columns, :], (((1,), (1,)), ((), ())), preferred_element_type=F32
        )
        for part in range(2):
            lanes = pl.ds(pl.multiple_of(which * HALF + part * 128, 128), 128)
            col_pair = labels[at, 0:1, lanes]
            col_dup = labels[at, 1:2, lanes]
            for start in range(0, ROWS, 64):
                rows = pl.ds(start, 64)
                power = dots[rows, part * 128 : (part + 1) * 128] * SLOPE - SLOPE
                value = jnp.exp2(power)
                mate = row_pairs[rows, :] == col_pair
                if own:
                    row_index = start + lax.broadcasted_iota(jnp.int32, (64, 128), 0)
                    col_index = which * HALF + part * 128 + lax.broadcasted_iota(jnp.int32, (64, 128), 1)
                    mate = jnp.logical_and(mate, row_index != col_index)
                apart = jnp.where(row_dups[rows, :] != col_dup, value, 0.0)
                paired = jnp.where(mate, value, 0.0)
                quot[piece, rows, part * 128 : (part + 1) * 128] = apart - paired
                acc[rows, :] += apart
                pos[rows, :] += paired

    def own_piece(part, carry):
        take(slot, part, True)
        return carry

    lax.fori_loop(0, 2, own_piece, 0)

    def next_piece(step, carry):
        which_ring = jnp.where(pick(step, 0) == 0, core, other)
        at = around(z, pick(step, 1)) * 2 + which_ring
        which = pick(step, 2)
        for sub in range(2):
            chunk = which * 2 + sub
            ring(at, chunk, 1, 0).wait_recv()

            @pl.when(step == 0)
            def _():
                ring(at, chunk, 1, 8 + sub).start()
                beside(at, chunk, 4 + sub).start()

            @pl.when(step == 3)
            def _():
                ring(at, chunk, 3, 10 + sub).start()
                beside(at, chunk, 6 + sub).start()

            for index, count in ((1, 8), (4, 10), (10, 12), (11, 14)):

                @pl.when(step == index)
                def _():
                    beside(at, chunk, count + sub).start()

        take(at, which, False)
        return carry

    lax.fori_loop(0, len(ORDER), next_piece, 0)

    total_row = jnp.sum((acc[...] + pos[...]).T, axis=0, keepdims=True)
    norms[slot] = 1.0 / total_row
    norm_copies = []
    for index, (step, which) in enumerate(
        [(0, other)] + [(step, which) for step in (1, 2, 3) for which in (core, other)]
    ):
        copy = remote(
            norms.at[slot], norms.at[slot], norm_send.at[index], norm_recv.at[slot], z_peer(step, which)
        )
        copy.start()
        norm_copies.append(copy)
    paired_row = jnp.sum(pos[...].T, axis=0, keepdims=True)
    loss_out[...] = jnp.broadcast_to(jnp.log(total_row) - jnp.log(paired_row), (8, ROWS))
    total = jnp.sum(acc[...] + pos[...], axis=1, keepdims=True)
    acc[...] = jnp.broadcast_to(1.0 / total, (ROWS, 128))

    def wait_norm(at):
        remote(norms.at[at], norms.at[at], norm_send.at[0], norm_recv.at[at], sibling).wait_recv()

    loss_back = remote(loss_out, loss_in, loss_send, loss_recv, partner)

    @pl.when(jnp.logical_not(stays))
    def _():
        loss_back.start()
        catch_up(1)

    def back(part):
        rows = pl.ds(part * HALF, HALF)
        return remote(pre.at[rows], home_pre.at[rows], back_send.at[part], back_recv.at[part], partner)

    for step in STEPS:
        pair = around(z, step)
        if step:
            wait_norm(pair * 2 + core)
        wait_norm(pair * 2 + other)
        buffer = step % 2
        for index in range(4):
            for lane in range(0, HALF, 128):
                column = (index % 2) * HALF + lane
                norm = norms[pair * 2 + index // 2, 0:1, column : column + 128]
                for start in range(0, ROWS, 64):
                    rows = pl.ds(start, 64)
                    value = quot[pair * 4 + index, rows, lane : lane + 128]
                    weight = jnp.abs(value) * (acc[rows, :] + norm) - jnp.where(value < 0.0, 2.0, 0.0)
                    weights[buffer, start : start + 64, index * HALF + lane : index * HALF + lane + 128] = (
                        weight.astype(BF16)
                    )
        term = jnp.dot(
            weights[buffer], emb[pl.ds(pair * 2, 2)].reshape(2 * ROWS, EMB), preferred_element_type=F32
        )
        if step:
            grad[...] += term
        else:
            grad[...] = term

    for start in range(0, ROWS, 64):
        rows = pl.ds(start, 64)
        unit = normed[rows, :]
        whole = scale_logits * grad[rows, :]
        along = jnp.sum(unit * whole, axis=1, keepdims=True)
        pre[rows, :] = (inverse[rows, 0:1] * (whole - unit * along)).astype(BF16)

    @pl.when(jnp.logical_not(stays))
    def _():
        for part in range(2):
            back(part).start()

    @pl.when(stays)
    def _():
        home_pre[...] = pre[...]

    reduce_copies = []
    for index, offset in enumerate(FAR_FIRST):
        group = around(first, offset)
        sib_out[group] = jnp.dot(featp[other, group], pre[...], preferred_element_type=F32).astype(BF16)
        copy = remote(sib_out.at[group], sib_in.at[group], rc_send.at[index], rc_recv.at[index], sibling)
        copy.start()
        reduce_copies.append(copy)
    for at in range(4):
        own_term[at] = jnp.dot(featp[core, at], pre[...], preferred_element_type=F32)
    def first_copy(index, count):
        return remote(
            first_out.at[index, count],
            first_in.at[index, count],
            rf_send.at[index * 3 + count],
            rf_recv.at[index * 3 + count],
            first_peer(FAR_FIRST[count]),
        )

    def send_group(index):
        group = around(second, FAR_FIRST[index])
        remote(
            sib_out.at[group], sib_in.at[group], rc_send.at[index], rc_recv.at[index], sibling
        ).wait_recv()
        for count, step in enumerate(FAR_FIRST):
            rows = pl.ds(pl.multiple_of(around(first, step) * 64, 64), 64)
            value = own_term[group, rows, :] + sib_in[group, rows, :].astype(F32)
            if step:
                first_out[index, count] = value.astype(BF16)
                first_copy(index, count).start()
            else:
                first_sum[index] = value

    send_group(0)
    send_group(1)
    for index, offset in enumerate(FAR_FIRST):
        for count in range(3):
            first_copy(index, count).wait_send()
        if index < 2:
            send_group(index + 2)
        whole = first_sum[index]
        for count in (1, 2, 0):
            first_copy(index, count).wait_recv()
            whole = whole + first_in[index, count].astype(F32)
        plane_out[index] = whole.astype(BF16)
        for step in FAR_FIRST:
            target = offset * 4 + step
            if target:
                copy = remote(
                    plane_out.at[index, pl.ds(pl.multiple_of(around(x, step) * 16, 16), 16)],
                    plane_in.at[target - 1],
                    rp_send.at[target - 1],
                    rp_recv.at[target - 1],
                    plane_peer(target),
                )
                copy.start()
                reduce_copies.append(copy)
        if offset == 0:
            first_sum[index] = whole
    @pl.when(jnp.logical_not(stays))
    def _():
        loss_back.wait_recv()
        for part in range(2):
            back(part).wait_recv()
        loss_ref[...] = loss_in[0:1, :]

    @pl.when(stays)
    def _():
        loss_ref[...] = loss_out[0:1, :]

    def feature_part(index, carry):
        columns = pl.ds(pl.multiple_of(index * 512, 512), 512)
        fgrad[:, columns] = lax.dot_general(
            home_pre[...], wfull[columns, :], (((1,), (1,)), ((), ())), preferred_element_type=F32
        ).astype(BF16)
        return carry

    lax.fori_loop(0, 4, feature_part, 0)
    store = pltpu.make_async_copy(fgrad, fgrad_hbm, fgrad_sem)
    store.start()

    value = first_sum[3, pl.ds(pl.multiple_of(x * 16, 16), 16), :]
    for offset in FAR_FIRST:
        for step in (1, 3, 2, 0):
            target = offset * 4 + step
            if target:
                remote(
                    plane_out.at[0, pl.ds(0, 16)],
                    plane_in.at[target - 1],
                    rp_send.at[target - 1],
                    rp_recv.at[target - 1],
                    plane_peer(target),
                ).wait_recv()
                value = value + plane_in[target - 1].astype(F32)
    wgrad_ref[...] = value * (1.0 / 256.0)

    for copy in started + lab_copies + norm_copies + reduce_copies:
        copy.wait_send()
    for index in range(12):
        ring(slot, 0, 1, index).wait_send()
    for index in range(16):
        beside(slot, 0, index).wait_send()

    @pl.when(jnp.logical_not(stays))
    def _():
        lab_swap.wait_send()
        for chunk in range(4):
            swap(chunk, z * 2 + other).wait_send()
        loss_back.wait_send()
        for part in range(2):
            back(part).wait_send()
        for chunk in range(4):
            follow(chunk).wait_send()

    store.wait()


def deliver(loss_in, fgrad_in, wgrad_in, loss_out, fgrad_out, wgrad_out, loss, fgrad, wgrad, load_sem, store_sem):
    parts = [
        (fgrad_in.at[pl.ds(at, 64)], fgrad.at[pl.ds(at, 64)], fgrad_out.at[pl.ds(at, 64)])
        for at in range(0, ROWS, 64)
    ]
    parts += [(loss_in, loss, loss_out), (wgrad_in, wgrad, wgrad_out)]
    loads = [
        pltpu.make_async_copy(source, held, load_sem.at[index]) for index, (source, held, _) in enumerate(parts)
    ]
    stores = [
        pltpu.make_async_copy(held, target, store_sem.at[index]) for index, (_, held, target) in enumerate(parts)
    ]
    for copy in loads:
        copy.start()
    for load, store in zip(loads, stores):
        load.wait()
        store.start()
    for store in stores:
        store.wait()


def body(features, weight, pair_ids, dup_ids):
    dma = pltpu.SemaphoreType.DMA
    vmem = pltpu.VMEM
    loss, feature_grad, weight_grad = pl.pallas_call(
        kernel,
        out_shape=(
            jax.ShapeDtypeStruct((1, ROWS), F32),
            jax.ShapeDtypeStruct((ROWS, FEAT), BF16),
            jax.ShapeDtypeStruct((16, EMB), F32),
        ),
        in_specs=[pl.BlockSpec(memory_space=pl.ANY)] * 4,
        out_specs=(
            pl.BlockSpec(memory_space=vmem),
            pl.BlockSpec(memory_space=pl.ANY),
            pl.BlockSpec(memory_space=vmem),
        ),
        scratch_shapes=[
            vmem((ROWS, FEAT), BF16),
            vmem((ROWS, FEAT), BF16),
            vmem((2, 4, 256, EMB), BF16),
            vmem((2, 4, 4, 4, 16, EMB), BF16),
            vmem((FEAT, EMB), BF16),
            vmem((ROWS, EMB), F32),
            vmem((ROWS, 128), F32),
            vmem((ROWS, EMB), BF16),
            vmem((8, ROWS, EMB), BF16),
            vmem((8, 8, ROWS), jnp.int32),
            vmem((8, ROWS), jnp.int32),
            vmem((ROWS, 128), jnp.int32),
            vmem((ROWS, 128), jnp.int32),
            vmem((2, ROWS, 2 * ROWS), BF16),
            vmem((ROWS, HALF), F32),
            vmem((16, ROWS, HALF), F32),
            vmem((ROWS, 128), F32),
            vmem((ROWS, 128), F32),
            vmem((8, 1, ROWS), F32),
            vmem((ROWS, EMB), F32),
            vmem((8, ROWS), F32),
            vmem((8, ROWS), F32),
            vmem((ROWS, EMB), BF16),
            vmem((ROWS, EMB), BF16),
            vmem((ROWS, FEAT), BF16),
            vmem((4, 256, EMB), BF16),
            vmem((4, 256, EMB), BF16),
            vmem((4, 256, EMB), F32),
            vmem((4, 3, 64, EMB), BF16),
            vmem((4, 3, 64, EMB), BF16),
            vmem((4, 64, EMB), F32),
            vmem((4, 64, EMB), BF16),
            vmem((15, 16, EMB), BF16),
            vmem((1, ROWS), jnp.int32),
            vmem((1, ROWS), jnp.int32),
            dma((3,)),
            dma,
            dma,
            dma((15,)),
            dma((15,)),
            dma((3, 4)),
            dma((3, 4)),
            dma((16,)),
            dma((16,)),
            dma((7,)),
            dma((8,)),
            dma((1,)),
            dma((1,)),
            dma((4,)),
            dma((4,)),
            dma((12,)),
            dma((16,)),
            dma((8, 4)),
            dma((7,)),
            dma((8,)),
            dma((2,)),
            dma((2,)),
            dma,
            dma,
            dma((4,)),
            dma((4,)),
            dma((4,)),
            dma((4,)),
            dma((12,)),
            dma((12,)),
            dma((15,)),
            dma((15,)),
        ],
        compiler_params=pltpu.CompilerParams(
            collective_id=0, has_side_effects=True, vmem_limit_bytes=56 << 20
        ),
        cost_estimate=pl.CostEstimate(
            flops=7_500_000_000, bytes_accessed=8 << 20, transcendentals=2 << 20
        ),
        name="infonce",
    )(features[0], weight, pair_ids, dup_ids)
    anywhere = pl.BlockSpec(memory_space=pl.ANY)
    loss, feature_grad, weight_grad = pl.pallas_call(
        deliver,
        out_shape=(
            jax.ShapeDtypeStruct((1, ROWS), F32),
            jax.ShapeDtypeStruct((ROWS, FEAT), BF16),
            jax.ShapeDtypeStruct((16, EMB), F32),
        ),
        in_specs=[anywhere] * 3,
        out_specs=(anywhere,) * 3,
        scratch_shapes=[
            vmem((1, ROWS), F32),
            vmem((ROWS, FEAT), BF16),
            vmem((16, EMB), F32),
            dma((10,)),
            dma((10,)),
        ],
        name="deliver",
    )(loss, feature_grad, weight_grad)
    return loss, feature_grad[None], weight_grad


def solution(mesh):
    return jax.shard_map(
        body,
        mesh=mesh,
        in_specs=(
            P("rep", "loop", None),
            P(("loop", "rep"), None),
            P("rep", "loop"),
            P("rep", "loop"),
        ),
        out_specs=(P("rep", "loop"), P("rep", "loop", None), P(("loop", "rep"), None)),
        check_vma=False,
    )
```

```python
import jax
import jax.numpy as jnp
from jax import lax
from jax.experimental import pallas as pl
from jax.experimental.pallas import tpu as pltpu
from jax.sharding import PartitionSpec as P

MESH = pl.DeviceIdType.MESH
scale_logits = 20.0
norm_eps = 1e-06
ROWS = 512
FEAT = 2048
EMB = 512
HALF = 256
SLOPE = 28.853900817779268
BF16 = jnp.bfloat16
F32 = jnp.float32

ORDER = (
    (0, 3, 0),
    (0, 1, 0),
    (1, 0, 0),
    (0, 1, 1),
    (0, 3, 1),
    (1, 0, 1),
    (1, 3, 0),
    (1, 1, 0),
    (1, 1, 1),
    (1, 3, 1),
    (0, 2, 0),
    (0, 2, 1),
    (1, 2, 0),
    (1, 2, 1),
)
STEPS = (0, 1, 3, 2)
FAR_FIRST = (2, 1, 3, 0)
PLANE = (2, 1, 3, 10, 6, 14, 9, 11, 8, 5, 7, 13, 15, 4, 12)


def device_at(x, y, z, core):
    return (lax.rem(x, 2) * 4 + z, lax.div(x, 2) * 8 + y * 2 + core)


def remote(src, dst, send_sem, recv_sem, device):
    return pltpu.make_async_remote_copy(
        src_ref=src,
        dst_ref=dst,
        send_sem=send_sem,
        recv_sem=recv_sem,
        device_id=device,
        device_id_type=MESH,
    )


def pick(step, column):
    value = jnp.int32(0)
    for index, entry in enumerate(ORDER):
        if entry[column]:
            value = jnp.where(step == index, entry[column], value)
    return value


def to_column(rows):
    return rows.T


def kernel(
    feat_hbm,
    weight_hbm,
    pair_hbm,
    dup_hbm,
    loss_ref,
    fgrad_hbm,
    wgrad_ref,
    feat,
    work,
    featp,
    wpart,
    wfull,
    normed,
    inverse,
    home_emb,
    emb,
    labels,
    label_home,
    row_pairs,
    row_dups,
    weights,
    dots,
    quot,
    acc,
    pos,
    norms,
    grad,
    loss_out,
    loss_in,
    pre,
    home_pre,
    fgrad,
    sib_out,
    sib_in,
    own_term,
    first_out,
    first_in,
    first_sum,
    plane_out,
    plane_in,
    pair_row,
    dup_row,
    small_sem,
    feat_sem,
    fgrad_sem,
    wp_send,
    wp_recv,
    wf_send,
    wf_recv,
    wc_send,
    wc_recv,
    lab_send,
    lab_recv,
    labx_send,
    labx_recv,
    swap_send,
    swap_recv,
    ring_send,
    sib_send,
    emb_recv,
    norm_send,
    norm_recv,
    back_send,
    back_recv,
    loss_send,
    loss_recv,
    feat_send,
    feat_recv,
    rc_send,
    rc_recv,
    rf_send,
    rf_recv,
    rp_send,
    rp_recv,
):
    loop, rep = lax.axis_index("loop"), lax.axis_index("rep")
    x_lo, z = lax.div(loop, 4), lax.rem(loop, 4)
    x_hi, y, core = lax.div(rep, 8), lax.rem(lax.div(rep, 2), 4), lax.rem(rep, 2)
    x = x_hi * 2 + x_lo
    other = 1 - core
    first = z * other + y * core
    second = y * other + z * core
    stays = core == x_lo
    slot = z * 2 + core

    def around(value, step):
        return lax.rem(value + step, 4)

    def plane_peer(index):
        step = index // 4
        return device_at(
            around(x, index % 4), around(y, step * other), around(z, step * core), core
        )

    def first_peer(step):
        return device_at(
            x, around(y, step * core), around(z, step * other), core
        )

    def z_peer(step, which):
        return device_at(x, y, around(z, step), which)

    sibling = device_at(x, y, z, other)
    partner = device_at(x_hi * 2 + 1 - x_lo, y, z, other)

    load = pltpu.make_async_copy(feat_hbm, feat, feat_sem)
    small_loads = [
        pltpu.make_async_copy(weight_hbm, wpart.at[core, first, second, x], small_sem.at[0]),
        pltpu.make_async_copy(pair_hbm, pair_row, small_sem.at[1]),
        pltpu.make_async_copy(dup_hbm, dup_row, small_sem.at[2]),
    ]
    for copy in small_loads:
        copy.start()
    load.start()

    barrier = pltpu.get_barrier_semaphore()
    everyone = [plane_peer(index) for index in PLANE]
    for step in (2, 1, 3):
        everyone += [z_peer(step, other), first_peer(step)]
    everyone += [partner, sibling]
    for device in everyone:
        pl.semaphore_signal(barrier, inc=1, device_id=device, device_id_type=MESH)

    label_home[...] = jnp.zeros((8, ROWS), jnp.int32)
    for copy in small_loads:
        copy.wait()
    label_home[0:1, :] = pair_row[...]
    label_home[1:2, :] = dup_row[...]
    pl.semaphore_wait(barrier, len(everyone))

    started = []
    for index in PLANE:
        copy = remote(
            wpart.at[core, first, second, x],
            wpart.at[core, first, second, x],
            wp_send.at[index - 1],
            wp_recv.at[index - 1],
            plane_peer(index),
        )
        copy.start()
        started.append(copy)

    lab_swap = remote(label_home, labels.at[z * 2 + other], labx_send.at[0], labx_recv.at[0], partner)
    lab_swap_in = remote(label_home, labels.at[slot], labx_send.at[0], labx_recv.at[0], partner)

    @pl.when(jnp.logical_not(stays))
    def _():
        lab_swap.start()

    @pl.when(stays)
    def _():
        labels[slot] = label_home[...]

    load.wait()

    def follow(chunk):
        rows = pl.ds(chunk * 128, 128)
        return remote(feat.at[rows], work.at[rows], feat_send.at[chunk], feat_recv.at[chunk], partner)

    @pl.when(jnp.logical_not(stays))
    def _():
        follow(0).start()

    def transpose_half(source, part):
        rows = pl.ds(part * HALF, HALF)

        def transpose_slab(slab, carry):
            slab_xlo, slab_z, slab_xhi = lax.div(slab, 8), lax.rem(lax.div(slab, 2), 4), lax.rem(slab, 2)
            slab_x = slab_xhi * 2 + slab_xlo
            turned = source[rows, pl.ds(pl.multiple_of(slab * 128, 128), 128)].T
            for at_y in range(4):
                zero = pl.multiple_of((slab_z * 4 + slab_x) * 16, 16)
                featp[0, at_y, pl.ds(zero, 16), rows] = turned[at_y * 32 : at_y * 32 + 16]
                one = pl.multiple_of((at_y * 4 + slab_x) * 16, 16)
                featp[1, slab_z, pl.ds(one, 16), rows] = turned[at_y * 32 + 16 : at_y * 32 + 32]
            return carry

        lax.fori_loop(0, 16, transpose_slab, 0)

    def give(source_first, source_second, at):
        copy = remote(
            wpart.at[core, source_first, source_second],
            wpart.at[core, source_first, source_second],
            wc_send.at[at],
            wc_recv.at[at],
            sibling,
        )
        copy.start()
        started.append(copy)

    for piece in STEPS:
        source = around(second, 4 - piece)
        for index in range(piece * 4, piece * 4 + 4):
            if index:
                block = wpart.at[core, first, source, around(x, 4 - index % 4)]
                remote(
                    block, block, wp_send.at[index - 1], wp_recv.at[index - 1], plane_peer(index)
                ).wait_recv()
        for step in (1, 3, 2):
            copy = remote(
                wpart.at[core, first, source],
                wpart.at[core, first, source],
                wf_send.at[step - 1, piece],
                wf_recv.at[step - 1, piece],
                first_peer(step),
            )
            copy.start()
            started.append(copy)
        give(first, source, piece)

    @pl.when(jnp.logical_not(stays))
    def _():
        follow(1).start()

    @pl.when(jnp.logical_not(stays))
    def _():
        lab_swap_in.wait_recv()

    lab_copies = []
    for index, (step, which) in enumerate(
        [(0, other)] + [(step, which) for step in (1, 2, 3) for which in (core, other)]
    ):
        copy = remote(
            labels.at[slot],
            labels.at[slot],
            lab_send.at[index],
            lab_recv.at[slot],
            z_peer(step, which),
        )
        copy.start()
        lab_copies.append(copy)
    turned_labels = to_column(labels[slot])
    row_pairs[...] = jnp.broadcast_to(turned_labels[:, 0:1], (ROWS, 128))
    row_dups[...] = jnp.broadcast_to(turned_labels[:, 1:2], (ROWS, 128))

    def place(which, at_first, at_second):
        at_z = at_first * (1 - which) + at_second * which
        at_y = at_second * (1 - which) + at_first * which
        for at_x in range(4):
            block = (at_x % 2) * 64 + at_z * 16 + (at_x // 2) * 8 + at_y * 2 + which
            wfull[pl.ds(pl.multiple_of(block * 16, 16), 16), :] = wpart[which, at_first, at_second, at_x]

    for steps in ((1, 3), (2,)):
        for piece in STEPS:
            at = around(second, 4 - piece)
            for step in steps:
                source = around(first, 4 - step)
                remote(
                    wpart.at[core, source, at],
                    wpart.at[core, source, at],
                    wf_send.at[step - 1, piece],
                    wf_recv.at[step - 1, piece],
                    first_peer(step),
                ).wait_recv()
                give(source, at, step * 4 + piece)
    for at_first in range(4):
        for at_second in range(4):
            place(core, at_first, at_second)
    for step in (0, 1, 3, 2):
        for piece in STEPS:
            source = (around(second, 4 - step), around(first, 4 - piece))
            block = wpart.at[other, source[0], source[1]]
            at = step * 4 + piece
            remote(block, block, wc_send.at[at], wc_recv.at[at], sibling).wait_recv()
            place(other, source[0], source[1])

    def chunk_of(at, chunk):
        return emb.at[at, pl.ds(pl.multiple_of(chunk * 128, 128), 128)]

    def ring(at, chunk, step, sem):
        block = chunk_of(at, chunk)
        return remote(block, block, ring_send.at[sem], emb_recv.at[at, chunk], z_peer(step, core))

    def beside(at, chunk, sem):
        block = chunk_of(at, chunk)
        return remote(block, block, sib_send.at[sem], emb_recv.at[at, chunk], sibling)

    def send_own(chunk):
        ring(slot, chunk, 1, chunk).start()
        ring(slot, chunk, 3, 4 + chunk).start()
        beside(slot, chunk, chunk).start()

    def swap(chunk, at):
        return remote(
            home_emb.at[pl.ds(chunk * 128, 128)],
            emb.at[at, pl.ds(chunk * 128, 128)],
            swap_send.at[chunk],
            swap_recv.at[chunk],
            partner,
        )

    def project(source, start, count):
        span = pl.ds(start, count)
        normed[span, :] = jnp.dot(source[span, :], wfull[...], preferred_element_type=F32)
        for at in range(start, start + count, 64):
            rows = pl.ds(at, 64)
            projected = normed[rows, :]
            scale = lax.rsqrt(jnp.sum(projected * projected, axis=1, keepdims=True) + norm_eps)
            normed[rows, :] = projected * scale
            inverse[rows, :] = jnp.broadcast_to(scale, (64, 128))

    for start, count in ((0, 128), (128, 128), (256, 256)):
        span = pl.ds(start, count)
        chunks = range(start // 128, (start + count) // 128)
        project(feat, start, count)

        @pl.when(jnp.logical_not(stays))
        def _():
            home_emb[span, :] = normed[span, :].astype(BF16)
            for chunk in chunks:
                swap(chunk, z * 2 + other).start()

        @pl.when(stays)
        def _():
            emb[slot, span, :] = normed[span, :].astype(BF16)
            for chunk in chunks:
                send_own(chunk)

    def catch_up(part):
        follow(2 * part).wait_recv()
        follow(2 * part + 1).wait_recv()
        project(work, part * HALF, HALF)
        transpose_half(work, part)

    acc[...] = jnp.zeros((ROWS, 128), F32)
    pos[...] = jnp.zeros((ROWS, 128), F32)

    @pl.when(stays)
    def _():
        for part in range(2):
            transpose_half(feat, part)


    @pl.when(jnp.logical_not(stays))
    def _():
        for chunk in range(4):
            swap(chunk, slot).wait_recv()
            send_own(chunk)
        follow(2).start()
        follow(3).start()
        catch_up(0)

    for index in range(7):
        other_slot = lax.rem(slot + 1 + index, 8)
        remote(
            labels.at[other_slot],
            labels.at[other_slot],
            lab_send.at[index],
            lab_recv.at[other_slot],
            sibling,
        ).wait_recv()

    def take(at, which, own):
        piece = at * 2 + which
        columns = pl.ds(pl.multiple_of(which * HALF, HALF), HALF)
        dots[...] = lax.dot_general(
            emb[slot], emb[at, columns, :], (((1,), (1,)), ((), ())), preferred_element_type=F32
        )
        for part in range(2):
            lanes = pl.ds(pl.multiple_of(which * HALF + part * 128, 128), 128)
            col_pair = labels[at, 0:1, lanes]
            col_dup = labels[at, 1:2, lanes]
            for start in range(0, ROWS, 64):
                rows = pl.ds(start, 64)
                power = dots[rows, part * 128 : (part + 1) * 128] * SLOPE - SLOPE
                value = jnp.exp2(power)
                mate = row_pairs[rows, :] == col_pair
                if own:
                    row_index = start + lax.broadcasted_iota(jnp.int32, (64, 128), 0)
                    col_index = which * HALF + part * 128 + lax.broadcasted_iota(jnp.int32, (64, 128), 1)
                    mate = jnp.logical_and(mate, row_index != col_index)
                apart = jnp.where(row_dups[rows, :] != col_dup, value, 0.0)
                paired = jnp.where(mate, value, 0.0)
                quot[piece, rows, part * 128 : (part + 1) * 128] = apart - paired
                acc[rows, :] += apart
                pos[rows, :] += paired

    def own_piece(part, carry):
        take(slot, part, True)
        return carry

    lax.fori_loop(0, 2, own_piece, 0)

    def next_piece(step, carry):
        which_ring = jnp.where(pick(step, 0) == 0, core, other)
        at = around(z, pick(step, 1)) * 2 + which_ring
        which = pick(step, 2)
        for sub in range(2):
            chunk = which * 2 + sub
            ring(at, chunk, 1, 0).wait_recv()

            @pl.when(step == 0)
            def _():
                ring(at, chunk, 1, 8 + sub).start()
                beside(at, chunk, 4 + sub).start()

            @pl.when(step == 3)
            def _():
                ring(at, chunk, 3, 10 + sub).start()
                beside(at, chunk, 6 + sub).start()

            for index, count in ((1, 8), (4, 10), (10, 12), (11, 14)):

                @pl.when(step == index)
                def _():
                    beside(at, chunk, count + sub).start()

        take(at, which, False)
        return carry

    lax.fori_loop(0, len(ORDER), next_piece, 0)

    total_row = jnp.sum((acc[...] + pos[...]).T, axis=0, keepdims=True)
    norms[slot] = 1.0 / total_row
    norm_copies = []
    for index, (step, which) in enumerate(
        [(0, other)] + [(step, which) for step in (1, 2, 3) for which in (core, other)]
    ):
        copy = remote(
            norms.at[slot], norms.at[slot], norm_send.at[index], norm_recv.at[slot], z_peer(step, which)
        )
        copy.start()
        norm_copies.append(copy)
    paired_row = jnp.sum(pos[...].T, axis=0, keepdims=True)
    loss_out[...] = jnp.broadcast_to(jnp.log(total_row) - jnp.log(paired_row), (8, ROWS))
    total = jnp.sum(acc[...] + pos[...], axis=1, keepdims=True)
    acc[...] = jnp.broadcast_to(1.0 / total, (ROWS, 128))

    def wait_norm(at):
        remote(norms.at[at], norms.at[at], norm_send.at[0], norm_recv.at[at], sibling).wait_recv()

    loss_back = remote(loss_out, loss_in, loss_send, loss_recv, partner)

    @pl.when(jnp.logical_not(stays))
    def _():
        loss_back.start()
        catch_up(1)

    def back(part):
        rows = pl.ds(part * HALF, HALF)
        return remote(pre.at[rows], home_pre.at[rows], back_send.at[part], back_recv.at[part], partner)

    for step in STEPS:
        pair = around(z, step)
        if step:
            wait_norm(pair * 2 + core)
        wait_norm(pair * 2 + other)
        buffer = step % 2
        for index in range(4):
            for lane in range(0, HALF, 128):
                column = (index % 2) * HALF + lane
                norm = norms[pair * 2 + index // 2, 0:1, column : column + 128]
                for start in range(0, ROWS, 64):
                    rows = pl.ds(start, 64)
                    value = quot[pair * 4 + index, rows, lane : lane + 128]
                    weight = jnp.abs(value) * (acc[rows, :] + norm) - jnp.where(value < 0.0, 2.0, 0.0)
                    weights[buffer, start : start + 64, index * HALF + lane : index * HALF + lane + 128] = (
                        weight.astype(BF16)
                    )
        term = jnp.dot(
            weights[buffer], emb[pl.ds(pair * 2, 2)].reshape(2 * ROWS, EMB), preferred_element_type=F32
        )
        if step:
            grad[...] += term
        else:
            grad[...] = term

    for start in range(0, ROWS, 64):
        rows = pl.ds(start, 64)
        unit = normed[rows, :]
        whole = scale_logits * grad[rows, :]
        along = jnp.sum(unit * whole, axis=1, keepdims=True)
        pre[rows, :] = (inverse[rows, 0:1] * (whole - unit * along)).astype(BF16)

    @pl.when(jnp.logical_not(stays))
    def _():
        for part in range(2):
            back(part).start()

    reduce_copies = []
    for index, offset in enumerate(FAR_FIRST):
        group = around(first, offset)
        sib_out[group] = jnp.dot(featp[other, group], pre[...], preferred_element_type=F32).astype(BF16)
        copy = remote(sib_out.at[group], sib_in.at[group], rc_send.at[index], rc_recv.at[index], sibling)
        copy.start()
        reduce_copies.append(copy)
    for at in range(4):
        own_term[at] = jnp.dot(featp[core, at], pre[...], preferred_element_type=F32)
    def first_copy(index, count):
        return remote(
            first_out.at[index, count],
            first_in.at[index, count],
            rf_send.at[index * 3 + count],
            rf_recv.at[index * 3 + count],
            first_peer(FAR_FIRST[count]),
        )

    def send_group(index):
        group = around(second, FAR_FIRST[index])
        remote(
            sib_out.at[group], sib_in.at[group], rc_send.at[index], rc_recv.at[index], sibling
        ).wait_recv()
        for count, step in enumerate(FAR_FIRST):
            rows = pl.ds(pl.multiple_of(around(first, step) * 64, 64), 64)
            value = own_term[group, rows, :] + sib_in[group, rows, :].astype(F32)
            if step:
                first_out[index, count] = value.astype(BF16)
                first_copy(index, count).start()
            else:
                first_sum[index] = value

    send_group(0)
    send_group(1)
    for index, offset in enumerate(FAR_FIRST):
        for count in range(3):
            first_copy(index, count).wait_send()
        if index < 2:
            send_group(index + 2)
        whole = first_sum[index]
        for count in (1, 2, 0):
            first_copy(index, count).wait_recv()
            whole = whole + first_in[index, count].astype(F32)
        plane_out[index] = whole.astype(BF16)
        for step in FAR_FIRST:
            target = offset * 4 + step
            if target:
                copy = remote(
                    plane_out.at[index, pl.ds(pl.multiple_of(around(x, step) * 16, 16), 16)],
                    plane_in.at[target - 1],
                    rp_send.at[target - 1],
                    rp_recv.at[target - 1],
                    plane_peer(target),
                )
                copy.start()
                reduce_copies.append(copy)
        if offset == 0:
            first_sum[index] = whole
    @pl.when(jnp.logical_not(stays))
    def _():
        loss_back.wait_recv()
        for part in range(2):
            back(part).wait_recv()
        loss_ref[...] = loss_in[0:1, :]

    @pl.when(stays)
    def _():
        loss_ref[...] = loss_out[0:1, :]
        home_pre[...] = pre[...]

    def feature_part(index, carry):
        columns = pl.ds(pl.multiple_of(index * 512, 512), 512)
        fgrad[:, columns] = lax.dot_general(
            home_pre[...], wfull[columns, :], (((1,), (1,)), ((), ())), preferred_element_type=F32
        ).astype(BF16)
        return carry

    lax.fori_loop(0, 4, feature_part, 0)
    store = pltpu.make_async_copy(fgrad, fgrad_hbm, fgrad_sem)
    store.start()

    value = first_sum[3, pl.ds(pl.multiple_of(x * 16, 16), 16), :]
    for offset in FAR_FIRST:
        for step in (1, 3, 2, 0):
            target = offset * 4 + step
            if target:
                remote(
                    plane_out.at[0, pl.ds(0, 16)],
                    plane_in.at[target - 1],
                    rp_send.at[target - 1],
                    rp_recv.at[target - 1],
                    plane_peer(target),
                ).wait_recv()
                value = value + plane_in[target - 1].astype(F32)
    wgrad_ref[...] = value * (1.0 / 256.0)

    for copy in started + lab_copies + norm_copies + reduce_copies:
        copy.wait_send()
    for index in range(12):
        ring(slot, 0, 1, index).wait_send()
    for index in range(16):
        beside(slot, 0, index).wait_send()

    @pl.when(jnp.logical_not(stays))
    def _():
        lab_swap.wait_send()
        for chunk in range(4):
            swap(chunk, z * 2 + other).wait_send()
        loss_back.wait_send()
        for part in range(2):
            back(part).wait_send()
        for chunk in range(4):
            follow(chunk).wait_send()

    store.wait()


def deliver(loss_in, fgrad_in, wgrad_in, loss_out, fgrad_out, wgrad_out, loss, fgrad, wgrad, load_sem, store_sem):
    parts = [
        (fgrad_in.at[pl.ds(at, 64)], fgrad.at[pl.ds(at, 64)], fgrad_out.at[pl.ds(at, 64)])
        for at in range(0, ROWS, 64)
    ]
    parts += [(loss_in, loss, loss_out), (wgrad_in, wgrad, wgrad_out)]
    loads = [
        pltpu.make_async_copy(source, held, load_sem.at[index]) for index, (source, held, _) in enumerate(parts)
    ]
    stores = [
        pltpu.make_async_copy(held, target, store_sem.at[index]) for index, (_, held, target) in enumerate(parts)
    ]
    for copy in loads:
        copy.start()
    for load, store in zip(loads, stores):
        load.wait()
        store.start()
    for store in stores:
        store.wait()


def body(features, weight, pair_ids, dup_ids):
    dma = pltpu.SemaphoreType.DMA
    vmem = pltpu.VMEM
    loss, feature_grad, weight_grad = pl.pallas_call(
        kernel,
        out_shape=(
            jax.ShapeDtypeStruct((1, ROWS), F32),
            jax.ShapeDtypeStruct((ROWS, FEAT), BF16),
            jax.ShapeDtypeStruct((16, EMB), F32),
        ),
        in_specs=[pl.BlockSpec(memory_space=pl.ANY)] * 4,
        out_specs=(
            pl.BlockSpec(memory_space=vmem),
            pl.BlockSpec(memory_space=pl.ANY),
            pl.BlockSpec(memory_space=vmem),
        ),
        scratch_shapes=[
            vmem((ROWS, FEAT), BF16),
            vmem((ROWS, FEAT), BF16),
            vmem((2, 4, 256, EMB), BF16),
            vmem((2, 4, 4, 4, 16, EMB), BF16),
            vmem((FEAT, EMB), BF16),
            vmem((ROWS, EMB), F32),
            vmem((ROWS, 128), F32),
            vmem((ROWS, EMB), BF16),
            vmem((8, ROWS, EMB), BF16),
            vmem((8, 8, ROWS), jnp.int32),
            vmem((8, ROWS), jnp.int32),
            vmem((ROWS, 128), jnp.int32),
            vmem((ROWS, 128), jnp.int32),
            vmem((2, ROWS, 2 * ROWS), BF16),
            vmem((ROWS, HALF), F32),
            vmem((16, ROWS, HALF), F32),
            vmem((ROWS, 128), F32),
            vmem((ROWS, 128), F32),
            vmem((8, 1, ROWS), F32),
            vmem((ROWS, EMB), F32),
            vmem((8, ROWS), F32),
            vmem((8, ROWS), F32),
            vmem((ROWS, EMB), BF16),
            vmem((ROWS, EMB), BF16),
            vmem((ROWS, FEAT), BF16),
            vmem((4, 256, EMB), BF16),
            vmem((4, 256, EMB), BF16),
            vmem((4, 256, EMB), F32),
            vmem((4, 3, 64, EMB), BF16),
            vmem((4, 3, 64, EMB), BF16),
            vmem((4, 64, EMB), F32),
            vmem((4, 64, EMB), BF16),
            vmem((15, 16, EMB), BF16),
            vmem((1, ROWS), jnp.int32),
            vmem((1, ROWS), jnp.int32),
            dma((3,)),
            dma,
            dma,
            dma((15,)),
            dma((15,)),
            dma((3, 4)),
            dma((3, 4)),
            dma((16,)),
            dma((16,)),
            dma((7,)),
            dma((8,)),
            dma((1,)),
            dma((1,)),
            dma((4,)),
            dma((4,)),
            dma((12,)),
            dma((16,)),
            dma((8, 4)),
            dma((7,)),
            dma((8,)),
            dma((2,)),
            dma((2,)),
            dma,
            dma,
            dma((4,)),
            dma((4,)),
            dma((4,)),
            dma((4,)),
            dma((12,)),
            dma((12,)),
            dma((15,)),
            dma((15,)),
        ],
        compiler_params=pltpu.CompilerParams(
            collective_id=0, has_side_effects=True, vmem_limit_bytes=56 << 20
        ),
        cost_estimate=pl.CostEstimate(
            flops=7_500_000_000, bytes_accessed=8 << 20, transcendentals=2 << 20
        ),
        name="infonce",
    )(features[0], weight, pair_ids, dup_ids)
    anywhere = pl.BlockSpec(memory_space=pl.ANY)
    loss, feature_grad, weight_grad = pl.pallas_call(
        deliver,
        out_shape=(
            jax.ShapeDtypeStruct((1, ROWS), F32),
            jax.ShapeDtypeStruct((ROWS, FEAT), BF16),
            jax.ShapeDtypeStruct((16, EMB), F32),
        ),
        in_specs=[anywhere] * 3,
        out_specs=(anywhere,) * 3,
        scratch_shapes=[
            vmem((1, ROWS), F32),
            vmem((ROWS, FEAT), BF16),
            vmem((16, EMB), F32),
            dma((10,)),
            dma((10,)),
        ],
        name="deliver",
    )(loss, feature_grad, weight_grad)
    return loss, feature_grad[None], weight_grad


def solution(mesh):
    return jax.shard_map(
        body,
        mesh=mesh,
        in_specs=(
            P("rep", "loop", None),
            P(("loop", "rep"), None),
            P("rep", "loop"),
            P("rep", "loop"),
        ),
        out_specs=(P("rep", "loop"), P("rep", "loop", None), P(("loop", "rep"), None)),
        check_vma=False,
    )
```
